32 devices in a mesh: band: 4 (over y, core), dom: 8 (over z, x).
Axes of the slice: x: 2, y: 2, z: 4, core: 2. Of those that a mesh axis runs over, the one named last changes fastest.
Arguments:
- trial_waves: float32 [64, 16, 16, 512], P('dom', None, None, 'band'), may hold values from -10 to 10
- potential: float32 [64, 16, 16], P('dom'), may hold values from -2 to 1
- proj_weights: float32 [16, 8, 256], P('dom'), may hold values from -0.5 to 0.5
- kb_energy: float32 [8], replicated, may hold values from 1 to 4
- atom_cell: int32 [16, 3], P('dom'), may hold values from 0 to 63, as said below
- point_codes: int32 [16, 256], P('dom'), may hold values from 0 to 728, as said below
Outputs:
- filtered: float32 [64, 16, 16, 512], P('dom', None, None, 'band')
- correlation: float32 [512, 512], P('band')
The draws below stay inside these ranges and needn't reach their ends.
Inputs may be any that keep to these rules, and one draw needn't show every extreme that they name: `atom_cell`: atom k's centre lies in the first-dimension planes k // 2 * 8 to (k // 2 + 1) * 8 - 1. `point_codes`: the 256 codes of one atom are distinct cells of the cube of side 2 * 4 + 1 around its centre.
All inputs are finite; a program needn't handle non-finite values.
Results may differ from the reference program's by a relative error of at most 0.0001.
Values sent between devices are 32-bit elements; how exact they have to be, the bound alone decides.
No kernel may reach another device: no remote copies, remote signals or barrier semaphores. Data moves between devices by JAX's collectives and lax.ppermute only.
A program may use at most 128 MiB of HBM per device.

```python
import jax
import jax.numpy as jnp
from jax import lax

BLOCK = 128
CX = 8
NY = 16
NZ = 16
REACH = 4
NPROJ = 8
NPT = 256
ATOMS_DEV = 2
DEGREE = 2
NX = 64
NA = 16
NB = 512
N_BAND = 4


def draw_trial_waves(key, part):
    key_noise, key_common, key_shares = jax.random.split(jax.random.fold_in(key, 11), 3)
    plane_pos = jnp.arange(NX, dtype=jnp.float32).reshape(NX, 1, 1, 1)
    amplitude = jnp.sqrt(1.0 + 2.0 * plane_pos / max(NX - 1, 1))
    shares = jax.random.uniform(key_shares, (1, 1, 1, NB), jnp.float32, 0.4, 1.2)
    noise_part = jax.random.normal(key_noise, (NX, NY, NZ, NB), jnp.float32)
    common = jax.random.normal(key_common, (NX, NY, NZ, 1), jnp.float32)
    return jnp.clip(amplitude * (noise_part + shares * common), -10.0, 10.0)


def draw_atom_cell(key, part):
    key_x, key_y, key_z = jax.random.split(jax.random.fold_in(key, 23), 3)
    atom_ids = jnp.arange(NA, dtype=jnp.int32)
    slab_index = atom_ids // ATOMS_DEV
    cell_x = slab_index * CX + jax.random.randint(key_x, (NA,), 0, CX, dtype=jnp.int32)
    cell_x = jnp.where(atom_ids == NA - 1, NX - 1, cell_x)
    cell_x = jnp.where(atom_ids == 0, 0, cell_x)
    cell_y = jax.random.randint(key_y, (NA,), 0, NY, dtype=jnp.int32)
    cell_z = jax.random.randint(key_z, (NA,), 0, NZ, dtype=jnp.int32)
    return jnp.stack([cell_x, cell_y, cell_z], axis=1).astype(jnp.int32)


def draw_point_codes(key, part):
    atom_keys = jax.random.split(jax.random.fold_in(key, 37), NA)
    cube_total = (2 * REACH + 1) ** 3
    return jax.vmap(lambda one_key: jax.random.permutation(one_key, cube_total)[:NPT])(atom_keys).astype(jnp.int32)


def block_levels(rng, shape, pieces, smallest, high):
    gain = 1.0
    for axis_at, blocks in pieces:
        heights = jax.random.uniform(jax.random.fold_in(jax.random.fold_in(rng, 6), axis_at), (blocks,), jnp.float32, smallest / len(pieces), high / len(pieces))
        gain = gain * jnp.repeat(jnp.exp(heights), shape[axis_at] // blocks).reshape((-1,) + (1,) * (len(shape) - 1 - axis_at))
    return gain


def noise(stream_key, dims, deviation, most, cuts=(), held_as=jnp.bfloat16):
    values = jax.random.normal(stream_key, dims, jnp.float32) * deviation
    if len(cuts) > 0:
        values = block_levels(stream_key, dims, cuts, -0.22, 0.18) * values
    return jnp.clip(values, min=-most, max=most).astype(held_as)


def setup_inputs(seed: int = 0) -> dict:
    streams_of = jax.random.split(jax.random.key(seed), 7)
    trial_waves = draw_trial_waves(jax.random.fold_in(streams_of[6], 71), 0)
    potential = jnp.clip(-2.0 + 3.0 * jax.random.uniform(streams_of[1], (NX, NY, NZ), jnp.float32) ** block_levels(streams_of[1], (NX, NY, NZ), ((0, 8),), -0.2, 0.2), -2.0, 1.0)
    proj_weights = noise(streams_of[2], (NA, NPROJ, NPT), (NPT * 4 // 9) ** -0.5, 0.5, ((0, 8),), jnp.float32)
    kb_energy = jnp.clip(jax.random.uniform(streams_of[3], (NPROJ,), jnp.float32, 1.0, 4.0), 1.0, 4.0)
    atom_cell = draw_atom_cell(jax.random.fold_in(streams_of[6], 71), 0)
    point_codes = draw_point_codes(jax.random.fold_in(streams_of[6], 71), 0)
    return {"trial_waves": trial_waves, "potential": potential, "proj_weights": proj_weights, "kb_energy": kb_energy, "atom_cell": atom_cell, "point_codes": point_codes}


COEFFS = (-5369.0 / 1800.0, 12.0 / 7.0, -15.0 / 56.0, 10.0 / 189.0, -1.0 / 112.0, 2.0 / 1925.0, -1.0 / 16632.0)
FILTER_LOWER = 5.0
FILTER_UPPER = 24.0
SPECTRUM_BOTTOM = 0.0
EPSILON = 1e-06

def kinetic(wavefield):
    summed = 3.0 * COEFFS[0] * wavefield
    for k in range(1, 7):
        for axis_id in (0, 1, 2):
            summed = summed + COEFFS[k] * (jnp.roll(wavefield, k, axis_id) + jnp.roll(wavefield, -k, axis_id))
    return -0.5 * summed

def support_index(atom_cell, point_codes):
    cube_side = 2 * REACH + 1
    off_x = point_codes // (cube_side * cube_side)
    off_y = point_codes // cube_side % cube_side
    off_z = point_codes % cube_side
    cell_x = (atom_cell[:, 0:1] + off_x - REACH) % NX
    cell_y = (atom_cell[:, 1:2] + off_y - REACH) % NY
    cell_z = (atom_cell[:, 2:3] + off_z - REACH) % NZ
    return ((cell_x * NY + cell_y) * NZ + cell_z).reshape(-1).astype(jnp.int32)

def hamiltonian(wavefield, potential, flat_index, proj_weights, scaled):
    band_count = wavefield.shape[-1]
    flat_rows = wavefield.reshape(-1, band_count)
    cell_rows = jnp.take(flat_rows, flat_index, axis=0).reshape(NA, NPT, band_count)
    projections = jnp.einsum('ajp,apb->ajb', proj_weights, cell_rows, precision=lax.Precision.HIGHEST)
    contrib = jnp.einsum('ajp,ajb->apb', scaled, projections, precision=lax.Precision.HIGHEST)
    nonlocal_term = jnp.zeros_like(flat_rows).at[flat_index].add(contrib.reshape(-1, band_count)).reshape(wavefield.shape)
    return kinetic(wavefield) + potential[..., None] * wavefield + nonlocal_term

def filter_block(band_block, potential, flat_index, proj_weights, scaled):
    half_width = (FILTER_UPPER - FILTER_LOWER) / 2.0
    centre = (FILTER_UPPER + FILTER_LOWER) / 2.0
    sigma_first = half_width / (SPECTRUM_BOTTOM - centre)
    sigma_prev = sigma_first
    older = band_block
    applied = hamiltonian(band_block, potential, flat_index, proj_weights, scaled)
    newer = sigma_first / half_width * (applied - centre * band_block)
    for _ in range(DEGREE - 1):
        sigma_next = 1.0 / (2.0 / sigma_first - sigma_prev)
        applied = hamiltonian(newer, potential, flat_index, proj_weights, scaled)
        newer, older = (2.0 * sigma_next / half_width * (applied - centre * newer) - sigma_prev * sigma_next * older, newer)
        sigma_prev = sigma_next
    return newer

def reference(trial_waves, potential, proj_weights, kb_energy, atom_cell, point_codes):
    flat_index = support_index(atom_cell, point_codes)
    scaled = proj_weights * kb_energy[None, :, None]
    blocks = trial_waves.reshape(NX, NY, NZ, N_BAND, BLOCK).transpose(3, 0, 1, 2, 4)
    result = lax.map(lambda band_block: filter_block(band_block, potential, flat_index, proj_weights, scaled), blocks)
    filtered_raw = result.transpose(1, 2, 3, 0, 4).reshape(NX, NY, NZ, N_BAND * BLOCK)
    cell_total = NX * NY * NZ
    flat_rows = filtered_raw.reshape(cell_total, -1)
    rms_band = jnp.sqrt(lax.optimization_barrier(jnp.sum(flat_rows * flat_rows, axis=0)) / cell_total + EPSILON)
    filtered = filtered_raw / rms_band
    scaled_rows = filtered.reshape(cell_total, -1)
    correlation = lax.dot_general(scaled_rows, scaled_rows, (((0,), (0,)), ((), ())), precision=lax.Precision.HIGHEST, preferred_element_type=jnp.float32) / cell_total
    return (filtered, correlation)
```

```python
import functools

import jax
import jax.numpy as jnp
import numpy as np
from jax import lax
from jax.experimental import pallas as pl
from jax.experimental.pallas import tpu as pltpu
from jax.sharding import PartitionSpec as P

HALO = 6
REACH = 4
SLAB = 8
SIDE = 16
LAT = SIDE * SIDE
CHUNKS = 1

COEFFS = (
    -5369.0 / 1800.0,
    12.0 / 7.0,
    -15.0 / 56.0,
    10.0 / 189.0,
    -1.0 / 112.0,
    2.0 / 1925.0,
    -1.0 / 16632.0,
)
FILTER_LOWER = 5.0
FILTER_UPPER = 24.0
SPECTRUM_BOTTOM = 0.0
EPSILON = 1e-06

HALF_WIDTH = (FILTER_UPPER - FILTER_LOWER) / 2.0
CENTRE = (FILTER_UPPER + FILTER_LOWER) / 2.0
SIGMA_1 = HALF_WIDTH / (SPECTRUM_BOTTOM - CENTRE)
SIGMA_2 = 1.0 / (2.0 / SIGMA_1 - SIGMA_1)

VMEM_LIMIT = 48 * 1024 * 1024
BF16 = jnp.bfloat16
F32 = jnp.float32
NN = (((1,), (0,)), ((), ()))
NT = (((1,), (1,)), ((), ()))


def dot(a, b, dims=NN):
    return lax.dot_general(a, b, dims, preferred_element_type=F32)


def halves(x):
    hi = x.astype(BF16)
    return hi, (x - hi.astype(F32)).astype(BF16)


def dot3(ah, al, bh, bl, dims=NN):
    return dot(ah, bh, dims) + dot(al, bh, dims) + dot(ah, bl, dims)


def lateral_matrix():
    line = np.zeros((SIDE, SIDE))
    at = np.arange(SIDE)
    for k in range(1, HALO + 1):
        for sign in (1, -1):
            np.add.at(line, ((at + sign * k) % SIDE, at), -0.5 * COEFFS[k])
    eye = np.eye(SIDE)
    return np.kron(line, eye) + np.kron(eye, line)


def relation():
    return [[-1, 0] if q < REACH else [0, 1] for q in range(SLAB)]


def fold_matrix():
    out = np.zeros((256, 384), np.float32)
    for q, pair in enumerate(relation()):
        for half, rel in enumerate(pair):
            for r in range(16):
                out[q * 32 + half * 16 + r, (rel + 1) * 128 + r] = 1.0
    return out


def split_const(matrix):
    matrix = np.asarray(matrix, np.float32)
    hi = jnp.asarray(matrix, F32).astype(BF16)
    lo = (jnp.asarray(matrix, F32) - hi.astype(F32)).astype(BF16)
    return hi, lo


def split_kernel(nd, nb, chunks, pos_ref, x_ref, *refs):
    outs, scratch = refs[:-1], refs[-1]
    i = pos_ref[0]
    for q in range(SLAB):
        scratch[q] = x_ref[q].T
    real = scratch.shape[1] // (nd * chunks)
    for c in range(chunks):
        for j in range(nd):
            start = c * nd * real + (i ^ j) * real
            for q in range(SLAB):
                outs[c * nd + j][q * nb : (q + 1) * nb] = scratch[q, pl.ds(pl.multiple_of(start, nb), nb)]


def weights_kernel(nd, pos_ref, *refs):
    parts, (wh_ref, wl_ref, v_ref, scratch) = refs[:4], refs[4:]
    i, b = pos_ref[0], pos_ref[1]
    for jb in range(4):
        rows = pl.ds(pl.multiple_of((b ^ jb) * 8, 8), 8)
        for j in range(nd):
            scratch[i ^ j, rows] = parts[jb][j]
    lat = lax.broadcasted_iota(jnp.int32, (LAT, 256), 0).astype(F32)
    plane = lax.broadcasted_iota(jnp.int32, (16, 1, 1), 0).astype(F32)
    diagonal = -1.5 * COEFFS[0] - CENTRE

    def body(s, carry):
        his, los = [], []
        for a in range(2):
            w = scratch[s, a * 8 : a * 8 + 8]
            px = scratch[s, 16 + a : 17 + a]
            place = scratch[s, 18 + a : 19 + a]
            hot = jnp.where(lat == place, 1.0, 0.0).astype(BF16)
            masked = jnp.where(px[None] == plane, w[None], 0.0).reshape(128, 256)
            mh, ml = halves(masked)
            his.append(dot(mh, hot, NT).reshape(16, 8, LAT))
            los.append(dot(ml, hot, NT).reshape(16, 8, LAT))
        hi = jnp.concatenate(his, axis=1).astype(BF16)
        lo = jnp.concatenate(los, axis=1).astype(BF16)
        for t in range(16):
            p = (s * SLAB - REACH + t + nd * SLAB) % (nd * SLAB) if isinstance(s, int) else lax.rem(
                s * SLAB - REACH + t + nd * SLAB, nd * SLAB
            )
            row = pl.ds(pl.multiple_of(p * 32 + (16 if t < SLAB else 0), 16), 16)
            wh_ref[row] = hi[t]
            wl_ref[row] = lo[t]
        v_ref[pl.ds(pl.multiple_of(s * SLAB, SLAB), SLAB)] = scratch[s, 24:32] + diagonal
        return carry

    if nd <= 8:
        for s in range(nd):
            body(s, 0)
    else:
        lax.fori_loop(0, nd, body, 0)


def filter_kernel(nd, nb, total, pos_ref, kb_ref, v_ref, wh_ref, wl_ref, lh_ref, ll_ref, fold_ref, spread_ref, *refs):
    pieces, outs = refs[:nd], refs[nd : 2 * nd]
    f0_ref, f1_ref, fold_out, spread_out = refs[2 * nd :]
    i = pos_ref[0]
    R = SLAB * nb
    rows_q = lax.broadcasted_iota(jnp.int32, (SLAB, nb, 256), 0)
    lanes_q = lax.broadcasted_iota(jnp.int32, (SLAB, nb, 256), 2) // 32
    same = rows_q == lanes_q

    def slab_rows(s, k=0):
        return pl.ds(pl.multiple_of((s * SLAB + HALO + k) * nb, nb), R)

    def wrap(ref):
        ref[0 : HALO * nb] = ref[nd * R : nd * R + HALO * nb]
        ref[HALO * nb + nd * R : 2 * HALO * nb + nd * R] = ref[HALO * nb : 2 * HALO * nb]

    def each(body):
        if nd <= 8:
            for s in range(nd):
                body(s)
        else:
            lax.fori_loop(0, nd, lambda s, c: (body(s), c)[1], 0)

    for j in range(nd):
        f0_ref[slab_rows(i ^ j)] = pieces[j][...]
    wrap(f0_ref)

    def apply(ref, finish):
        def project(s):
            fh, fl = halves(ref[slab_rows(s)])
            w = pl.ds(pl.multiple_of(s * 256, 256), 256)
            g = dot3(fh, fl, wh_ref[w], wl_ref[w], NT).reshape(SLAB, nb, 256)
            fold_out[pl.ds(pl.multiple_of(s * nb, nb), nb)] = jnp.sum(jnp.where(same, g, 0.0), axis=0)

        each(project)
        gh, gl = halves(fold_out[...])
        h = dot(gh, fold_ref[...]) + dot(gl, fold_ref[...])
        below, at, above = h[:, :128], h[:, 128:256], h[:, 256:]

        def next_slab(x):
            return jnp.concatenate([x[-nb:], x[:-nb]], axis=0)

        def previous_slab(x):
            return jnp.concatenate([x[nb:], x[:nb]], axis=0)

        p = (at + next_slab(above) + previous_slab(below)) * kb_ref[...]
        wide = jnp.concatenate([next_slab(p), p, previous_slab(p)], axis=1)
        ph, plo = halves(wide)
        spread_out[...] = dot(ph, spread_ref[...], NT) + dot(plo, spread_ref[...], NT)

        def step(s):
            f = ref[slab_rows(s)]
            fh, fl = halves(f)
            x = jnp.where(same, spread_out[pl.ds(pl.multiple_of(s * nb, nb), nb)][None], 0.0).reshape(R, 256)
            xh, xl = halves(x)
            w = pl.ds(pl.multiple_of(s * 256, 256), 256)
            acc = dot3(xh, xl, wh_ref[w], wl_ref[w]) + dot3(fh, fl, lh_ref[...], ll_ref[...])
            v = v_ref[pl.ds(pl.multiple_of(s * SLAB, SLAB), SLAB)]
            acc = acc + (f.reshape(SLAB, nb, LAT) * v[:, None, :]).reshape(R, LAT)
            for k in range(1, HALO + 1):
                acc = acc + (-0.5 * COEFFS[k]) * (ref[slab_rows(s, k)] + ref[slab_rows(s, -k)])
            finish(s, acc)

        each(step)

    def first(s, acc):
        f1_ref[slab_rows(s)] = (SIGMA_1 / HALF_WIDTH) * acc

    apply(f0_ref, first)
    wrap(f1_ref)

    def second(s, acc):
        f0_ref_new = (2.0 * SIGMA_2 / HALF_WIDTH) * acc - (SIGMA_1 * SIGMA_2) * f0_ref[slab_rows(s)]
        y2_store(s, f0_ref_new)

    def y2_store(s, value):
        f0_ref[slab_rows(s)] = value

    apply(f1_ref, second)
    square = jnp.zeros((nb, LAT), F32)
    if nd <= 8:
        for s in range(nd):
            y = f0_ref[slab_rows(s)].reshape(SLAB, nb, LAT)
            square = square + jnp.sum(y * y, axis=0)
    else:

        def add(s, total_square):
            y = f0_ref[slab_rows(s)].reshape(SLAB, nb, LAT)
            return total_square + jnp.sum(y * y, axis=0)

        square = lax.fori_loop(0, nd, add, square)
    scale = 1.0 / jnp.sqrt(jnp.sum(square, axis=1, keepdims=True) / total + EPSILON)
    for j in range(nd):
        y = f0_ref[slab_rows(i ^ j)].reshape(SLAB, nb, LAT)
        outs[j][...] = (y * scale[None]).reshape(R, LAT)


def join_kernel(nd, nb, real, pos_ref, *refs):
    pieces, (z_ref, send_ref) = refs[:nd], refs[nd:]
    i, y = pos_ref[0], pos_ref[2]
    for j in range(nd):
        rows = pl.ds(pl.multiple_of((i ^ j) * real, real), real)
        for q in range(SLAB):
            z_ref[q, rows] = pieces[j][q * nb : q * nb + real]
    half = SLAB // 2
    for q in range(half):
        send_ref[q] = z_ref[(1 - y) * half + q]


def gram_kernel(chunks, pos_ref, *refs):
    own, core, far, far_core = (refs[k * chunks : (k + 1) * chunks] for k in range(4))
    g_ref, far_ref = refs[4 * chunks :]
    b, y = pos_ref[1], pos_ref[2]
    half = SLAB // 2

    def load(group, q):
        return halves(jnp.concatenate([r[q] for r in group], axis=0))

    def add(totals, place, value):
        totals[place] = value if totals.get(place) is None else totals[place] + value

    totals = {}
    for q in range(half):
        for mine in (True, False):
            at = q + y * half if mine else q + (1 - y) * half
            zh, zl = load(own, at)
            ch, cl = load(core, at)
            add(totals, "own", dot3(zh, zl, zh, zl, NT))
            add(totals, "core", dot3(zh, zl, ch, cl, NT))
            if mine:
                fh, fl = load(far, q)
                gh, gl = load(far_core, q)
                add(totals, "far", dot3(zh, zl, fh, fl, NT))
                add(totals, "far_core", dot3(zh, zl, gh, gl, NT))
                add(totals, "back", dot3(fh, fl, zh, zl, NT))
                add(totals, "back_core", dot3(fh, fl, ch, cl, NT))
    g_ref[b] = totals["own"]
    g_ref[b ^ 1] = totals["core"]
    g_ref[b ^ 2] = totals["far"]
    g_ref[b ^ 3] = totals["far_core"]
    far_ref[b & 1] = totals["back"]
    far_ref[(b & 1) ^ 1] = totals["back_core"]


def output_kernel(chunks, *refs):
    zs, out_ref = refs[:chunks], refs[chunks]
    for q in range(SLAB):
        out_ref[q] = jnp.concatenate([z[q] for z in zs], axis=0).T


def part_kernel(nd, pos_ref, g_ref, far_ref, *outs):
    i, y = pos_ref[0], pos_ref[2]
    size = outs[0].shape[1]
    for j in range(nd):
        rows = pl.ds(pl.multiple_of((i ^ j) * size, size), size)
        for c in range(2):
            outs[j][y * 2 + c] = g_ref[y * 2 + c, rows]
            outs[j][(1 - y) * 2 + c] = g_ref[(1 - y) * 2 + c, rows] + far_ref[c, rows]


def sum_kernel(total, *refs):
    acc = refs[0][...]
    for r in refs[1:-1]:
        acc = acc + r[...]
    refs[-1][...] = acc * (1.0 / total)


def place_kernel(nd, pos_ref, *refs):
    pieces, out_ref = refs[:nd], refs[nd]
    i = pos_ref[0]
    size = pieces[0].shape[1]
    for j in range(nd):
        rows = pl.ds(pl.multiple_of((i ^ j) * size, size), size)
        for k in range(4):
            out_ref[rows, k * 128 : (k + 1) * 128] = pieces[j][k]


def call(kernel, out_shape, operands, scratch=(), name=None):
    specs = [
        pl.BlockSpec(memory_space=pltpu.SMEM) if o.dtype == jnp.int32 else pl.BlockSpec(memory_space=pltpu.VMEM)
        for o in operands
    ]
    single = not isinstance(out_shape, (list, tuple))
    return pl.pallas_call(
        kernel,
        out_shape=out_shape,
        in_specs=specs,
        out_specs=(
            pl.BlockSpec(memory_space=pltpu.VMEM)
            if single
            else [pl.BlockSpec(memory_space=pltpu.VMEM) for _ in out_shape]
        ),
        scratch_shapes=list(scratch),
        compiler_params=pltpu.CompilerParams(vmem_limit_bytes=VMEM_LIMIT),
        name=name,
    )(*operands)


def shape(*dims, dtype=F32):
    return jax.ShapeDtypeStruct(dims, dtype)


def xor_permute(value, axis, step):
    count = lax.axis_size(axis)
    return lax.ppermute(value, axis, [(k, k ^ step) for k in range(count)])


def swap_all(pieces, direct):
    if direct:
        return [pieces[0]] + [xor_permute(p, "dom", j) for j, p in enumerate(pieces) if j]
    stacked = lax.all_to_all(jnp.stack(pieces), "dom", 0, 0, tiled=True)
    return [stacked[j] for j in range(len(pieces))]


def packed_atoms(potential, proj_weights, atom_cell, point_codes):
    cube = 2 * REACH + 1
    off_x = point_codes // (cube * cube)
    off_y = point_codes // cube % cube
    off_z = point_codes % cube
    plane = atom_cell[:, 0:1] % SLAB + off_x
    cell_y = (atom_cell[:, 1:2] + off_y - REACH) % SIDE
    cell_z = (atom_cell[:, 2:3] + off_z - REACH) % SIDE
    lateral = cell_y * SIDE + cell_z
    return jnp.concatenate(
        [
            proj_weights.reshape(-1, 256),
            plane.astype(F32),
            lateral.astype(F32),
            jnp.zeros((4, 256), F32),
            potential.reshape(SLAB, LAT),
        ],
        axis=0,
    )


def on_device(trial_waves, potential, proj_weights, kb_energy, atom_cell, point_codes):
    nd = lax.axis_size("dom")
    bands = trial_waves.shape[-1]
    direct = nd == 8
    chunks = CHUNKS if direct else 1
    real = bands // (nd * chunks)
    nb = max(real, 8)
    total = nd * SLAB * LAT
    dom = lax.axis_index("dom") if direct else jnp.int32(0)
    band = lax.axis_index("band")
    pos = jnp.stack([dom, band if direct else jnp.int32(0), band // 2]).astype(jnp.int32)
    pos_band = jnp.stack([dom, band, band // 2]).astype(jnp.int32)
    R = SLAB * nb

    packed = packed_atoms(potential, proj_weights, atom_cell, point_codes)
    if direct:
        mine = lax.dynamic_slice_in_dim(packed, band * 8, 8, 0)
        gathered = jnp.stack([mine] + [xor_permute(mine, "dom", j) for j in range(1, nd)])
        parts = [gathered] + [xor_permute(gathered, "band", j) for j in range(1, 4)]
    else:
        gathered = lax.all_gather(packed, "dom", axis=0)
        parts = [gathered[:, k * 8 : k * 8 + 8] for k in range(4)]

    waves = trial_waves.reshape(SLAB, LAT, bands)
    if direct:
        cut = call(
            functools.partial(split_kernel, nd, nb, chunks),
            [shape(R, LAT)] * (nd * chunks),
            [pos, waves],
            [pltpu.VMEM((SLAB, bands, LAT), F32)],
            "split",
        )
    else:
        turned = waves.transpose(0, 2, 1).reshape(SLAB, nd, real, LAT).transpose(1, 0, 2, 3)
        cut = [turned[j] for j in range(nd)]

    wh, wl, shifted = call(
        functools.partial(weights_kernel, nd),
        [shape(nd * 256, 256, dtype=BF16), shape(nd * 256, 256, dtype=BF16), shape(nd * SLAB, LAT)],
        [pos] + parts,
        [pltpu.VMEM((nd, 32, 256), F32)],
        "weights",
    )
    lh, ll = split_const(lateral_matrix())
    fold = jnp.asarray(fold_matrix()).astype(BF16)
    kb_row = jnp.concatenate([kb_energy, kb_energy, jnp.zeros((112,), F32)])[None]
    spread = fold
    arrived = [swap_all(cut[c * nd : (c + 1) * nd], direct) for c in range(chunks)]
    joined, sends = [], []
    for c in range(chunks):
        pieces = arrived[c]
        if not direct:
            pieces = [jnp.pad(p, ((0, 0), (0, nb - real), (0, 0))).reshape(R, LAT) for p in pieces]
        ready = call(
            functools.partial(filter_kernel, nd, nb, float(total)),
            [shape(R, LAT)] * nd,
            [pos, kb_row, shifted, wh, wl, lh, ll, fold, spread] + pieces,
            [
                pltpu.VMEM(((nd * SLAB + 2 * HALO) * nb, LAT), F32),
                pltpu.VMEM(((nd * SLAB + 2 * HALO) * nb, LAT), F32),
                pltpu.VMEM((nd * nb, 256), F32),
                pltpu.VMEM((nd * nb, 256), F32),
            ],
            "filter",
        )
        if not direct:
            ready = [p.reshape(SLAB, nb, LAT)[:, :real] for p in ready]
        back = swap_all(ready, direct)
        if direct:
            z, send = call(
                functools.partial(join_kernel, nd, nb, real),
                [shape(SLAB, nd * real, LAT), shape(SLAB // 2, nd * real, LAT)],
                [pos_band] + back,
                (),
                "join",
            )
        else:
            z = jnp.concatenate(back, axis=1)
            send = lax.dynamic_slice_in_dim(z, (1 - band // 2) * (SLAB // 2), SLAB // 2, 0)
        joined.append(z)
        sends.append(send)

    core = [xor_permute(z, "band", 1) for z in joined]
    far = [xor_permute(s, "band", 2) for s in sends]
    far_core = [xor_permute(s, "band", 1) for s in far]
    gram, gram_far = call(
        functools.partial(gram_kernel, chunks),
        [shape(4, bands, bands), shape(2, bands, bands)],
        [pos_band] + joined + core + far + far_core,
        (),
        "gram",
    )
    far_share = xor_permute(gram_far, "band", 2)
    filtered = call(functools.partial(output_kernel, chunks), shape(SLAB, LAT, bands), joined, (), "output")
    if direct:
        size = bands // nd
        cut_gram = call(
            functools.partial(part_kernel, nd),
            [shape(4, size, bands)] * nd,
            [pos_band, gram, far_share],
            (),
            "part",
        )
        summed = call(
            functools.partial(sum_kernel, float(total)), shape(4, size, bands), swap_all(cut_gram, direct), (), "sum"
        )
        everyone = [summed] + [xor_permute(summed, "dom", j) for j in range(1, nd)]
        correlation = call(
            functools.partial(place_kernel, nd), shape(bands, 4 * bands), [pos_band] + everyone, (), "place"
        )
    else:
        start = (1 - band // 2) * 2
        cross = lax.dynamic_slice_in_dim(gram, start, 2, 0) + far_share
        gram = lax.dynamic_update_slice_in_dim(gram, cross, start, 0)
        wide = gram.transpose(1, 0, 2).reshape(bands, 4 * bands)
        correlation = lax.psum(wide, "dom") / total
    return filtered.reshape(trial_waves.shape), correlation


def solution(mesh):
    return jax.shard_map(
        on_device,
        mesh=mesh,
        in_specs=(
            P("dom", None, None, "band"),
            P("dom", None, None),
            P("dom", None, None),
            P(),
            P("dom", None),
            P("dom", None),
        ),
        out_specs=(P("dom", None, None, "band"), P("band", None)),
        check_vma=False,
    )
```

```python
import functools

import jax
import jax.numpy as jnp
import numpy as np
from jax import lax
from jax.experimental import pallas as pl
from jax.experimental.pallas import tpu as pltpu
from jax.sharding import PartitionSpec as P

HALO = 6
REACH = 4
SLAB = 8
SIDE = 16
LAT = SIDE * SIDE
CHUNKS = 1

COEFFS = (
    -5369.0 / 1800.0,
    12.0 / 7.0,
    -15.0 / 56.0,
    10.0 / 189.0,
    -1.0 / 112.0,
    2.0 / 1925.0,
    -1.0 / 16632.0,
)
FILTER_LOWER = 5.0
FILTER_UPPER = 24.0
SPECTRUM_BOTTOM = 0.0
EPSILON = 1e-06

HALF_WIDTH = (FILTER_UPPER - FILTER_LOWER) / 2.0
CENTRE = (FILTER_UPPER + FILTER_LOWER) / 2.0
SIGMA_1 = HALF_WIDTH / (SPECTRUM_BOTTOM - CENTRE)
SIGMA_2 = 1.0 / (2.0 / SIGMA_1 - SIGMA_1)

VMEM_LIMIT = 48 * 1024 * 1024
BF16 = jnp.bfloat16
F32 = jnp.float32
NN = (((1,), (0,)), ((), ()))
NT = (((1,), (1,)), ((), ()))


def dot(a, b, dims=NN):
    return lax.dot_general(a, b, dims, preferred_element_type=F32)


def halves(x):
    hi = x.astype(BF16)
    return hi, (x - hi.astype(F32)).astype(BF16)


def dot3(ah, al, bh, bl, dims=NN):
    return dot(ah, bh, dims) + dot(al, bh, dims) + dot(ah, bl, dims)


def lateral_matrix():
    line = np.zeros((SIDE, SIDE))
    at = np.arange(SIDE)
    for k in range(1, HALO + 1):
        for sign in (1, -1):
            np.add.at(line, ((at + sign * k) % SIDE, at), -0.5 * COEFFS[k])
    eye = np.eye(SIDE)
    return np.kron(line, eye) + np.kron(eye, line)


def relation():
    return [[-1, 0] if q < REACH else [0, 1] for q in range(SLAB)]


def fold_matrix():
    out = np.zeros((256, 384), np.float32)
    for q, pair in enumerate(relation()):
        for half, rel in enumerate(pair):
            for r in range(16):
                out[q * 32 + half * 16 + r, (rel + 1) * 128 + r] = 1.0
    return out


def split_const(matrix):
    matrix = np.asarray(matrix, np.float32)
    hi = jnp.asarray(matrix, F32).astype(BF16)
    lo = (jnp.asarray(matrix, F32) - hi.astype(F32)).astype(BF16)
    return hi, lo


def split_kernel(nd, nb, chunks, pos_ref, x_ref, *refs):
    outs, scratch = refs[:-1], refs[-1]
    i = pos_ref[0]
    for q in range(SLAB):
        scratch[q] = x_ref[q].T
    real = scratch.shape[1] // (nd * chunks)
    for c in range(chunks):
        for j in range(nd):
            start = c * nd * real + (i ^ j) * real
            for q in range(SLAB):
                outs[c * nd + j][q * nb : (q + 1) * nb] = scratch[q, pl.ds(pl.multiple_of(start, nb), nb)]


def weights_kernel(nd, pos_ref, *refs):
    parts, (wh_ref, wl_ref, v_ref, scratch) = refs[:2], refs[2:]
    i, core = pos_ref[0], pos_ref[1] & 1
    for jb in range(2):
        rows = pl.ds(pl.multiple_of((core ^ jb) * 16, 16), 16)
        for j in range(nd):
            scratch[i ^ j, rows] = parts[jb][j]
    lat = lax.broadcasted_iota(jnp.int32, (LAT, 256), 0).astype(F32)
    plane = lax.broadcasted_iota(jnp.int32, (16, 1, 1), 0).astype(F32)
    diagonal = -1.5 * COEFFS[0] - CENTRE

    def body(s, carry):
        his, los = [], []
        for a in range(2):
            w = scratch[s, a * 8 : a * 8 + 8]
            px = scratch[s, 16 + a : 17 + a]
            place = scratch[s, 18 + a : 19 + a]
            hot = jnp.where(lat == place, 1.0, 0.0).astype(BF16)
            masked = jnp.where(px[None] == plane, w[None], 0.0).reshape(128, 256)
            mh, ml = halves(masked)
            his.append(dot(mh, hot, NT).reshape(16, 8, LAT))
            los.append(dot(ml, hot, NT).reshape(16, 8, LAT))
        hi = jnp.concatenate(his, axis=1).astype(BF16)
        lo = jnp.concatenate(los, axis=1).astype(BF16)
        for t in range(16):
            p = (s * SLAB - REACH + t + nd * SLAB) % (nd * SLAB) if isinstance(s, int) else lax.rem(
                s * SLAB - REACH + t + nd * SLAB, nd * SLAB
            )
            row = pl.ds(pl.multiple_of(p * 32 + (16 if t < SLAB else 0), 16), 16)
            wh_ref[row] = hi[t]
            wl_ref[row] = lo[t]
        v_ref[pl.ds(pl.multiple_of(s * SLAB, SLAB), SLAB)] = scratch[s, 24:32] + diagonal
        return carry

    if nd <= 8:
        for s in range(nd):
            body(s, 0)
    else:
        lax.fori_loop(0, nd, body, 0)


def filter_kernel(nd, nb, total, pos_ref, kb_ref, v_ref, wh_ref, wl_ref, lh_ref, ll_ref, fold_ref, spread_ref, *refs):
    pieces, outs = refs[:nd], refs[nd : 2 * nd]
    f0_ref, f1_ref, fold_out, spread_out = refs[2 * nd :]
    i = pos_ref[0]
    R = SLAB * nb
    rows_q = lax.broadcasted_iota(jnp.int32, (SLAB, nb, 256), 0)
    lanes_q = lax.broadcasted_iota(jnp.int32, (SLAB, nb, 256), 2) // 32
    same = rows_q == lanes_q

    def slab_rows(s, k=0):
        return pl.ds(pl.multiple_of((s * SLAB + HALO + k) * nb, nb), R)

    def wrap(ref):
        ref[0 : HALO * nb] = ref[nd * R : nd * R + HALO * nb]
        ref[HALO * nb + nd * R : 2 * HALO * nb + nd * R] = ref[HALO * nb : 2 * HALO * nb]

    def each(body):
        if nd <= 8:
            for s in range(nd):
                body(s)
        else:
            lax.fori_loop(0, nd, lambda s, c: (body(s), c)[1], 0)

    for j in range(nd):
        f0_ref[slab_rows(i ^ j)] = pieces[j][...]
    wrap(f0_ref)

    def apply(ref, finish):
        def project(s):
            fh, fl = halves(ref[slab_rows(s)])
            w = pl.ds(pl.multiple_of(s * 256, 256), 256)
            g = dot3(fh, fl, wh_ref[w], wl_ref[w], NT).reshape(SLAB, nb, 256)
            fold_out[pl.ds(pl.multiple_of(s * nb, nb), nb)] = jnp.sum(jnp.where(same, g, 0.0), axis=0)

        each(project)
        gh, gl = halves(fold_out[...])
        h = dot(gh, fold_ref[...]) + dot(gl, fold_ref[...])
        below, at, above = h[:, :128], h[:, 128:256], h[:, 256:]

        def next_slab(x):
            return jnp.concatenate([x[-nb:], x[:-nb]], axis=0)

        def previous_slab(x):
            return jnp.concatenate([x[nb:], x[:nb]], axis=0)

        p = (at + next_slab(above) + previous_slab(below)) * kb_ref[...]
        wide = jnp.concatenate([next_slab(p), p, previous_slab(p)], axis=1)
        ph, plo = halves(wide)
        spread_out[...] = dot(ph, spread_ref[...], NT) + dot(plo, spread_ref[...], NT)

        def step(s):
            f = ref[slab_rows(s)]
            fh, fl = halves(f)
            x = jnp.where(same, spread_out[pl.ds(pl.multiple_of(s * nb, nb), nb)][None], 0.0).reshape(R, 256)
            xh, xl = halves(x)
            w = pl.ds(pl.multiple_of(s * 256, 256), 256)
            acc = dot3(xh, xl, wh_ref[w], wl_ref[w]) + dot3(fh, fl, lh_ref[...], ll_ref[...])
            v = v_ref[pl.ds(pl.multiple_of(s * SLAB, SLAB), SLAB)]
            acc = acc + (f.reshape(SLAB, nb, LAT) * v[:, None, :]).reshape(R, LAT)
            for k in range(1, HALO + 1):
                acc = acc + (-0.5 * COEFFS[k]) * (ref[slab_rows(s, k)] + ref[slab_rows(s, -k)])
            finish(s, acc)

        each(step)

    def first(s, acc):
        f1_ref[slab_rows(s)] = (SIGMA_1 / HALF_WIDTH) * acc

    apply(f0_ref, first)
    wrap(f1_ref)

    def second(s, acc):
        f0_ref_new = (2.0 * SIGMA_2 / HALF_WIDTH) * acc - (SIGMA_1 * SIGMA_2) * f0_ref[slab_rows(s)]
        y2_store(s, f0_ref_new)

    def y2_store(s, value):
        f0_ref[slab_rows(s)] = value

    apply(f1_ref, second)
    square = jnp.zeros((nb, LAT), F32)
    if nd <= 8:
        for s in range(nd):
            y = f0_ref[slab_rows(s)].reshape(SLAB, nb, LAT)
            square = square + jnp.sum(y * y, axis=0)
    else:

        def add(s, total_square):
            y = f0_ref[slab_rows(s)].reshape(SLAB, nb, LAT)
            return total_square + jnp.sum(y * y, axis=0)

        square = lax.fori_loop(0, nd, add, square)
    scale = 1.0 / jnp.sqrt(jnp.sum(square, axis=1, keepdims=True) / total + EPSILON)
    for j in range(nd):
        y = f0_ref[slab_rows(i ^ j)].reshape(SLAB, nb, LAT)
        outs[j][...] = (y * scale[None]).reshape(R, LAT)


def join_kernel(count, nb, pos_ref, *refs):
    pieces, (z_ref, send_ref) = refs[:count], refs[count:]
    i, y = pos_ref[0], pos_ref[2]
    for j in range(count):
        rows = pl.ds(pl.multiple_of(((i ^ j) & (count - 1)) * nb, nb), nb)
        for q in range(SLAB):
            z_ref[q, rows] = pieces[j][q * nb : (q + 1) * nb]
    half = SLAB // 2
    for q in range(half):
        send_ref[q] = z_ref[(1 - y) * half + q]


def place_halves(pos_ref, near, far, out):
    h = pos_ref[0] // 4
    for q in range(out.shape[0]):
        out[q, pl.ds(pl.multiple_of(h * 64, 64), 64)] = near[q]
        out[q, pl.ds(pl.multiple_of((1 - h) * 64, 64), 64)] = far[q]


def own_kernel(pos_ref, near, far, core_near, core_far, z_ref, zc_ref, keep_ref, send_ref, g_ref):
    i, b = pos_ref[0], pos_ref[1]
    place_halves(pos_ref, near, far, z_ref)
    place_halves(pos_ref, core_near, core_far, zc_ref)
    own = core = None
    for q in range(SLAB):
        zh, zl = halves(z_ref[q])
        ch, cl = halves(zc_ref[q])
        mine, other = dot3(zh, zl, zh, zl, NT), dot3(zh, zl, ch, cl, NT)
        own, core = (mine, other) if own is None else (own + mine, core + other)
    g_ref[b & 1] = own
    g_ref[(b & 1) ^ 1] = core
    cut_rows(i, g_ref, keep_ref, send_ref)


def cut_rows(i, g_ref, keep_ref, send_ref):
    x = i & 1
    for c in range(2):
        keep_ref[c] = g_ref[c, pl.ds(pl.multiple_of(x * 64, 64), 64)]
        send_ref[c] = g_ref[c, pl.ds(pl.multiple_of((1 - x) * 64, 64), 64)]


def cross_kernel(pos_ref, z_ref, zc_ref, near, far, core_near, core_far, g_ref, back_ref, f_ref, fc_ref):
    b, y = pos_ref[1], pos_ref[2]
    half = SLAB // 2
    place_halves(pos_ref, near, far, f_ref)
    place_halves(pos_ref, core_near, core_far, fc_ref)
    totals = None
    for q in range(half):
        zh, zl = halves(z_ref[y * half + q])
        ch, cl = halves(zc_ref[y * half + q])
        fh, fl = halves(f_ref[q])
        gh, gl = halves(fc_ref[q])
        now = (
            dot3(zh, zl, fh, fl, NT),
            dot3(zh, zl, gh, gl, NT),
            dot3(fh, fl, zh, zl, NT),
            dot3(fh, fl, ch, cl, NT),
        )
        totals = now if totals is None else tuple(t + n for t, n in zip(totals, now))
    c = b & 1
    g_ref[c], g_ref[c ^ 1], back_ref[c], back_ref[c ^ 1] = totals


def part_kernel(pos_ref, g_ref, share_ref, keep_ref, send_ref, sum_ref):
    sum_ref[...] = g_ref[...] + share_ref[...]
    cut_rows(pos_ref[0], sum_ref, keep_ref, send_ref)


def output_kernel(z_ref, out_ref):
    for q in range(SLAB):
        out_ref[q] = z_ref[q].T


def place_kernel(total, pos_ref, own, own_other, cross, cross_other, out_ref):
    i, y = pos_ref[0], pos_ref[2]
    x = i & 1
    for c in range(2):
        for mine, other, chip in ((own, own_other, y), (cross, cross_other, 1 - y)):
            lanes = pl.ds(pl.multiple_of((chip * 2 + c) * 128, 128), 128)
            out_ref[pl.ds(pl.multiple_of(x * 64, 64), 64), lanes] = mine[c] * (1.0 / total)
            out_ref[pl.ds(pl.multiple_of((1 - x) * 64, 64), 64), lanes] = other[c] * (1.0 / total)


def gram_kernel(pos_ref, own, core, far, far_core, g_ref, far_ref):
    b, y = pos_ref[1], pos_ref[2]
    half = SLAB // 2

    def add(totals, place, value):
        totals[place] = value if totals.get(place) is None else totals[place] + value

    totals = {}
    for q in range(half):
        for mine in (True, False):
            at = q + y * half if mine else q + (1 - y) * half
            zh, zl = halves(own[at])
            ch, cl = halves(core[at])
            add(totals, "own", dot3(zh, zl, zh, zl, NT))
            add(totals, "core", dot3(zh, zl, ch, cl, NT))
            if mine:
                fh, fl = halves(far[q])
                gh, gl = halves(far_core[q])
                add(totals, "far", dot3(zh, zl, fh, fl, NT))
                add(totals, "far_core", dot3(zh, zl, gh, gl, NT))
                add(totals, "back", dot3(fh, fl, zh, zl, NT))
                add(totals, "back_core", dot3(fh, fl, ch, cl, NT))
    g_ref[b] = totals["own"]
    g_ref[b ^ 1] = totals["core"]
    g_ref[b ^ 2] = totals["far"]
    g_ref[b ^ 3] = totals["far_core"]
    far_ref[b & 1] = totals["back"]
    far_ref[(b & 1) ^ 1] = totals["back_core"]


def call(kernel, out_shape, operands, scratch=(), name=None):
    specs = [
        pl.BlockSpec(memory_space=pltpu.SMEM) if o.dtype == jnp.int32 else pl.BlockSpec(memory_space=pltpu.VMEM)
        for o in operands
    ]
    single = not isinstance(out_shape, (list, tuple))
    return pl.pallas_call(
        kernel,
        out_shape=out_shape,
        in_specs=specs,
        out_specs=(
            pl.BlockSpec(memory_space=pltpu.VMEM)
            if single
            else [pl.BlockSpec(memory_space=pltpu.VMEM) for _ in out_shape]
        ),
        scratch_shapes=list(scratch),
        compiler_params=pltpu.CompilerParams(vmem_limit_bytes=VMEM_LIMIT),
        name=name,
    )(*operands)


def shape(*dims, dtype=F32):
    return jax.ShapeDtypeStruct(dims, dtype)


def xor_permute(value, axis, step):
    count = lax.axis_size(axis)
    return lax.ppermute(value, axis, [(k, k ^ step) for k in range(count)])


def swap_all(pieces, direct):
    if direct:
        return [pieces[0]] + [xor_permute(p, "dom", j) for j, p in enumerate(pieces) if j]
    stacked = lax.all_to_all(jnp.stack(pieces), "dom", 0, 0, tiled=True)
    return [stacked[j] for j in range(len(pieces))]


def packed_atoms(potential, proj_weights, atom_cell, point_codes):
    cube = 2 * REACH + 1
    off_x = point_codes // (cube * cube)
    off_y = point_codes // cube % cube
    off_z = point_codes % cube
    plane = atom_cell[:, 0:1] % SLAB + off_x
    cell_y = (atom_cell[:, 1:2] + off_y - REACH) % SIDE
    cell_z = (atom_cell[:, 2:3] + off_z - REACH) % SIDE
    lateral = cell_y * SIDE + cell_z
    return jnp.concatenate(
        [
            proj_weights.reshape(-1, 256),
            plane.astype(F32),
            lateral.astype(F32),
            jnp.zeros((4, 256), F32),
            potential.reshape(SLAB, LAT),
        ],
        axis=0,
    )


def on_device(trial_waves, potential, proj_weights, kb_energy, atom_cell, point_codes):
    nd = lax.axis_size("dom")
    bands = trial_waves.shape[-1]
    direct = nd == 8
    chunks = CHUNKS if direct else 1
    real = bands // (nd * chunks)
    nb = max(real, 8)
    total = nd * SLAB * LAT
    dom = lax.axis_index("dom") if direct else jnp.int32(0)
    band = lax.axis_index("band")
    pos = jnp.stack([dom, band if direct else jnp.int32(0), band // 2]).astype(jnp.int32)
    pos_band = jnp.stack([dom, band, band // 2]).astype(jnp.int32)
    R = SLAB * nb

    packed = packed_atoms(potential, proj_weights, atom_cell, point_codes)
    if direct:
        gathered = lax.dynamic_slice_in_dim(packed, band % 2 * 16, 16, 0)[None]
        for step in (1, 2, 4):
            gathered = jnp.concatenate([gathered, xor_permute(gathered, "dom", step)])
        parts = [gathered, xor_permute(gathered, "band", 1)]
    else:
        gathered = lax.all_gather(packed, "dom", axis=0)
        parts = [gathered[:, :16], gathered[:, 16:]]

    waves = trial_waves.reshape(SLAB, LAT, bands)
    if direct:
        cut = call(
            functools.partial(split_kernel, nd, nb, chunks),
            [shape(R, LAT)] * (nd * chunks),
            [pos, waves],
            [pltpu.VMEM((SLAB, bands, LAT), F32)],
            "split",
        )
    else:
        turned = waves.transpose(0, 2, 1).reshape(SLAB, nd, real, LAT).transpose(1, 0, 2, 3)
        cut = [turned[j] for j in range(nd)]

    wh, wl, shifted = call(
        functools.partial(weights_kernel, nd),
        [shape(nd * 256, 256, dtype=BF16), shape(nd * 256, 256, dtype=BF16), shape(nd * SLAB, LAT)],
        [pos] + parts,
        [pltpu.VMEM((nd, 32, 256), F32)],
        "weights",
    )
    lh, ll = split_const(lateral_matrix())
    fold = jnp.asarray(fold_matrix()).astype(BF16)
    kb_row = jnp.concatenate([kb_energy, kb_energy, jnp.zeros((112,), F32)])[None]
    spread = fold
    arrived = [swap_all(cut[c * nd : (c + 1) * nd], direct) for c in range(chunks)]
    for c in range(chunks):
        pieces = arrived[c]
        if not direct:
            pieces = [jnp.pad(p, ((0, 0), (0, nb - real), (0, 0))).reshape(R, LAT) for p in pieces]
        ready = call(
            functools.partial(filter_kernel, nd, nb, float(total)),
            [shape(R, LAT)] * nd,
            [pos, kb_row, shifted, wh, wl, lh, ll, fold, spread] + pieces,
            [
                pltpu.VMEM(((nd * SLAB + 2 * HALO) * nb, LAT), F32),
                pltpu.VMEM(((nd * SLAB + 2 * HALO) * nb, LAT), F32),
                pltpu.VMEM((nd * nb, 256), F32),
                pltpu.VMEM((nd * nb, 256), F32),
            ],
            "filter",
        )
        if not direct:
            ready = [p.reshape(SLAB, nb, LAT)[:, :real] for p in ready]
        back = swap_all(ready, direct)
    if direct:
        filtered, correlation = finish_direct(back, pos, nb, bands, float(total))
    else:
        filtered, correlation = finish_plain(jnp.concatenate(back, axis=1), pos_band, band, bands, float(total))
    return filtered.reshape(trial_waves.shape), correlation


def finish_direct(back, pos, nb, bands, total):
    group = len(back) // 2
    half = SLAB // 2

    def exchanged(pieces):
        z, send = call(
            functools.partial(join_kernel, group, nb),
            [shape(SLAB, group * nb, LAT), shape(half, group * nb, LAT)],
            [pos] + pieces,
            (),
            "join",
        )
        far = xor_permute(send, "band", 2)
        return z, xor_permute(z, "band", 1), far, xor_permute(far, "band", 1)

    z_near, core_near, far_near, far_core_near = exchanged(back[:group])
    z_far, core_far, far_far, far_core_far = exchanged(back[group:])
    part = shape(2, bands // 2, bands)
    block = pltpu.VMEM((2, bands, bands), F32)
    z, z_core, own_keep, own_send = call(
        own_kernel,
        [shape(SLAB, bands, LAT), shape(SLAB, bands, LAT), part, part],
        [pos, z_near, z_far, core_near, core_far],
        [block],
        "own",
    )
    gram, share = call(
        cross_kernel,
        [shape(2, bands, bands), shape(2, bands, bands)],
        [pos, z, z_core, far_near, far_far, far_core_near, far_core_far],
        [pltpu.VMEM((half, bands, LAT), F32), pltpu.VMEM((half, bands, LAT), F32)],
        "cross",
    )
    cross_keep, cross_send = call(
        part_kernel, [part, part], [pos, gram, xor_permute(share, "band", 2)], [block], "part"
    )

    def summed(keep, send):
        rows = keep + xor_permute(send, "dom", 1)
        rows = rows + xor_permute(rows, "dom", 2)
        rows = rows + xor_permute(rows, "dom", 4)
        return [rows, xor_permute(rows, "dom", 1)]

    rows = summed(own_keep, own_send) + summed(cross_keep, cross_send)
    filtered = call(output_kernel, shape(SLAB, LAT, bands), [z], (), "output")
    correlation = call(functools.partial(place_kernel, total), shape(bands, 4 * bands), [pos] + rows, (), "place")
    return filtered, correlation


def finish_plain(z, pos, band, bands, total):
    send = lax.dynamic_slice_in_dim(z, (1 - band // 2) * (SLAB // 2), SLAB // 2, 0)
    far = xor_permute(send, "band", 2)
    gram, gram_far = call(
        gram_kernel,
        [shape(4, bands, bands), shape(2, bands, bands)],
        [pos, z, xor_permute(z, "band", 1), far, xor_permute(far, "band", 1)],
        (),
        "gram",
    )
    filtered = call(output_kernel, shape(SLAB, LAT, bands), [z], (), "output")
    start = (1 - band // 2) * 2
    cross = lax.dynamic_slice_in_dim(gram, start, 2, 0) + xor_permute(gram_far, "band", 2)
    gram = lax.dynamic_update_slice_in_dim(gram, cross, start, 0)
    wide = gram.transpose(1, 0, 2).reshape(bands, 4 * bands)
    return filtered, lax.psum(wide, "dom") / total


def solution(mesh):
    return jax.shard_map(
        on_device,
        mesh=mesh,
        in_specs=(
            P("dom", None, None, "band"),
            P("dom", None, None),
            P("dom", None, None),
            P(),
            P("dom", None),
            P("dom", None),
        ),
        out_specs=(P("dom", None, None, "band"), P("band", None)),
        check_vma=False,
    )
```

```python
import functools

import jax
import jax.numpy as jnp
import numpy as np
from jax import lax
from jax.experimental import pallas as pl
from jax.experimental.pallas import tpu as pltpu
from jax.sharding import PartitionSpec as P

HALO = 6
REACH = 4
SLAB = 8
SIDE = 16
LAT = SIDE * SIDE
ORDER = (5, 6, 7, 1, 2, 3, 4)

COEFFS = (
    -5369.0 / 1800.0,
    12.0 / 7.0,
    -15.0 / 56.0,
    10.0 / 189.0,
    -1.0 / 112.0,
    2.0 / 1925.0,
    -1.0 / 16632.0,
)
FILTER_LOWER = 5.0
FILTER_UPPER = 24.0
SPECTRUM_BOTTOM = 0.0
EPSILON = 1e-06

HALF_WIDTH = (FILTER_UPPER - FILTER_LOWER) / 2.0
CENTRE = (FILTER_UPPER + FILTER_LOWER) / 2.0
SIGMA_1 = HALF_WIDTH / (SPECTRUM_BOTTOM - CENTRE)
SIGMA_2 = 1.0 / (2.0 / SIGMA_1 - SIGMA_1)

VMEM_LIMIT = 48 * 1024 * 1024
BF16 = jnp.bfloat16
F32 = jnp.float32
NN = (((1,), (0,)), ((), ()))
NT = (((1,), (1,)), ((), ()))


def dot(a, b, dims=NN):
    return lax.dot_general(a, b, dims, preferred_element_type=F32)


def halves(x):
    hi = x.astype(BF16)
    return hi, (x - hi.astype(F32)).astype(BF16)


def dot3(ah, al, bh, bl, dims=NN):
    return dot(ah, bh, dims) + dot(al, bh, dims) + dot(ah, bl, dims)


def lateral_matrix():
    line = np.zeros((SIDE, SIDE))
    at = np.arange(SIDE)
    for k in range(1, HALO + 1):
        for sign in (1, -1):
            np.add.at(line, ((at + sign * k) % SIDE, at), -0.5 * COEFFS[k])
    eye = np.eye(SIDE)
    return np.kron(line, eye) + np.kron(eye, line)


def relation():
    return [[-1, 0] if q < REACH else [0, 1] for q in range(SLAB)]


def fold_matrix():
    out = np.zeros((256, 384), np.float32)
    for q, pair in enumerate(relation()):
        for half, rel in enumerate(pair):
            for r in range(16):
                out[q * 32 + half * 16 + r, (rel + 1) * 128 + r] = 1.0
    return out


def split_const(matrix):
    matrix = np.asarray(matrix, np.float32)
    hi = jnp.asarray(matrix, F32).astype(BF16)
    lo = (jnp.asarray(matrix, F32) - hi.astype(F32)).astype(BF16)
    return hi, lo


def split_kernel(nd, nb, pos_ref, cell_ref, x_ref, v_ref, w_ref, code_ref, mine_ref, *refs):
    outs, (scratch, packed) = refs[:-2], refs[-2:]
    i, core = pos_ref[0], pos_ref[1] & 1
    cube = 2 * REACH + 1
    code = code_ref[...].astype(F32)
    off_x = jnp.floor((code + 0.5) * (1.0 / (cube * cube)))
    rest = code - off_x * (cube * cube)
    off_y = jnp.floor((rest + 0.5) * (1.0 / cube))
    off_z = rest - off_y * cube
    for a in range(2):
        packed[a * 8 : a * 8 + 8] = w_ref[a]
        cell_x, cell_y, cell_z = (
            lax.rem(cell_ref[a, k], n).astype(F32) for k, n in enumerate((SLAB, SIDE, SIDE))
        )
        y = off_y[a : a + 1] + (cell_y + float(SIDE - REACH))
        z = off_z[a : a + 1] + (cell_z + float(SIDE - REACH))
        y = y - SIDE * jnp.floor(y * (1.0 / SIDE))
        z = z - SIDE * jnp.floor(z * (1.0 / SIDE))
        packed[16 + a : 17 + a] = off_x[a : a + 1] + cell_x
        packed[18 + a : 19 + a] = y * SIDE + z
    packed[20:24] = jnp.zeros((4, LAT), F32)
    packed[24:32] = jnp.concatenate([v_ref[:, y, :] for y in range(SIDE)], axis=1)
    mine_ref[0] = packed[pl.ds(pl.multiple_of(core * 16, 16), 16)]
    for q in range(SLAB):
        scratch[q] = x_ref[q].T
    for j in range(nd):
        start = (i ^ j) * nb
        for q in range(SLAB):
            outs[j][q * nb : (q + 1) * nb] = scratch[q, pl.ds(pl.multiple_of(start, nb), nb)]


def weights_kernel(nd, pos_ref, *refs):
    parts, (wh_ref, wl_ref, v_ref, scratch) = refs[:2], refs[2:]
    i, core = pos_ref[0], pos_ref[1] & 1
    for jb in range(2):
        rows = pl.ds(pl.multiple_of((core ^ jb) * 16, 16), 16)
        for j in range(nd):
            scratch[i ^ j, rows] = parts[jb][j]
    lat = lax.broadcasted_iota(jnp.int32, (LAT, 256), 0).astype(F32)
    plane = lax.broadcasted_iota(jnp.int32, (16, 1, 1), 0).astype(F32)
    diagonal = -1.5 * COEFFS[0] - CENTRE

    def body(s, carry):
        his, los = [], []
        for a in range(2):
            w = scratch[s, a * 8 : a * 8 + 8]
            px = scratch[s, 16 + a : 17 + a]
            place = scratch[s, 18 + a : 19 + a]
            hot = jnp.where(lat == place, 1.0, 0.0).astype(BF16)
            masked = jnp.where(px[None] == plane, w[None], 0.0).reshape(128, 256)
            mh, ml = halves(masked)
            his.append(dot(mh, hot, NT).reshape(16, 8, LAT))
            los.append(dot(ml, hot, NT).reshape(16, 8, LAT))
        hi = jnp.concatenate(his, axis=1).astype(BF16)
        lo = jnp.concatenate(los, axis=1).astype(BF16)
        for t in range(16):
            p = (s * SLAB - REACH + t + nd * SLAB) % (nd * SLAB) if isinstance(s, int) else lax.rem(
                s * SLAB - REACH + t + nd * SLAB, nd * SLAB
            )
            row = pl.ds(pl.multiple_of(p * 32 + (16 if t < SLAB else 0), 16), 16)
            wh_ref[row] = hi[t]
            wl_ref[row] = lo[t]
        v_ref[pl.ds(pl.multiple_of(s * SLAB, SLAB), SLAB)] = scratch[s, 24:32] + diagonal
        return carry

    if nd <= 8:
        for s in range(nd):
            body(s, 0)
    else:
        lax.fori_loop(0, nd, body, 0)


def filter_kernel(nd, nb, total, pos_ref, kb_ref, v_ref, wh_ref, wl_ref, lh_ref, ll_ref, fold_ref, spread_ref, *refs):
    pieces, outs = refs[:nd], refs[nd : 2 * nd]
    f0_ref, f1_ref, fold_out, spread_out = refs[2 * nd :]
    i = pos_ref[0]
    R = SLAB * nb
    rows_q = lax.broadcasted_iota(jnp.int32, (SLAB, nb, 256), 0)
    lanes_q = lax.broadcasted_iota(jnp.int32, (SLAB, nb, 256), 2) // 32
    same = rows_q == lanes_q

    def slab_rows(s, k=0):
        return pl.ds(pl.multiple_of((s * SLAB + HALO + k) * nb, nb), R)

    def wrap(ref):
        ref[0 : HALO * nb] = ref[nd * R : nd * R + HALO * nb]
        ref[HALO * nb + nd * R : 2 * HALO * nb + nd * R] = ref[HALO * nb : 2 * HALO * nb]

    def each(body):
        if nd <= 8:
            for s in range(nd):
                body(s)
        else:
            lax.fori_loop(0, nd, lambda s, c: (body(s), c)[1], 0)

    for j in range(nd):
        f0_ref[slab_rows(i ^ j)] = pieces[j][...]
    wrap(f0_ref)

    def apply(ref, finish):
        def project(s):
            fh, fl = halves(ref[slab_rows(s)])
            w = pl.ds(pl.multiple_of(s * 256, 256), 256)
            g = dot3(fh, fl, wh_ref[w], wl_ref[w], NT).reshape(SLAB, nb, 256)
            fold_out[pl.ds(pl.multiple_of(s * nb, nb), nb)] = jnp.sum(jnp.where(same, g, 0.0), axis=0)

        each(project)
        gh, gl = halves(fold_out[...])
        h = dot(gh, fold_ref[...]) + dot(gl, fold_ref[...])
        below, at, above = h[:, :128], h[:, 128:256], h[:, 256:]

        def next_slab(x):
            return jnp.concatenate([x[-nb:], x[:-nb]], axis=0)

        def previous_slab(x):
            return jnp.concatenate([x[nb:], x[:nb]], axis=0)

        p = (at + next_slab(above) + previous_slab(below)) * kb_ref[...]
        wide = jnp.concatenate([next_slab(p), p, previous_slab(p)], axis=1)
        ph, plo = halves(wide)
        spread_out[...] = dot(ph, spread_ref[...], NT) + dot(plo, spread_ref[...], NT)

        def step(s):
            f = ref[slab_rows(s)]
            fh, fl = halves(f)
            x = jnp.where(same, spread_out[pl.ds(pl.multiple_of(s * nb, nb), nb)][None], 0.0).reshape(R, 256)
            xh, xl = halves(x)
            w = pl.ds(pl.multiple_of(s * 256, 256), 256)
            acc = dot3(xh, xl, wh_ref[w], wl_ref[w]) + dot3(fh, fl, lh_ref[...], ll_ref[...])
            v = v_ref[pl.ds(pl.multiple_of(s * SLAB, SLAB), SLAB)]
            acc = acc + (f.reshape(SLAB, nb, LAT) * v[:, None, :]).reshape(R, LAT)
            for k in range(1, HALO + 1):
                acc = acc + (-0.5 * COEFFS[k]) * (ref[slab_rows(s, k)] + ref[slab_rows(s, -k)])
            finish(s, acc)

        each(step)

    def first(s, acc):
        f1_ref[slab_rows(s)] = (SIGMA_1 / HALF_WIDTH) * acc

    apply(f0_ref, first)
    wrap(f1_ref)

    def second(s, acc):
        f0_ref_new = (2.0 * SIGMA_2 / HALF_WIDTH) * acc - (SIGMA_1 * SIGMA_2) * f0_ref[slab_rows(s)]
        y2_store(s, f0_ref_new)

    def y2_store(s, value):
        f0_ref[slab_rows(s)] = value

    apply(f1_ref, second)
    square = jnp.zeros((nb, LAT), F32)
    if nd <= 8:
        for s in range(nd):
            y = f0_ref[slab_rows(s)].reshape(SLAB, nb, LAT)
            square = square + jnp.sum(y * y, axis=0)
    else:

        def add(s, total_square):
            y = f0_ref[slab_rows(s)].reshape(SLAB, nb, LAT)
            return total_square + jnp.sum(y * y, axis=0)

        square = lax.fori_loop(0, nd, add, square)
    scale = 1.0 / jnp.sqrt(jnp.sum(square, axis=1, keepdims=True) / total + EPSILON)
    for j in range(nd):
        y = f0_ref[slab_rows(i ^ j)].reshape(SLAB, nb, LAT)
        outs[j][...] = (y * scale[None]).reshape(R, LAT)


def join_kernel(count, nb, ties, pos_ref, *refs):
    pieces, (z_ref, send_ref) = refs[:count], refs[count + ties :]
    i, y = pos_ref[0], pos_ref[2]
    for j in range(count):
        rows = pl.ds(pl.multiple_of(((i ^ j) & (count - 1)) * nb, nb), nb)
        for q in range(SLAB):
            z_ref[q, rows] = pieces[j][q * nb : (q + 1) * nb]
    half = SLAB // 2
    for q in range(half):
        send_ref[q] = z_ref[(1 - y) * half + q]


def place_halves(pos_ref, near, far, out):
    h = pos_ref[0] // 4
    for q in range(out.shape[0]):
        out[q, pl.ds(pl.multiple_of(h * 64, 64), 64)] = near[q]
        out[q, pl.ds(pl.multiple_of((1 - h) * 64, 64), 64)] = far[q]


def own_kernel(pos_ref, near, far, core_near, core_far, z_ref, zc_ref, keep_ref, send_ref, g_ref):
    i, b = pos_ref[0], pos_ref[1]
    place_halves(pos_ref, near, far, z_ref)
    place_halves(pos_ref, core_near, core_far, zc_ref)
    own = core = None
    for q in range(SLAB):
        zh, zl = halves(z_ref[q])
        ch, cl = halves(zc_ref[q])
        mine, other = dot3(zh, zl, zh, zl, NT), dot3(zh, zl, ch, cl, NT)
        own, core = (mine, other) if own is None else (own + mine, core + other)
    g_ref[b & 1] = own
    g_ref[(b & 1) ^ 1] = core
    cut_rows(i, g_ref, keep_ref, send_ref)


def cut_rows(i, g_ref, keep_ref, send_ref):
    x = i & 1
    for c in range(2):
        keep_ref[c] = g_ref[c, pl.ds(pl.multiple_of(x * 64, 64), 64)]
        send_ref[c] = g_ref[c, pl.ds(pl.multiple_of((1 - x) * 64, 64), 64)]


def cross_kernel(
    pos_ref, z_ref, zc_ref, near, far, core_near, core_far, tie, keep, send, back, back_send, g_ref, back_ref, f_ref, fc_ref
):
    i, b, y = pos_ref[0], pos_ref[1], pos_ref[2]
    half = SLAB // 2
    place_halves(pos_ref, near, far, f_ref)
    place_halves(pos_ref, core_near, core_far, fc_ref)
    totals = None
    for q in range(half):
        zh, zl = halves(z_ref[y * half + q])
        ch, cl = halves(zc_ref[y * half + q])
        fh, fl = halves(f_ref[q])
        gh, gl = halves(fc_ref[q])
        now = (
            dot3(zh, zl, fh, fl, NT),
            dot3(zh, zl, gh, gl, NT),
            dot3(fh, fl, zh, zl, NT),
            dot3(fh, fl, ch, cl, NT),
        )
        totals = now if totals is None else tuple(t + n for t, n in zip(totals, now))
    c = b & 1
    g_ref[c], g_ref[c ^ 1], back_ref[c], back_ref[c ^ 1] = totals
    cut_rows(i, g_ref, keep, send)
    cut_rows(i, back_ref, back, back_send)


def sum_kernel(a_ref, b_ref, c_ref, d_ref, tie, out_ref):
    out_ref[...] = (a_ref[...] + b_ref[...]) + (c_ref[...] + d_ref[...])


def pair_kernel(total, pos_ref, own, cross, cross_other, out_ref):
    y = pos_ref[2]
    for c in range(2):
        out_ref[y * 2 + c] = own[c] * (1.0 / total)
        out_ref[(1 - y) * 2 + c] = (cross[c] + cross_other[c]) * (1.0 / total)


def output_kernel(z_ref, out_ref):
    for q in range(SLAB):
        out_ref[q] = z_ref[q].T


def place_kernel(pos_ref, mine, other, out_ref):
    x = pos_ref[0] & 1
    for k in range(4):
        lanes = slice(k * 128, (k + 1) * 128)
        out_ref[pl.ds(pl.multiple_of(x * 64, 64), 64), lanes] = mine[k]
        out_ref[pl.ds(pl.multiple_of((1 - x) * 64, 64), 64), lanes] = other[k]


def gram_kernel(pos_ref, own, core, far, far_core, g_ref, far_ref):
    b, y = pos_ref[1], pos_ref[2]
    half = SLAB // 2

    def add(totals, place, value):
        totals[place] = value if totals.get(place) is None else totals[place] + value

    totals = {}
    for q in range(half):
        for mine in (True, False):
            at = q + y * half if mine else q + (1 - y) * half
            zh, zl = halves(own[at])
            ch, cl = halves(core[at])
            add(totals, "own", dot3(zh, zl, zh, zl, NT))
            add(totals, "core", dot3(zh, zl, ch, cl, NT))
            if mine:
                fh, fl = halves(far[q])
                gh, gl = halves(far_core[q])
                add(totals, "far", dot3(zh, zl, fh, fl, NT))
                add(totals, "far_core", dot3(zh, zl, gh, gl, NT))
                add(totals, "back", dot3(fh, fl, zh, zl, NT))
                add(totals, "back_core", dot3(fh, fl, ch, cl, NT))
    g_ref[b] = totals["own"]
    g_ref[b ^ 1] = totals["core"]
    g_ref[b ^ 2] = totals["far"]
    g_ref[b ^ 3] = totals["far_core"]
    far_ref[b & 1] = totals["back"]
    far_ref[(b & 1) ^ 1] = totals["back_core"]


def call(kernel, out_shape, operands, scratch=(), name=None, ties=()):
    specs = [
        pl.BlockSpec(memory_space=pltpu.SMEM if o.dtype == jnp.int32 and o.size < 128 else pltpu.VMEM) for o in operands
    ] + [pl.BlockSpec(memory_space=pl.ANY) for _ in ties]
    single = not isinstance(out_shape, (list, tuple))
    return pl.pallas_call(
        kernel,
        out_shape=out_shape,
        in_specs=specs,
        out_specs=(
            pl.BlockSpec(memory_space=pltpu.VMEM)
            if single
            else [pl.BlockSpec(memory_space=pltpu.VMEM) for _ in out_shape]
        ),
        scratch_shapes=list(scratch),
        compiler_params=pltpu.CompilerParams(vmem_limit_bytes=VMEM_LIMIT),
        name=name,
    )(*operands, *ties)


def shape(*dims, dtype=F32):
    return jax.ShapeDtypeStruct(dims, dtype)


def xor_permute(value, axis, step):
    count = lax.axis_size(axis)
    return lax.ppermute(value, axis, [(k, k ^ step) for k in range(count)])


def both_permute(value):
    nd, ng = lax.axis_size("dom"), lax.axis_size("band")
    pairs = [(b * nd + d, (b ^ 2) * nd + (d ^ 1)) for b in range(ng) for d in range(nd)]
    return lax.ppermute(value, ("band", "dom"), pairs)


def swap_all(pieces, direct):
    if direct:
        got = {0: pieces[0]}
        for j in ORDER:
            got[j] = xor_permute(pieces[j], "dom", j)
        return [got[j] for j in range(len(pieces))]
    stacked = lax.all_to_all(jnp.stack(pieces), "dom", 0, 0, tiled=True)
    return [stacked[j] for j in range(len(pieces))]


def packed_atoms(potential, proj_weights, atom_cell, point_codes):
    cube = 2 * REACH + 1
    off_x = point_codes // (cube * cube)
    off_y = point_codes // cube % cube
    off_z = point_codes % cube
    plane = atom_cell[:, 0:1] % SLAB + off_x
    cell_y = (atom_cell[:, 1:2] + off_y - REACH) % SIDE
    cell_z = (atom_cell[:, 2:3] + off_z - REACH) % SIDE
    lateral = cell_y * SIDE + cell_z
    return jnp.concatenate(
        [
            proj_weights.reshape(-1, 256),
            plane.astype(F32),
            lateral.astype(F32),
            jnp.zeros((4, 256), F32),
            potential.reshape(SLAB, LAT),
        ],
        axis=0,
    )


def on_device(trial_waves, potential, proj_weights, kb_energy, atom_cell, point_codes):
    nd = lax.axis_size("dom")
    bands = trial_waves.shape[-1]
    direct = nd == 8
    real = bands // nd
    nb = max(real, 8)
    total = nd * SLAB * LAT
    dom = lax.axis_index("dom") if direct else jnp.int32(0)
    band = lax.axis_index("band")
    pos = jnp.stack([dom, band if direct else jnp.int32(0), band // 2]).astype(jnp.int32)
    pos_band = jnp.stack([dom, band, band // 2]).astype(jnp.int32)
    R = SLAB * nb

    waves = trial_waves.reshape(SLAB, LAT, bands)
    if direct:
        gathered, *cut = call(
            functools.partial(split_kernel, nd, nb),
            [shape(1, 16, 256)] + [shape(R, LAT)] * nd,
            [pos, atom_cell, waves, potential, proj_weights, point_codes],
            [pltpu.VMEM((SLAB, bands, LAT), F32), pltpu.VMEM((32, 256), F32)],
            "split",
        )
        for step in (1, 2, 4):
            gathered = jnp.concatenate([gathered, xor_permute(gathered, "dom", step)])
        parts = [gathered, xor_permute(gathered, "band", 1)]
    else:
        packed = packed_atoms(potential, proj_weights, atom_cell, point_codes)
        gathered = lax.all_gather(packed, "dom", axis=0)
        parts = [gathered[:, :16], gathered[:, 16:]]
        turned = waves.transpose(0, 2, 1).reshape(SLAB, nd, real, LAT).transpose(1, 0, 2, 3)
        cut = [turned[j] for j in range(nd)]

    wh, wl, shifted = call(
        functools.partial(weights_kernel, nd),
        [shape(nd * 256, 256, dtype=BF16), shape(nd * 256, 256, dtype=BF16), shape(nd * SLAB, LAT)],
        [pos] + parts,
        [pltpu.VMEM((nd, 32, 256), F32)],
        "weights",
    )
    lh, ll = split_const(lateral_matrix())
    fold = jnp.asarray(fold_matrix()).astype(BF16)
    kb_row = jnp.concatenate([kb_energy, kb_energy, jnp.zeros((112,), F32)])[None]
    spread = fold
    pieces = swap_all(cut, direct)
    if not direct:
        pieces = [jnp.pad(p, ((0, 0), (0, nb - real), (0, 0))).reshape(R, LAT) for p in pieces]
    ready = call(
        functools.partial(filter_kernel, nd, nb, float(total)),
        [shape(R, LAT)] * nd,
        [pos, kb_row, shifted, wh, wl, lh, ll, fold, spread] + pieces,
        [
            pltpu.VMEM(((nd * SLAB + 2 * HALO) * nb, LAT), F32),
            pltpu.VMEM(((nd * SLAB + 2 * HALO) * nb, LAT), F32),
            pltpu.VMEM((nd * nb, 256), F32),
            pltpu.VMEM((nd * nb, 256), F32),
        ],
        "filter",
    )
    if not direct:
        ready = [p.reshape(SLAB, nb, LAT)[:, :real] for p in ready]
    back = swap_all(ready, direct)
    if direct:
        filtered, correlation = finish_direct(back, pos, nb, bands, float(total))
    else:
        filtered, correlation = finish_plain(jnp.concatenate(back, axis=1), pos_band, band, bands, float(total))
    return filtered.reshape(trial_waves.shape), correlation


def finish_direct(back, pos, nb, bands, total):
    group = len(back) // 2
    half = SLAB // 2

    def exchanged(pieces, ties):
        z, send = call(
            functools.partial(join_kernel, group, nb, len(ties)),
            [shape(SLAB, group * nb, LAT), shape(half, group * nb, LAT)],
            [pos] + pieces,
            (),
            "join",
            ties,
        )
        far = xor_permute(send, "band", 2)
        return z, xor_permute(z, "band", 1), far, xor_permute(far, "band", 1)

    z_near, core_near, far_near, far_core_near = exchanged(back[:group], [])
    z_far, core_far, far_far, far_core_far = exchanged(back[group:], [far_near])
    part = shape(2, bands // 2, bands)
    block = pltpu.VMEM((2, bands, bands), F32)
    z, z_core, own_keep, own_send = call(
        own_kernel,
        [shape(SLAB, bands, LAT), shape(SLAB, bands, LAT), part, part],
        [pos, z_near, z_far, core_near, core_far],
        [block],
        "own",
    )
    own = own_keep + xor_permute(own_send, "dom", 1)
    own_tie = own
    own = own + xor_permute(own, "dom", 2)
    own = own + xor_permute(own, "dom", 4)
    keep, send, back_keep, back_send = call(
        cross_kernel,
        [part] * 4,
        [pos, z, z_core, far_near, far_far, far_core_near, far_core_far],
        [block, block, pltpu.VMEM((half, bands, LAT), F32), pltpu.VMEM((half, bands, LAT), F32)],
        "cross",
        [own_tie],
    )
    cross = call(
        sum_kernel,
        part,
        [
            keep,
            xor_permute(send, "dom", 1),
            xor_permute(back_keep, "band", 2),
            both_permute(back_send),
        ],
        (),
        "sum",
        [own],
    )
    cross = cross + xor_permute(cross, "dom", 2)
    rows = call(
        functools.partial(pair_kernel, total),
        shape(4, bands // 2, bands),
        [pos, own, cross, xor_permute(cross, "dom", 4)],
        (),
        "pair",
    )
    filtered = call(output_kernel, shape(SLAB, LAT, bands), [z], (), "output")
    correlation = call(place_kernel, shape(bands, 4 * bands), [pos, rows, xor_permute(rows, "dom", 1)], (), "place")
    return filtered, correlation


def finish_plain(z, pos, band, bands, total):
    send = lax.dynamic_slice_in_dim(z, (1 - band // 2) * (SLAB // 2), SLAB // 2, 0)
    far = xor_permute(send, "band", 2)
    gram, gram_far = call(
        gram_kernel,
        [shape(4, bands, bands), shape(2, bands, bands)],
        [pos, z, xor_permute(z, "band", 1), far, xor_permute(far, "band", 1)],
        (),
        "gram",
    )
    filtered = call(output_kernel, shape(SLAB, LAT, bands), [z], (), "output")
    start = (1 - band // 2) * 2
    cross = lax.dynamic_slice_in_dim(gram, start, 2, 0) + xor_permute(gram_far, "band", 2)
    gram = lax.dynamic_update_slice_in_dim(gram, cross, start, 0)
    wide = gram.transpose(1, 0, 2).reshape(bands, 4 * bands)
    return filtered, lax.psum(wide, "dom") / total


def solution(mesh):
    return jax.shard_map(
        on_device,
        mesh=mesh,
        in_specs=(
            P("dom", None, None, "band"),
            P("dom", None, None),
            P("dom", None, None),
            P(),
            P("dom", None),
            P("dom", None),
        ),
        out_specs=(P("dom", None, None, "band"), P("band", None)),
        check_vma=False,
    )
```

```python
import functools

import jax
import jax.numpy as jnp
import numpy as np
from jax import lax
from jax.experimental import pallas as pl
from jax.experimental.pallas import tpu as pltpu
from jax.sharding import PartitionSpec as P

HALO = 6
REACH = 4
SLAB = 8
SIDE = 16
LAT = SIDE * SIDE

COEFFS = (
    -5369.0 / 1800.0,
    12.0 / 7.0,
    -15.0 / 56.0,
    10.0 / 189.0,
    -1.0 / 112.0,
    2.0 / 1925.0,
    -1.0 / 16632.0,
)
FILTER_LOWER = 5.0
FILTER_UPPER = 24.0
SPECTRUM_BOTTOM = 0.0
EPSILON = 1e-06

HALF_WIDTH = (FILTER_UPPER - FILTER_LOWER) / 2.0
CENTRE = (FILTER_UPPER + FILTER_LOWER) / 2.0
SIGMA_1 = HALF_WIDTH / (SPECTRUM_BOTTOM - CENTRE)
SIGMA_2 = 1.0 / (2.0 / SIGMA_1 - SIGMA_1)

VMEM_LIMIT = 48 * 1024 * 1024
BF16 = jnp.bfloat16
F32 = jnp.float32
NN = (((1,), (0,)), ((), ()))
NT = (((1,), (1,)), ((), ()))


def dot(a, b, dims=NN):
    return lax.dot_general(a, b, dims, preferred_element_type=F32)


def halves(x):
    hi = x.astype(BF16)
    return hi, (x - hi.astype(F32)).astype(BF16)


def dot3(ah, al, bh, bl, dims=NN):
    return dot(ah, bh, dims) + dot(al, bh, dims) + dot(ah, bl, dims)


def lateral_matrix():
    line = np.zeros((SIDE, SIDE))
    at = np.arange(SIDE)
    for k in range(1, HALO + 1):
        for sign in (1, -1):
            np.add.at(line, ((at + sign * k) % SIDE, at), -0.5 * COEFFS[k])
    eye = np.eye(SIDE)
    return np.kron(line, eye) + np.kron(eye, line)


def relation():
    return [[-1, 0] if q < REACH else [0, 1] for q in range(SLAB)]


def fold_matrix():
    out = np.zeros((256, 384), np.float32)
    for q, pair in enumerate(relation()):
        for half, rel in enumerate(pair):
            for r in range(16):
                out[q * 32 + half * 16 + r, (rel + 1) * 128 + r] = 1.0
    return out


def split_const(matrix):
    matrix = np.asarray(matrix, np.float32)
    hi = jnp.asarray(matrix, F32).astype(BF16)
    lo = (jnp.asarray(matrix, F32) - hi.astype(F32)).astype(BF16)
    return hi, lo


def split_kernel(nd, nb, pos_ref, cell_ref, x_ref, v_ref, w_ref, code_ref, *refs):
    outs, (scratch, packed) = refs[:-2], refs[-2:]
    i = pos_ref[0]
    cube = 2 * REACH + 1
    code = code_ref[...].astype(F32)
    off_x = jnp.floor((code + 0.5) * (1.0 / (cube * cube)))
    rest = code - off_x * (cube * cube)
    off_y = jnp.floor((rest + 0.5) * (1.0 / cube))
    off_z = rest - off_y * cube
    for a in range(2):
        packed[a * 8 : a * 8 + 8] = w_ref[a]
        cell_x, cell_y, cell_z = (
            lax.rem(cell_ref[a, k], n).astype(F32) for k, n in enumerate((SLAB, SIDE, SIDE))
        )
        y = off_y[a : a + 1] + (cell_y + float(SIDE - REACH))
        z = off_z[a : a + 1] + (cell_z + float(SIDE - REACH))
        y = y - SIDE * jnp.floor(y * (1.0 / SIDE))
        z = z - SIDE * jnp.floor(z * (1.0 / SIDE))
        packed[16 + a : 17 + a] = off_x[a : a + 1] + cell_x
        packed[18 + a : 19 + a] = y * SIDE + z
    packed[20:24] = jnp.zeros((4, LAT), F32)
    packed[24:32] = jnp.concatenate([v_ref[:, y, :] for y in range(SIDE)], axis=1)
    for q in range(SLAB):
        scratch[q] = x_ref[q].T
    for j in range(nd):
        start = (i ^ j) * nb
        for q in range(SLAB):
            outs[j][q * nb : (q + 1) * nb] = scratch[q, pl.ds(pl.multiple_of(start, nb), nb)]
        outs[j][SLAB * nb :] = packed[...]


def build_projectors(nd, scratch, wh_ref, wl_ref, v_ref):
    lat = lax.broadcasted_iota(jnp.int32, (LAT, 256), 0).astype(F32)
    plane = lax.broadcasted_iota(jnp.int32, (16, 1, 1), 0).astype(F32)
    diagonal = -1.5 * COEFFS[0] - CENTRE

    def body(s, carry):
        his, los = [], []
        for a in range(2):
            w = scratch[s, a * 8 : a * 8 + 8]
            px = scratch[s, 16 + a : 17 + a]
            place = scratch[s, 18 + a : 19 + a]
            hot = jnp.where(lat == place, 1.0, 0.0).astype(BF16)
            masked = jnp.where(px[None] == plane, w[None], 0.0).reshape(128, 256)
            mh, ml = halves(masked)
            his.append(dot(mh, hot, NT).reshape(16, 8, LAT))
            los.append(dot(ml, hot, NT).reshape(16, 8, LAT))
        hi = jnp.concatenate(his, axis=1).astype(BF16)
        lo = jnp.concatenate(los, axis=1).astype(BF16)
        for t in range(16):
            p = (s * SLAB - REACH + t + nd * SLAB) % (nd * SLAB) if isinstance(s, int) else lax.rem(
                s * SLAB - REACH + t + nd * SLAB, nd * SLAB
            )
            row = pl.ds(pl.multiple_of(p * 32 + (16 if t < SLAB else 0), 16), 16)
            wh_ref[row] = hi[t]
            wl_ref[row] = lo[t]
        v_ref[pl.ds(pl.multiple_of(s * SLAB, SLAB), SLAB)] = scratch[s, 24:32] + diagonal
        return carry

    if nd <= 8:
        for s in range(nd):
            body(s, 0)
    else:
        lax.fori_loop(0, nd, body, 0)


def filter_kernel(nd, nb, total, pos_ref, kb_ref, lh_ref, ll_ref, fold_ref, *refs):
    pieces, outs = refs[:nd], refs[nd : 2 * nd]
    f0_ref, f1_ref, fold_out, spread_out, wh_ref, wl_ref, v_ref, packed = refs[2 * nd :]
    i = pos_ref[0]
    R = SLAB * nb
    rows_q = lax.broadcasted_iota(jnp.int32, (SLAB, nb, 256), 0)
    lanes_q = lax.broadcasted_iota(jnp.int32, (SLAB, nb, 256), 2) // 32
    same = rows_q == lanes_q

    def slab_rows(s, k=0):
        return pl.ds(pl.multiple_of((s * SLAB + HALO + k) * nb, nb), R)

    def wrap(ref):
        ref[0 : HALO * nb] = ref[nd * R : nd * R + HALO * nb]
        ref[HALO * nb + nd * R : 2 * HALO * nb + nd * R] = ref[HALO * nb : 2 * HALO * nb]

    def each(body):
        if nd <= 8:
            for s in range(nd):
                body(s)
        else:
            lax.fori_loop(0, nd, lambda s, c: (body(s), c)[1], 0)

    for j in range(nd):
        f0_ref[slab_rows(i ^ j)] = pieces[j][:R]
        packed[i ^ j] = pieces[j][R:]
    wrap(f0_ref)
    build_projectors(nd, packed, wh_ref, wl_ref, v_ref)

    def apply(ref, finish):
        def project(s):
            fh, fl = halves(ref[slab_rows(s)])
            w = pl.ds(pl.multiple_of(s * 256, 256), 256)
            g = dot3(fh, fl, wh_ref[w], wl_ref[w], NT).reshape(SLAB, nb, 256)
            fold_out[pl.ds(pl.multiple_of(s * nb, nb), nb)] = jnp.sum(jnp.where(same, g, 0.0), axis=0)

        each(project)
        gh, gl = halves(fold_out[...])
        h = dot(gh, fold_ref[...]) + dot(gl, fold_ref[...])
        below, at, above = h[:, :128], h[:, 128:256], h[:, 256:]

        def next_slab(x):
            return jnp.concatenate([x[-nb:], x[:-nb]], axis=0)

        def previous_slab(x):
            return jnp.concatenate([x[nb:], x[:nb]], axis=0)

        p = (at + next_slab(above) + previous_slab(below)) * kb_ref[...]
        wide = jnp.concatenate([next_slab(p), p, previous_slab(p)], axis=1)
        ph, plo = halves(wide)
        spread_out[...] = dot(ph, fold_ref[...], NT) + dot(plo, fold_ref[...], NT)

        def step(s):
            f = ref[slab_rows(s)]
            fh, fl = halves(f)
            x = jnp.where(same, spread_out[pl.ds(pl.multiple_of(s * nb, nb), nb)][None], 0.0).reshape(R, 256)
            xh, xl = halves(x)
            w = pl.ds(pl.multiple_of(s * 256, 256), 256)
            acc = dot3(xh, xl, wh_ref[w], wl_ref[w]) + dot3(fh, fl, lh_ref[...], ll_ref[...])
            v = v_ref[pl.ds(pl.multiple_of(s * SLAB, SLAB), SLAB)]
            acc = acc + (f.reshape(SLAB, nb, LAT) * v[:, None, :]).reshape(R, LAT)
            for k in range(1, HALO + 1):
                acc = acc + (-0.5 * COEFFS[k]) * (ref[slab_rows(s, k)] + ref[slab_rows(s, -k)])
            finish(s, acc)

        each(step)

    def first(s, acc):
        f1_ref[slab_rows(s)] = (SIGMA_1 / HALF_WIDTH) * acc

    apply(f0_ref, first)
    wrap(f1_ref)

    def second(s, acc):
        f0_ref_new = (2.0 * SIGMA_2 / HALF_WIDTH) * acc - (SIGMA_1 * SIGMA_2) * f0_ref[slab_rows(s)]
        y2_store(s, f0_ref_new)

    def y2_store(s, value):
        f0_ref[slab_rows(s)] = value

    apply(f1_ref, second)
    square = jnp.zeros((nb, LAT), F32)
    if nd <= 8:
        for s in range(nd):
            y = f0_ref[slab_rows(s)].reshape(SLAB, nb, LAT)
            square = square + jnp.sum(y * y, axis=0)
    else:

        def add(s, total_square):
            y = f0_ref[slab_rows(s)].reshape(SLAB, nb, LAT)
            return total_square + jnp.sum(y * y, axis=0)

        square = lax.fori_loop(0, nd, add, square)
    scale = 1.0 / jnp.sqrt(jnp.sum(square, axis=1, keepdims=True) / total + EPSILON)
    for j in range(nd):
        y = f0_ref[slab_rows(i ^ j)].reshape(SLAB, nb, LAT)
        outs[j][...] = (y * scale[None]).reshape(R, LAT)


def join_kernel(nd, nb, pos_ref, *refs):
    pieces, (z_ref, first_ref, second_ref) = refs[:nd], refs[nd:]
    i, y = pos_ref[0], pos_ref[2]
    for j in range(nd):
        rows = pl.ds(pl.multiple_of((i ^ j) * nb, nb), nb)
        for q in range(SLAB):
            z_ref[q, rows] = pieces[j][q * nb : (q + 1) * nb]
    half = SLAB // 2
    for q in range(half // 2):
        first_ref[q] = z_ref[(1 - y) * half + q]
        second_ref[q] = z_ref[(1 - y) * half + half // 2 + q]


def own_kernel(pos_ref, z_ref, zc_ref, keep_ref, send_ref, g_ref):
    i, b = pos_ref[0], pos_ref[1]
    own = core = None
    for q in range(SLAB):
        zh, zl = halves(z_ref[q])
        ch, cl = halves(zc_ref[q])
        mine, other = dot3(zh, zl, zh, zl, NT), dot3(zh, zl, ch, cl, NT)
        own, core = (mine, other) if own is None else (own + mine, core + other)
    g_ref[b & 1] = own
    g_ref[(b & 1) ^ 1] = core
    cut_rows(i, g_ref, keep_ref, send_ref)


def cut_rows(i, g_ref, keep_ref, send_ref):
    x = i & 1
    for c in range(2):
        keep_ref[c] = g_ref[c, pl.ds(pl.multiple_of(x * 64, 64), 64)]
        send_ref[c] = g_ref[c, pl.ds(pl.multiple_of((1 - x) * 64, 64), 64)]


def cross_kernel(
    pos_ref, z_ref, zc_ref, first, second, core_first, core_second, tie, keep, send, back, back_send, g_ref, back_ref
):
    i, b, y = pos_ref[0], pos_ref[1], pos_ref[2]
    half = SLAB // 2
    totals = None
    for q in range(half):
        zh, zl = halves(z_ref[y * half + q])
        ch, cl = halves(zc_ref[y * half + q])
        fh, fl = halves((first, second)[q // (half // 2)][q % (half // 2)])
        gh, gl = halves((core_first, core_second)[q // (half // 2)][q % (half // 2)])
        now = (
            dot3(zh, zl, fh, fl, NT),
            dot3(zh, zl, gh, gl, NT),
            dot3(fh, fl, zh, zl, NT),
            dot3(fh, fl, ch, cl, NT),
        )
        totals = now if totals is None else tuple(t + n for t, n in zip(totals, now))
    c = b & 1
    g_ref[c], g_ref[c ^ 1], back_ref[c], back_ref[c ^ 1] = totals
    cut_rows(i, g_ref, keep, send)
    cut_rows(i, back_ref, back, back_send)


def sum_kernel(a_ref, b_ref, c_ref, d_ref, tie, out_ref):
    out_ref[...] = (a_ref[...] + b_ref[...]) + (c_ref[...] + d_ref[...])


def pair_kernel(total, pos_ref, own, cross, cross_other, out_ref):
    y = pos_ref[2]
    for c in range(2):
        out_ref[y * 2 + c] = own[c] * (1.0 / total)
        out_ref[(1 - y) * 2 + c] = (cross[c] + cross_other[c]) * (1.0 / total)


def output_kernel(z_ref, out_ref):
    for q in range(SLAB):
        out_ref[q] = z_ref[q].T


def place_kernel(pos_ref, mine, other, out_ref):
    x = pos_ref[0] & 1
    for k in range(4):
        lanes = slice(k * 128, (k + 1) * 128)
        out_ref[pl.ds(pl.multiple_of(x * 64, 64), 64), lanes] = mine[k]
        out_ref[pl.ds(pl.multiple_of((1 - x) * 64, 64), 64), lanes] = other[k]


def gram_kernel(pos_ref, own, core, far, far_core, g_ref, far_ref):
    b, y = pos_ref[1], pos_ref[2]
    half = SLAB // 2

    def add(totals, place, value):
        totals[place] = value if totals.get(place) is None else totals[place] + value

    totals = {}
    for q in range(half):
        for mine in (True, False):
            at = q + y * half if mine else q + (1 - y) * half
            zh, zl = halves(own[at])
            ch, cl = halves(core[at])
            add(totals, "own", dot3(zh, zl, zh, zl, NT))
            add(totals, "core", dot3(zh, zl, ch, cl, NT))
            if mine:
                fh, fl = halves(far[q])
                gh, gl = halves(far_core[q])
                add(totals, "far", dot3(zh, zl, fh, fl, NT))
                add(totals, "far_core", dot3(zh, zl, gh, gl, NT))
                add(totals, "back", dot3(fh, fl, zh, zl, NT))
                add(totals, "back_core", dot3(fh, fl, ch, cl, NT))
    g_ref[b] = totals["own"]
    g_ref[b ^ 1] = totals["core"]
    g_ref[b ^ 2] = totals["far"]
    g_ref[b ^ 3] = totals["far_core"]
    far_ref[b & 1] = totals["back"]
    far_ref[(b & 1) ^ 1] = totals["back_core"]


def call(kernel, out_shape, operands, scratch=(), name=None, ties=()):
    specs = [
        pl.BlockSpec(memory_space=pltpu.SMEM if o.dtype == jnp.int32 and o.size < 128 else pltpu.VMEM) for o in operands
    ] + [pl.BlockSpec(memory_space=pl.ANY) for _ in ties]
    single = not isinstance(out_shape, (list, tuple))
    return pl.pallas_call(
        kernel,
        out_shape=out_shape,
        in_specs=specs,
        out_specs=(
            pl.BlockSpec(memory_space=pltpu.VMEM)
            if single
            else [pl.BlockSpec(memory_space=pltpu.VMEM) for _ in out_shape]
        ),
        scratch_shapes=list(scratch),
        compiler_params=pltpu.CompilerParams(vmem_limit_bytes=VMEM_LIMIT),
        name=name,
    )(*operands, *ties)


def shape(*dims, dtype=F32):
    return jax.ShapeDtypeStruct(dims, dtype)


def xor_permute(value, axis, step):
    count = lax.axis_size(axis)
    return lax.ppermute(value, axis, [(k, k ^ step) for k in range(count)])


def both_permute(value):
    nd, ng = lax.axis_size("dom"), lax.axis_size("band")
    pairs = [(b * nd + d, (b ^ 2) * nd + (d ^ 1)) for b in range(ng) for d in range(nd)]
    return lax.ppermute(value, ("band", "dom"), pairs)


def swap_all(pieces, direct):
    if direct:
        got = {0: pieces[0]}
        for j in range(1, len(pieces)):
            got[j] = xor_permute(pieces[j], "dom", j)
        return [got[j] for j in range(len(pieces))]
    stacked = lax.all_to_all(jnp.stack(pieces), "dom", 0, 0, tiled=True)
    return [stacked[j] for j in range(len(pieces))]


def packed_atoms(potential, proj_weights, atom_cell, point_codes):
    cube = 2 * REACH + 1
    off_x = point_codes // (cube * cube)
    off_y = point_codes // cube % cube
    off_z = point_codes % cube
    plane = atom_cell[:, 0:1] % SLAB + off_x
    cell_y = (atom_cell[:, 1:2] + off_y - REACH) % SIDE
    cell_z = (atom_cell[:, 2:3] + off_z - REACH) % SIDE
    lateral = cell_y * SIDE + cell_z
    return jnp.concatenate(
        [
            proj_weights.reshape(-1, 256),
            plane.astype(F32),
            lateral.astype(F32),
            jnp.zeros((4, 256), F32),
            potential.reshape(SLAB, LAT),
        ],
        axis=0,
    )


def on_device(trial_waves, potential, proj_weights, kb_energy, atom_cell, point_codes):
    nd = lax.axis_size("dom")
    bands = trial_waves.shape[-1]
    direct = nd == 8
    real = bands // nd
    nb = max(real, 8)
    total = nd * SLAB * LAT
    dom = lax.axis_index("dom") if direct else jnp.int32(0)
    band = lax.axis_index("band")
    pos = jnp.stack([dom, band if direct else jnp.int32(0), band // 2]).astype(jnp.int32)
    pos_band = jnp.stack([dom, band, band // 2]).astype(jnp.int32)
    R = SLAB * nb

    waves = trial_waves.reshape(SLAB, LAT, bands)
    if direct:
        cut = call(
            functools.partial(split_kernel, nd, nb),
            [shape(R + 32, LAT)] * nd,
            [pos, atom_cell, waves, potential, proj_weights, point_codes],
            [pltpu.VMEM((SLAB, bands, LAT), F32), pltpu.VMEM((32, 256), F32)],
            "split",
        )
    else:
        packed = packed_atoms(potential, proj_weights, atom_cell, point_codes)
        gathered = lax.all_gather(packed, "dom", axis=0)
        turned = waves.transpose(0, 2, 1).reshape(SLAB, nd, real, LAT).transpose(1, 0, 2, 3)
        cut = [turned[j] for j in range(nd)]

    lh, ll = split_const(lateral_matrix())
    fold = jnp.asarray(fold_matrix()).astype(BF16)
    kb_row = jnp.concatenate([kb_energy, kb_energy, jnp.zeros((112,), F32)])[None]
    pieces = swap_all(cut, direct)
    if not direct:
        pieces = [
            jnp.concatenate([jnp.pad(p, ((0, 0), (0, nb - real), (0, 0))).reshape(R, LAT), gathered[j]])
            for j, p in enumerate(pieces)
        ]
    ready = call(
        functools.partial(filter_kernel, nd, nb, float(total)),
        [shape(R, LAT)] * nd,
        [pos, kb_row, lh, ll, fold] + pieces,
        [
            pltpu.VMEM(((nd * SLAB + 2 * HALO) * nb, LAT), F32),
            pltpu.VMEM(((nd * SLAB + 2 * HALO) * nb, LAT), F32),
            pltpu.VMEM((nd * nb, 256), F32),
            pltpu.VMEM((nd * nb, 256), F32),
            pltpu.VMEM((nd * 256, 256), BF16),
            pltpu.VMEM((nd * 256, 256), BF16),
            pltpu.VMEM((nd * SLAB, LAT), F32),
            pltpu.VMEM((nd, 32, 256), F32),
        ],
        "filter",
    )
    if not direct:
        ready = [p.reshape(SLAB, nb, LAT)[:, :real] for p in ready]
    back = swap_all(ready, direct)
    if direct:
        filtered, correlation = finish_direct(back, pos, nb, bands, float(total))
    else:
        filtered, correlation = finish_plain(jnp.concatenate(back, axis=1), pos_band, band, bands, float(total))
    return filtered.reshape(trial_waves.shape), correlation


def finish_direct(back, pos, nb, bands, total):
    nd, half = len(back), SLAB // 2
    z, first, second = call(
        functools.partial(join_kernel, nd, nb),
        [shape(SLAB, bands, LAT), shape(half // 2, bands, LAT), shape(half // 2, bands, LAT)],
        [pos] + back,
        (),
        "join",
    )
    far_first = xor_permute(first, "band", 2)
    z_core = xor_permute(z, "band", 1)
    far_second = xor_permute(second, "band", 2)
    part = shape(2, bands // 2, bands)
    block = pltpu.VMEM((2, bands, bands), F32)
    own_keep, own_send = call(own_kernel, [part, part], [pos, z, z_core], [block], "own")
    own_1 = own_keep + xor_permute(own_send, "dom", 1)
    far_second, own_1 = lax.optimization_barrier((far_second, own_1))
    own_2 = own_1 + xor_permute(own_1, "dom", 2)
    own = own_2 + xor_permute(own_2, "dom", 4)
    keep, send, back_keep, back_send = call(
        cross_kernel,
        [part] * 4,
        [pos, z, z_core, far_first, far_second, xor_permute(far_first, "band", 1), xor_permute(far_second, "band", 1)],
        [block, block],
        "cross",
        [own_2],
    )
    cross = call(
        sum_kernel,
        part,
        [
            keep,
            xor_permute(send, "dom", 1),
            xor_permute(back_keep, "band", 2),
            both_permute(back_send),
        ],
        (),
        "sum",
        [own],
    )
    cross = cross + xor_permute(cross, "dom", 2)
    rows = call(
        functools.partial(pair_kernel, total),
        shape(4, bands // 2, bands),
        [pos, own, cross, xor_permute(cross, "dom", 4)],
        (),
        "pair",
    )
    filtered = call(output_kernel, shape(SLAB, LAT, bands), [z], (), "output")
    correlation = call(place_kernel, shape(bands, 4 * bands), [pos, rows, xor_permute(rows, "dom", 1)], (), "place")
    return filtered, correlation


def finish_plain(z, pos, band, bands, total):
    send = lax.dynamic_slice_in_dim(z, (1 - band // 2) * (SLAB // 2), SLAB // 2, 0)
    far = xor_permute(send, "band", 2)
    gram, gram_far = call(
        gram_kernel,
        [shape(4, bands, bands), shape(2, bands, bands)],
        [pos, z, xor_permute(z, "band", 1), far, xor_permute(far, "band", 1)],
        (),
        "gram",
    )
    filtered = call(output_kernel, shape(SLAB, LAT, bands), [z], (), "output")
    start = (1 - band // 2) * 2
    cross = lax.dynamic_slice_in_dim(gram, start, 2, 0) + xor_permute(gram_far, "band", 2)
    gram = lax.dynamic_update_slice_in_dim(gram, cross, start, 0)
    wide = gram.transpose(1, 0, 2).reshape(bands, 4 * bands)
    return filtered, lax.psum(wide, "dom") / total


def solution(mesh):
    return jax.shard_map(
        on_device,
        mesh=mesh,
        in_specs=(
            P("dom", None, None, "band"),
            P("dom", None, None),
            P("dom", None, None),
            P(),
            P("dom", None),
            P("dom", None),
        ),
        out_specs=(P("dom", None, None, "band"), P("band", None)),
        check_vma=False,
    )
```

```python
import functools

import jax
import jax.numpy as jnp
import numpy as np
from jax import lax
from jax.experimental import pallas as pl
from jax.experimental.pallas import tpu as pltpu
from jax.sharding import PartitionSpec as P

HALO = 6
REACH = 4
SLAB = 8
SIDE = 16
LAT = SIDE * SIDE

COEFFS = (
    -5369.0 / 1800.0,
    12.0 / 7.0,
    -15.0 / 56.0,
    10.0 / 189.0,
    -1.0 / 112.0,
    2.0 / 1925.0,
    -1.0 / 16632.0,
)
FILTER_LOWER = 5.0
FILTER_UPPER = 24.0
SPECTRUM_BOTTOM = 0.0
EPSILON = 1e-06

HALF_WIDTH = (FILTER_UPPER - FILTER_LOWER) / 2.0
CENTRE = (FILTER_UPPER + FILTER_LOWER) / 2.0
SIGMA_1 = HALF_WIDTH / (SPECTRUM_BOTTOM - CENTRE)
SIGMA_2 = 1.0 / (2.0 / SIGMA_1 - SIGMA_1)

VMEM_LIMIT = 48 * 1024 * 1024
BF16 = jnp.bfloat16
F32 = jnp.float32
NN = (((1,), (0,)), ((), ()))
NT = (((1,), (1,)), ((), ()))


def dot(a, b, dims=NN):
    return lax.dot_general(a, b, dims, preferred_element_type=F32)


def halves(x):
    hi = x.astype(BF16)
    return hi, (x - hi.astype(F32)).astype(BF16)


def dot3(ah, al, bh, bl, dims=NN):
    return dot(ah, bh, dims) + dot(al, bh, dims) + dot(ah, bl, dims)


def lateral_matrix():
    line = np.zeros((SIDE, SIDE))
    at = np.arange(SIDE)
    for k in range(1, HALO + 1):
        for sign in (1, -1):
            np.add.at(line, ((at + sign * k) % SIDE, at), -0.5 * COEFFS[k])
    eye = np.eye(SIDE)
    return np.kron(line, eye) + np.kron(eye, line)


def relation():
    return [[-1, 0] if q < REACH else [0, 1] for q in range(SLAB)]


def fold_matrix():
    out = np.zeros((256, 384), np.float32)
    for q, pair in enumerate(relation()):
        for half, rel in enumerate(pair):
            for r in range(16):
                out[q * 32 + half * 16 + r, (rel + 1) * 128 + r] = 1.0
    return out


def split_const(matrix):
    matrix = np.asarray(matrix, np.float32)
    hi = jnp.asarray(matrix, F32).astype(BF16)
    lo = (jnp.asarray(matrix, F32) - hi.astype(F32)).astype(BF16)
    return hi, lo


def split_kernel(nd, nb, pos_ref, cell_ref, x_ref, v_ref, w_ref, code_ref, *refs):
    outs, (scratch, packed) = refs[:-2], refs[-2:]
    i = pos_ref[0]
    cube = 2 * REACH + 1
    code = code_ref[...].astype(F32)
    off_x = jnp.floor((code + 0.5) * (1.0 / (cube * cube)))
    rest = code - off_x * (cube * cube)
    off_y = jnp.floor((rest + 0.5) * (1.0 / cube))
    off_z = rest - off_y * cube
    for a in range(2):
        packed[a * 8 : a * 8 + 8] = w_ref[a]
        cell_x, cell_y, cell_z = (
            lax.rem(cell_ref[a, k], n).astype(F32) for k, n in enumerate((SLAB, SIDE, SIDE))
        )
        y = off_y[a : a + 1] + (cell_y + float(SIDE - REACH))
        z = off_z[a : a + 1] + (cell_z + float(SIDE - REACH))
        y = y - SIDE * jnp.floor(y * (1.0 / SIDE))
        z = z - SIDE * jnp.floor(z * (1.0 / SIDE))
        packed[16 + a : 17 + a] = off_x[a : a + 1] + cell_x
        packed[18 + a : 19 + a] = y * SIDE + z
    packed[20:24] = jnp.zeros((4, LAT), F32)
    packed[24:32] = jnp.concatenate([v_ref[:, y, :] for y in range(SIDE)], axis=1)
    for q in range(SLAB):
        scratch[q] = x_ref[q].T
    for j in range(nd):
        start = (i ^ j) * nb
        for q in range(SLAB):
            outs[j][q * nb : (q + 1) * nb] = scratch[q, pl.ds(pl.multiple_of(start, nb), nb)]
        outs[j][SLAB * nb :] = packed[...]


def build_projectors(nd, scratch, wh_ref, wl_ref, v_ref):
    lat = lax.broadcasted_iota(jnp.int32, (LAT, 256), 0).astype(F32)
    plane = lax.broadcasted_iota(jnp.int32, (16, 1, 1), 0).astype(F32)
    diagonal = -1.5 * COEFFS[0] - CENTRE

    def body(s, carry):
        his, los = [], []
        for a in range(2):
            w = scratch[s, a * 8 : a * 8 + 8]
            px = scratch[s, 16 + a : 17 + a]
            place = scratch[s, 18 + a : 19 + a]
            hot = jnp.where(lat == place, 1.0, 0.0).astype(BF16)
            masked = jnp.where(px[None] == plane, w[None], 0.0).reshape(128, 256)
            mh, ml = halves(masked)
            his.append(dot(mh, hot, NT).reshape(16, 8, LAT))
            los.append(dot(ml, hot, NT).reshape(16, 8, LAT))
        hi = jnp.concatenate(his, axis=1).astype(BF16)
        lo = jnp.concatenate(los, axis=1).astype(BF16)
        for t in range(16):
            p = (s * SLAB - REACH + t + nd * SLAB) % (nd * SLAB) if isinstance(s, int) else lax.rem(
                s * SLAB - REACH + t + nd * SLAB, nd * SLAB
            )
            row = pl.ds(pl.multiple_of(p * 32 + (16 if t < SLAB else 0), 16), 16)
            wh_ref[row] = hi[t]
            wl_ref[row] = lo[t]
        v_ref[pl.ds(pl.multiple_of(s * SLAB, SLAB), SLAB)] = scratch[s, 24:32] + diagonal
        return carry

    if nd <= 8:
        for s in range(nd):
            body(s, 0)
    else:
        lax.fori_loop(0, nd, body, 0)


def arrival_order(nd):
    return [*range(nd // 2, nd), *range(1, nd // 2), 0]


def filter_kernel(nd, nb, total, pos_ref, kb_ref, lh_ref, ll_ref, fold_ref, *refs):
    pieces, outs = refs[:nd], refs[nd : 2 * nd]
    f0_ref, f1_ref, fold_out, spread_out, wh_ref, wl_ref, v_ref, packed = refs[2 * nd :]
    i = pos_ref[0]
    R = SLAB * nb
    rows_q = lax.broadcasted_iota(jnp.int32, (SLAB, nb, 256), 0)
    lanes_q = lax.broadcasted_iota(jnp.int32, (SLAB, nb, 256), 2) // 32
    same = rows_q == lanes_q

    def slab_rows(s, k=0):
        return pl.ds(pl.multiple_of((s * SLAB + HALO + k) * nb, nb), R)

    def wrap(ref):
        ref[0 : HALO * nb] = ref[nd * R : nd * R + HALO * nb]
        ref[HALO * nb + nd * R : 2 * HALO * nb + nd * R] = ref[HALO * nb : 2 * HALO * nb]

    def each(body):
        if nd <= 8:
            for s in range(nd):
                body(s)
        else:
            lax.fori_loop(0, nd, lambda s, c: (body(s), c)[1], 0)

    for piece, j in zip(pieces, arrival_order(nd)):
        f0_ref[slab_rows(i ^ j)] = piece[:R]
        packed[i ^ j] = piece[R:]
    wrap(f0_ref)
    build_projectors(nd, packed, wh_ref, wl_ref, v_ref)

    def apply(ref, finish):
        def project(s):
            fh, fl = halves(ref[slab_rows(s)])
            w = pl.ds(pl.multiple_of(s * 256, 256), 256)
            g = dot3(fh, fl, wh_ref[w], wl_ref[w], NT).reshape(SLAB, nb, 256)
            fold_out[pl.ds(pl.multiple_of(s * nb, nb), nb)] = jnp.sum(jnp.where(same, g, 0.0), axis=0)

        each(project)
        gh, gl = halves(fold_out[...])
        h = dot(gh, fold_ref[...]) + dot(gl, fold_ref[...])
        below, at, above = h[:, :128], h[:, 128:256], h[:, 256:]

        def next_slab(x):
            return jnp.concatenate([x[-nb:], x[:-nb]], axis=0)

        def previous_slab(x):
            return jnp.concatenate([x[nb:], x[:nb]], axis=0)

        p = (at + next_slab(above) + previous_slab(below)) * kb_ref[...]
        wide = jnp.concatenate([next_slab(p), p, previous_slab(p)], axis=1)
        ph, plo = halves(wide)
        spread_out[...] = dot(ph, fold_ref[...], NT) + dot(plo, fold_ref[...], NT)

        def step(s):
            f = ref[slab_rows(s)]
            fh, fl = halves(f)
            x = jnp.where(same, spread_out[pl.ds(pl.multiple_of(s * nb, nb), nb)][None], 0.0).reshape(R, 256)
            xh, xl = halves(x)
            w = pl.ds(pl.multiple_of(s * 256, 256), 256)
            acc = dot3(xh, xl, wh_ref[w], wl_ref[w]) + dot3(fh, fl, lh_ref[...], ll_ref[...])
            v = v_ref[pl.ds(pl.multiple_of(s * SLAB, SLAB), SLAB)]
            acc = acc + (f.reshape(SLAB, nb, LAT) * v[:, None, :]).reshape(R, LAT)
            for k in range(1, HALO + 1):
                acc = acc + (-0.5 * COEFFS[k]) * (ref[slab_rows(s, k)] + ref[slab_rows(s, -k)])
            finish(s, acc)

        each(step)

    def first(s, acc):
        f1_ref[slab_rows(s)] = (SIGMA_1 / HALF_WIDTH) * acc

    apply(f0_ref, first)
    wrap(f1_ref)

    def second(s, acc):
        f0_ref_new = (2.0 * SIGMA_2 / HALF_WIDTH) * acc - (SIGMA_1 * SIGMA_2) * f0_ref[slab_rows(s)]
        y2_store(s, f0_ref_new)

    def y2_store(s, value):
        f0_ref[slab_rows(s)] = value

    apply(f1_ref, second)
    square = jnp.zeros((nb, LAT), F32)
    if nd <= 8:
        for s in range(nd):
            y = f0_ref[slab_rows(s)].reshape(SLAB, nb, LAT)
            square = square + jnp.sum(y * y, axis=0)
    else:

        def add(s, total_square):
            y = f0_ref[slab_rows(s)].reshape(SLAB, nb, LAT)
            return total_square + jnp.sum(y * y, axis=0)

        square = lax.fori_loop(0, nd, add, square)
    scale = 1.0 / jnp.sqrt(jnp.sum(square, axis=1, keepdims=True) / total + EPSILON)
    for j in range(nd):
        y = f0_ref[slab_rows(i ^ j)].reshape(SLAB, nb, LAT)
        outs[j][...] = (y * scale[None]).reshape(R, LAT)


def join_kernel(nd, nb, pos_ref, *refs):
    pieces, (z_ref, first_ref, second_ref) = refs[:nd], refs[nd:]
    i, y = pos_ref[0], pos_ref[2]
    for j in range(nd):
        rows = pl.ds(pl.multiple_of((i ^ j) * nb, nb), nb)
        for q in range(SLAB):
            z_ref[q, rows] = pieces[j][q * nb : (q + 1) * nb]
    half = SLAB // 2
    for q in range(half // 2):
        first_ref[q] = z_ref[(1 - y) * half + q]
        second_ref[q] = z_ref[(1 - y) * half + half // 2 + q]


def own_kernel(pos_ref, z_ref, zc_ref, keep_ref, send_ref, g_ref):
    i, b = pos_ref[0], pos_ref[1]
    own = core = None
    for q in range(SLAB):
        zh, zl = halves(z_ref[q])
        ch, cl = halves(zc_ref[q])
        mine, other = dot3(zh, zl, zh, zl, NT), dot3(zh, zl, ch, cl, NT)
        own, core = (mine, other) if own is None else (own + mine, core + other)
    g_ref[b & 1] = own
    g_ref[(b & 1) ^ 1] = core
    cut_rows(i, g_ref, keep_ref, send_ref)


def cut_rows(i, g_ref, keep_ref, send_ref):
    x = i & 1
    for c in range(2):
        keep_ref[c] = g_ref[c, pl.ds(pl.multiple_of(x * 64, 64), 64)]
        send_ref[c] = g_ref[c, pl.ds(pl.multiple_of((1 - x) * 64, 64), 64)]


def cross_kernel(
    pos_ref, z_ref, zc_ref, first, second, core_first, core_second, tie, keep, send, back, back_send, g_ref, back_ref
):
    i, b, y = pos_ref[0], pos_ref[1], pos_ref[2]
    half = SLAB // 2
    totals = None
    for q in range(half):
        zh, zl = halves(z_ref[y * half + q])
        ch, cl = halves(zc_ref[y * half + q])
        fh, fl = halves((first, second)[q // (half // 2)][q % (half // 2)])
        gh, gl = halves((core_first, core_second)[q // (half // 2)][q % (half // 2)])
        now = (
            dot3(zh, zl, fh, fl, NT),
            dot3(zh, zl, gh, gl, NT),
            dot3(fh, fl, zh, zl, NT),
            dot3(fh, fl, ch, cl, NT),
        )
        totals = now if totals is None else tuple(t + n for t, n in zip(totals, now))
    c = b & 1
    g_ref[c], g_ref[c ^ 1], back_ref[c], back_ref[c ^ 1] = totals
    cut_rows(i, g_ref, keep, send)
    cut_rows(i, back_ref, back, back_send)


def sum_kernel(a_ref, b_ref, c_ref, d_ref, tie, out_ref):
    out_ref[...] = (a_ref[...] + b_ref[...]) + (c_ref[...] + d_ref[...])


def pair_kernel(total, pos_ref, own, cross, cross_other, out_ref):
    y = pos_ref[2]
    for c in range(2):
        out_ref[y * 2 + c] = own[c] * (1.0 / total)
        out_ref[(1 - y) * 2 + c] = (cross[c] + cross_other[c]) * (1.0 / total)


def output_kernel(z_ref, out_ref):
    for q in range(SLAB):
        out_ref[q] = z_ref[q].T


def place_kernel(pos_ref, mine, other, out_ref):
    x = pos_ref[0] & 1
    for k in range(4):
        lanes = slice(k * 128, (k + 1) * 128)
        out_ref[pl.ds(pl.multiple_of(x * 64, 64), 64), lanes] = mine[k]
        out_ref[pl.ds(pl.multiple_of((1 - x) * 64, 64), 64), lanes] = other[k]


def gram_kernel(pos_ref, own, core, far, far_core, g_ref, far_ref):
    b, y = pos_ref[1], pos_ref[2]
    half = SLAB // 2

    def add(totals, place, value):
        totals[place] = value if totals.get(place) is None else totals[place] + value

    totals = {}
    for q in range(half):
        for mine in (True, False):
            at = q + y * half if mine else q + (1 - y) * half
            zh, zl = halves(own[at])
            ch, cl = halves(core[at])
            add(totals, "own", dot3(zh, zl, zh, zl, NT))
            add(totals, "core", dot3(zh, zl, ch, cl, NT))
            if mine:
                fh, fl = halves(far[q])
                gh, gl = halves(far_core[q])
                add(totals, "far", dot3(zh, zl, fh, fl, NT))
                add(totals, "far_core", dot3(zh, zl, gh, gl, NT))
                add(totals, "back", dot3(fh, fl, zh, zl, NT))
                add(totals, "back_core", dot3(fh, fl, ch, cl, NT))
    g_ref[b] = totals["own"]
    g_ref[b ^ 1] = totals["core"]
    g_ref[b ^ 2] = totals["far"]
    g_ref[b ^ 3] = totals["far_core"]
    far_ref[b & 1] = totals["back"]
    far_ref[(b & 1) ^ 1] = totals["back_core"]


def call(kernel, out_shape, operands, scratch=(), name=None, ties=()):
    specs = [
        pl.BlockSpec(memory_space=pltpu.SMEM if o.dtype == jnp.int32 and o.size < 128 else pltpu.VMEM) for o in operands
    ] + [pl.BlockSpec(memory_space=pl.ANY) for _ in ties]
    single = not isinstance(out_shape, (list, tuple))
    return pl.pallas_call(
        kernel,
        out_shape=out_shape,
        in_specs=specs,
        out_specs=(
            pl.BlockSpec(memory_space=pltpu.VMEM)
            if single
            else [pl.BlockSpec(memory_space=pltpu.VMEM) for _ in out_shape]
        ),
        scratch_shapes=list(scratch),
        compiler_params=pltpu.CompilerParams(vmem_limit_bytes=VMEM_LIMIT),
        name=name,
    )(*operands, *ties)


def shape(*dims, dtype=F32):
    return jax.ShapeDtypeStruct(dims, dtype)


def xor_permute(value, axis, step):
    count = lax.axis_size(axis)
    return lax.ppermute(value, axis, [(k, k ^ step) for k in range(count)])


def both_permute(value):
    nd, ng = lax.axis_size("dom"), lax.axis_size("band")
    pairs = [(b * nd + d, (b ^ 2) * nd + (d ^ 1)) for b in range(ng) for d in range(nd)]
    return lax.ppermute(value, ("band", "dom"), pairs)


def swap_all(pieces, direct):
    if direct:
        got = {0: pieces[0]}
        for j in range(1, len(pieces)):
            got[j] = xor_permute(pieces[j], "dom", j)
        return [got[j] for j in range(len(pieces))]
    stacked = lax.all_to_all(jnp.stack(pieces), "dom", 0, 0, tiled=True)
    return [stacked[j] for j in range(len(pieces))]


def packed_atoms(potential, proj_weights, atom_cell, point_codes):
    cube = 2 * REACH + 1
    off_x = point_codes // (cube * cube)
    off_y = point_codes // cube % cube
    off_z = point_codes % cube
    plane = atom_cell[:, 0:1] % SLAB + off_x
    cell_y = (atom_cell[:, 1:2] + off_y - REACH) % SIDE
    cell_z = (atom_cell[:, 2:3] + off_z - REACH) % SIDE
    lateral = cell_y * SIDE + cell_z
    return jnp.concatenate(
        [
            proj_weights.reshape(-1, 256),
            plane.astype(F32),
            lateral.astype(F32),
            jnp.zeros((4, 256), F32),
            potential.reshape(SLAB, LAT),
        ],
        axis=0,
    )


def on_device(trial_waves, potential, proj_weights, kb_energy, atom_cell, point_codes):
    nd = lax.axis_size("dom")
    bands = trial_waves.shape[-1]
    direct = nd == 8
    real = bands // nd
    nb = max(real, 8)
    total = nd * SLAB * LAT
    dom = lax.axis_index("dom") if direct else jnp.int32(0)
    band = lax.axis_index("band")
    pos = jnp.stack([dom, band if direct else jnp.int32(0), band // 2]).astype(jnp.int32)
    pos_band = jnp.stack([dom, band, band // 2]).astype(jnp.int32)
    R = SLAB * nb

    waves = trial_waves.reshape(SLAB, LAT, bands)
    if direct:
        cut = call(
            functools.partial(split_kernel, nd, nb),
            [shape(R + 32, LAT)] * nd,
            [pos, atom_cell, waves, potential, proj_weights, point_codes],
            [pltpu.VMEM((SLAB, bands, LAT), F32), pltpu.VMEM((32, 256), F32)],
            "split",
        )
    else:
        packed = packed_atoms(potential, proj_weights, atom_cell, point_codes)
        gathered = lax.all_gather(packed, "dom", axis=0)
        turned = waves.transpose(0, 2, 1).reshape(SLAB, nd, real, LAT).transpose(1, 0, 2, 3)
        cut = [turned[j] for j in range(nd)]

    lh, ll = split_const(lateral_matrix())
    fold = jnp.asarray(fold_matrix()).astype(BF16)
    kb_row = jnp.concatenate([kb_energy, kb_energy, jnp.zeros((112,), F32)])[None]
    pieces = swap_all(cut, direct)
    if not direct:
        pieces = [
            jnp.concatenate([jnp.pad(p, ((0, 0), (0, nb - real), (0, 0))).reshape(R, LAT), gathered[j]])
            for j, p in enumerate(pieces)
        ]
    ready = call(
        functools.partial(filter_kernel, nd, nb, float(total)),
        [shape(R, LAT)] * nd,
        [pos, kb_row, lh, ll, fold] + [pieces[j] for j in arrival_order(nd)],
        [
            pltpu.VMEM(((nd * SLAB + 2 * HALO) * nb, LAT), F32),
            pltpu.VMEM(((nd * SLAB + 2 * HALO) * nb, LAT), F32),
            pltpu.VMEM((nd * nb, 256), F32),
            pltpu.VMEM((nd * nb, 256), F32),
            pltpu.VMEM((nd * 256, 256), BF16),
            pltpu.VMEM((nd * 256, 256), BF16),
            pltpu.VMEM((nd * SLAB, LAT), F32),
            pltpu.VMEM((nd, 32, 256), F32),
        ],
        "filter",
    )
    if not direct:
        ready = [p.reshape(SLAB, nb, LAT)[:, :real] for p in ready]
    back = swap_all(ready, direct)
    if direct:
        filtered, correlation = finish_direct(back, pos, nb, bands, float(total))
    else:
        filtered, correlation = finish_plain(jnp.concatenate(back, axis=1), pos_band, band, bands, float(total))
    return filtered.reshape(trial_waves.shape), correlation


def finish_direct(back, pos, nb, bands, total):
    nd, half = len(back), SLAB // 2
    z, first, second = call(
        functools.partial(join_kernel, nd, nb),
        [shape(SLAB, bands, LAT), shape(half // 2, bands, LAT), shape(half // 2, bands, LAT)],
        [pos] + back,
        (),
        "join",
    )
    far_first = xor_permute(first, "band", 2)
    z_core = xor_permute(z, "band", 1)
    far_second = xor_permute(second, "band", 2)
    part = shape(2, bands // 2, bands)
    block = pltpu.VMEM((2, bands, bands), F32)
    own_keep, own_send = call(own_kernel, [part, part], [pos, z, z_core], [block], "own")
    own_1 = own_keep + xor_permute(own_send, "dom", 1)
    far_second, own_1 = lax.optimization_barrier((far_second, own_1))
    own_2 = own_1 + xor_permute(own_1, "dom", 2)
    own = own_2 + xor_permute(own_2, "dom", 4)
    keep, send, back_keep, back_send = call(
        cross_kernel,
        [part] * 4,
        [pos, z, z_core, far_first, far_second, xor_permute(far_first, "band", 1), xor_permute(far_second, "band", 1)],
        [block, block],
        "cross",
        [own_2],
    )
    cross = call(
        sum_kernel,
        part,
        [
            keep,
            xor_permute(send, "dom", 1),
            xor_permute(back_keep, "band", 2),
            both_permute(back_send),
        ],
        (),
        "sum",
        [own],
    )
    cross = cross + xor_permute(cross, "dom", 2)
    rows = call(
        functools.partial(pair_kernel, total),
        shape(4, bands // 2, bands),
        [pos, own, cross, xor_permute(cross, "dom", 4)],
        (),
        "pair",
    )
    filtered = call(output_kernel, shape(SLAB, LAT, bands), [z], (), "output")
    correlation = call(place_kernel, shape(bands, 4 * bands), [pos, rows, xor_permute(rows, "dom", 1)], (), "place")
    return filtered, correlation


def finish_plain(z, pos, band, bands, total):
    send = lax.dynamic_slice_in_dim(z, (1 - band // 2) * (SLAB // 2), SLAB // 2, 0)
    far = xor_permute(send, "band", 2)
    gram, gram_far = call(
        gram_kernel,
        [shape(4, bands, bands), shape(2, bands, bands)],
        [pos, z, xor_permute(z, "band", 1), far, xor_permute(far, "band", 1)],
        (),
        "gram",
    )
    filtered = call(output_kernel, shape(SLAB, LAT, bands), [z], (), "output")
    start = (1 - band // 2) * 2
    cross = lax.dynamic_slice_in_dim(gram, start, 2, 0) + xor_permute(gram_far, "band", 2)
    gram = lax.dynamic_update_slice_in_dim(gram, cross, start, 0)
    wide = gram.transpose(1, 0, 2).reshape(bands, 4 * bands)
    return filtered, lax.psum(wide, "dom") / total


def solution(mesh):
    return jax.shard_map(
        on_device,
        mesh=mesh,
        in_specs=(
            P("dom", None, None, "band"),
            P("dom", None, None),
            P("dom", None, None),
            P(),
            P("dom", None),
            P("dom", None),
        ),
        out_specs=(P("dom", None, None, "band"), P("band", None)),
        check_vma=False,
    )
```

```python
import functools

import jax
import jax.numpy as jnp
import numpy as np
from jax import lax
from jax.experimental import pallas as pl
from jax.experimental.pallas import tpu as pltpu
from jax.sharding import PartitionSpec as P

HALO = 6
REACH = 4
SLAB = 8
CHUNKS = 2
SIDE = 16
LAT = SIDE * SIDE

COEFFS = (
    -5369.0 / 1800.0,
    12.0 / 7.0,
    -15.0 / 56.0,
    10.0 / 189.0,
    -1.0 / 112.0,
    2.0 / 1925.0,
    -1.0 / 16632.0,
)
FILTER_LOWER = 5.0
FILTER_UPPER = 24.0
SPECTRUM_BOTTOM = 0.0
EPSILON = 1e-06

HALF_WIDTH = (FILTER_UPPER - FILTER_LOWER) / 2.0
CENTRE = (FILTER_UPPER + FILTER_LOWER) / 2.0
SIGMA_1 = HALF_WIDTH / (SPECTRUM_BOTTOM - CENTRE)
SIGMA_2 = 1.0 / (2.0 / SIGMA_1 - SIGMA_1)

VMEM_LIMIT = 48 * 1024 * 1024
BF16 = jnp.bfloat16
F32 = jnp.float32
NN = (((1,), (0,)), ((), ()))
NT = (((1,), (1,)), ((), ()))


def dot(a, b, dims=NN):
    return lax.dot_general(a, b, dims, preferred_element_type=F32)


def halves(x):
    hi = x.astype(BF16)
    return hi, (x - hi.astype(F32)).astype(BF16)


def dot3(ah, al, bh, bl, dims=NN):
    return dot(ah, bh, dims) + dot(al, bh, dims) + dot(ah, bl, dims)


def lateral_matrix():
    line = np.zeros((SIDE, SIDE))
    at = np.arange(SIDE)
    for k in range(1, HALO + 1):
        for sign in (1, -1):
            np.add.at(line, ((at + sign * k) % SIDE, at), -0.5 * COEFFS[k])
    eye = np.eye(SIDE)
    return np.kron(line, eye) + np.kron(eye, line)


def relation():
    return [[-1, 0] if q < REACH else [0, 1] for q in range(SLAB)]


def fold_matrix():
    out = np.zeros((256, 384), np.float32)
    for q, pair in enumerate(relation()):
        for half, rel in enumerate(pair):
            for r in range(16):
                out[q * 32 + half * 16 + r, (rel + 1) * 128 + r] = 1.0
    return out


def split_const(matrix):
    matrix = np.asarray(matrix, np.float32)
    hi = jnp.asarray(matrix, F32).astype(BF16)
    lo = (jnp.asarray(matrix, F32) - hi.astype(F32)).astype(BF16)
    return hi, lo


def split_kernel(nd, nb, chunks, pos_ref, cell_ref, x_ref, v_ref, w_ref, code_ref, *refs):
    outs, (scratch, packed) = refs[:-2], refs[-2:]
    i = pos_ref[0]
    cube = 2 * REACH + 1
    code = code_ref[...].astype(F32)
    off_x = jnp.floor((code + 0.5) * (1.0 / (cube * cube)))
    rest = code - off_x * (cube * cube)
    off_y = jnp.floor((rest + 0.5) * (1.0 / cube))
    off_z = rest - off_y * cube
    for a in range(2):
        packed[a * 8 : a * 8 + 8] = w_ref[a]
        cell_x, cell_y, cell_z = (
            lax.rem(cell_ref[a, k], n).astype(F32) for k, n in enumerate((SLAB, SIDE, SIDE))
        )
        y = off_y[a : a + 1] + (cell_y + float(SIDE - REACH))
        z = off_z[a : a + 1] + (cell_z + float(SIDE - REACH))
        y = y - SIDE * jnp.floor(y * (1.0 / SIDE))
        z = z - SIDE * jnp.floor(z * (1.0 / SIDE))
        packed[16 + a : 17 + a] = off_x[a : a + 1] + cell_x
        packed[18 + a : 19 + a] = y * SIDE + z
    packed[20:24] = jnp.zeros((4, LAT), F32)
    packed[24:32] = jnp.concatenate([v_ref[:, y, :] for y in range(SIDE)], axis=1)
    for q in range(SLAB):
        scratch[q] = x_ref[q].T
    for c in range(chunks):
        for j in range(nd):
            start = c * (nd * nb) + (i ^ j) * nb
            out = outs[c * nd + j]
            for q in range(SLAB):
                out[q * nb : (q + 1) * nb] = scratch[q, pl.ds(pl.multiple_of(start, nb), nb)]
            if c == 0:
                out[SLAB * nb :] = packed[...]


def weights_kernel(nd, R, pos_ref, *refs):
    pieces, (wh_ref, wl_ref, v_ref, scratch) = refs[:nd], refs[nd:]
    i = pos_ref[0]
    for piece, j in zip(pieces, arrival_order(nd)):
        scratch[i ^ j] = piece[R:]
    lat = lax.broadcasted_iota(jnp.int32, (LAT, 256), 0).astype(F32)
    plane = lax.broadcasted_iota(jnp.int32, (16, 1, 1), 0).astype(F32)
    diagonal = -1.5 * COEFFS[0] - CENTRE

    def body(s, carry):
        his, los = [], []
        for a in range(2):
            w = scratch[s, a * 8 : a * 8 + 8]
            px = scratch[s, 16 + a : 17 + a]
            place = scratch[s, 18 + a : 19 + a]
            hot = jnp.where(lat == place, 1.0, 0.0).astype(BF16)
            masked = jnp.where(px[None] == plane, w[None], 0.0).reshape(128, 256)
            mh, ml = halves(masked)
            his.append(dot(mh, hot, NT).reshape(16, 8, LAT))
            los.append(dot(ml, hot, NT).reshape(16, 8, LAT))
        hi = jnp.concatenate(his, axis=1).astype(BF16)
        lo = jnp.concatenate(los, axis=1).astype(BF16)
        for t in range(16):
            p = (s * SLAB - REACH + t + nd * SLAB) % (nd * SLAB) if isinstance(s, int) else lax.rem(
                s * SLAB - REACH + t + nd * SLAB, nd * SLAB
            )
            row = pl.ds(pl.multiple_of(p * 32 + (16 if t < SLAB else 0), 16), 16)
            wh_ref[row] = hi[t]
            wl_ref[row] = lo[t]
        v_ref[pl.ds(pl.multiple_of(s * SLAB, SLAB), SLAB)] = scratch[s, 24:32] + diagonal
        return carry

    if nd <= 8:
        for s in range(nd):
            body(s, 0)
    else:
        lax.fori_loop(0, nd, body, 0)


def arrival_order(nd):
    return [*range(nd // 2, nd), *range(1, nd // 2), 0]


def filter_kernel(nd, nb, total, pos_ref, kb_ref, lh_ref, ll_ref, fold_ref, wh_ref, wl_ref, v_ref, *refs):
    pieces, outs = refs[:nd], refs[nd : 2 * nd]
    f0_ref, f1_ref, fold_out, spread_out = refs[2 * nd :]
    i = pos_ref[0]
    R = SLAB * nb
    rows_q = lax.broadcasted_iota(jnp.int32, (SLAB, nb, 256), 0)
    lanes_q = lax.broadcasted_iota(jnp.int32, (SLAB, nb, 256), 2) // 32
    same = rows_q == lanes_q

    def slab_rows(s, k=0):
        return pl.ds(pl.multiple_of((s * SLAB + HALO + k) * nb, nb), R)

    def wrap(ref):
        ref[0 : HALO * nb] = ref[nd * R : nd * R + HALO * nb]
        ref[HALO * nb + nd * R : 2 * HALO * nb + nd * R] = ref[HALO * nb : 2 * HALO * nb]

    def each(body):
        if nd <= 8:
            for s in range(nd):
                body(s)
        else:
            lax.fori_loop(0, nd, lambda s, c: (body(s), c)[1], 0)

    for piece, j in zip(pieces, arrival_order(nd)):
        f0_ref[slab_rows(i ^ j)] = piece[:R]
    wrap(f0_ref)

    def apply(ref, finish):
        def project(s):
            fh, fl = halves(ref[slab_rows(s)])
            w = pl.ds(pl.multiple_of(s * 256, 256), 256)
            g = dot3(fh, fl, wh_ref[w], wl_ref[w], NT).reshape(SLAB, nb, 256)
            fold_out[pl.ds(pl.multiple_of(s * nb, nb), nb)] = jnp.sum(jnp.where(same, g, 0.0), axis=0)

        each(project)
        gh, gl = halves(fold_out[...])
        h = dot(gh, fold_ref[...]) + dot(gl, fold_ref[...])
        below, at, above = h[:, :128], h[:, 128:256], h[:, 256:]

        def next_slab(x):
            return jnp.concatenate([x[-nb:], x[:-nb]], axis=0)

        def previous_slab(x):
            return jnp.concatenate([x[nb:], x[:nb]], axis=0)

        p = (at + next_slab(above) + previous_slab(below)) * kb_ref[...]
        wide = jnp.concatenate([next_slab(p), p, previous_slab(p)], axis=1)
        ph, plo = halves(wide)
        spread_out[...] = dot(ph, fold_ref[...], NT) + dot(plo, fold_ref[...], NT)

        def step(s):
            f = ref[slab_rows(s)]
            fh, fl = halves(f)
            x = jnp.where(same, spread_out[pl.ds(pl.multiple_of(s * nb, nb), nb)][None], 0.0).reshape(R, 256)
            xh, xl = halves(x)
            w = pl.ds(pl.multiple_of(s * 256, 256), 256)
            acc = dot3(xh, xl, wh_ref[w], wl_ref[w]) + dot3(fh, fl, lh_ref[...], ll_ref[...])
            v = v_ref[pl.ds(pl.multiple_of(s * SLAB, SLAB), SLAB)]
            acc = acc + (f.reshape(SLAB, nb, LAT) * v[:, None, :]).reshape(R, LAT)
            for k in range(1, HALO + 1):
                acc = acc + (-0.5 * COEFFS[k]) * (ref[slab_rows(s, k)] + ref[slab_rows(s, -k)])
            finish(s, acc)

        each(step)

    def first(s, acc):
        f1_ref[slab_rows(s)] = (SIGMA_1 / HALF_WIDTH) * acc

    apply(f0_ref, first)
    wrap(f1_ref)

    def second(s, acc):
        f0_ref_new = (2.0 * SIGMA_2 / HALF_WIDTH) * acc - (SIGMA_1 * SIGMA_2) * f0_ref[slab_rows(s)]
        y2_store(s, f0_ref_new)

    def y2_store(s, value):
        f0_ref[slab_rows(s)] = value

    apply(f1_ref, second)
    square = jnp.zeros((nb, LAT), F32)
    if nd <= 8:
        for s in range(nd):
            y = f0_ref[slab_rows(s)].reshape(SLAB, nb, LAT)
            square = square + jnp.sum(y * y, axis=0)
    else:

        def add(s, total_square):
            y = f0_ref[slab_rows(s)].reshape(SLAB, nb, LAT)
            return total_square + jnp.sum(y * y, axis=0)

        square = lax.fori_loop(0, nd, add, square)
    scale = 1.0 / jnp.sqrt(jnp.sum(square, axis=1, keepdims=True) / total + EPSILON)
    for j in range(nd):
        y = f0_ref[slab_rows(i ^ j)].reshape(SLAB, nb, LAT)
        outs[j][...] = (y * scale[None]).reshape(R, LAT)


def join_kernel(nd, nb, pos_ref, *refs):
    pieces, (z_ref, send_ref) = refs[:nd], refs[-2:]
    i, y = pos_ref[0], pos_ref[2]
    for j in range(nd):
        rows = pl.ds(pl.multiple_of((i ^ j) * nb, nb), nb)
        for q in range(SLAB):
            z_ref[q, rows] = pieces[j][q * nb : (q + 1) * nb]
    half = SLAB // 2
    for q in range(half):
        send_ref[q] = z_ref[(1 - y) * half + q]


def bands_of(group, q):
    return halves(jnp.concatenate([r[q] for r in group], axis=0))


def own_kernel(chunks, pos_ref, *refs):
    zs, cs, (keep_ref, send_ref, g_ref) = refs[:chunks], refs[chunks : 2 * chunks], refs[2 * chunks :]
    i, b = pos_ref[0], pos_ref[1]
    own = core = None
    for q in range(SLAB):
        zh, zl = bands_of(zs, q)
        ch, cl = bands_of(cs, q)
        mine, other = dot3(zh, zl, zh, zl, NT), dot3(zh, zl, ch, cl, NT)
        own, core = (mine, other) if own is None else (own + mine, core + other)
    g_ref[b & 1] = own
    g_ref[(b & 1) ^ 1] = core
    cut_rows(i, g_ref, keep_ref, send_ref)


def cut_rows(i, g_ref, keep_ref, send_ref):
    x = i & 1
    for c in range(2):
        keep_ref[c] = g_ref[c, pl.ds(pl.multiple_of(x * 64, 64), 64)]
        send_ref[c] = g_ref[c, pl.ds(pl.multiple_of((1 - x) * 64, 64), 64)]


def cross_kernel(chunks, pos_ref, *refs):
    zs, cs, fs, gs = (refs[k * chunks : (k + 1) * chunks] for k in range(4))
    tie, keep, send, back, back_send, g_ref, back_ref = refs[4 * chunks :]
    i, b, y = pos_ref[0], pos_ref[1], pos_ref[2]
    half = SLAB // 2
    totals = None
    for q in range(half):
        zh, zl = bands_of(zs, y * half + q)
        ch, cl = bands_of(cs, y * half + q)
        fh, fl = bands_of(fs, q)
        gh, gl = bands_of(gs, q)
        now = (
            dot3(zh, zl, fh, fl, NT),
            dot3(zh, zl, gh, gl, NT),
            dot3(fh, fl, zh, zl, NT),
            dot3(fh, fl, ch, cl, NT),
        )
        totals = now if totals is None else tuple(t + n for t, n in zip(totals, now))
    c = b & 1
    g_ref[c], g_ref[c ^ 1], back_ref[c], back_ref[c ^ 1] = totals
    cut_rows(i, g_ref, keep, send)
    cut_rows(i, back_ref, back, back_send)


def sum_kernel(a_ref, b_ref, c_ref, d_ref, tie, out_ref):
    out_ref[...] = (a_ref[...] + b_ref[...]) + (c_ref[...] + d_ref[...])


def pair_kernel(total, pos_ref, own, cross, cross_other, out_ref):
    y = pos_ref[2]
    for c in range(2):
        out_ref[y * 2 + c] = own[c] * (1.0 / total)
        out_ref[(1 - y) * 2 + c] = (cross[c] + cross_other[c]) * (1.0 / total)


def output_kernel(*refs):
    for q in range(SLAB):
        refs[-1][q] = jnp.concatenate([z[q] for z in refs[:-1]], axis=0).T


def place_kernel(pos_ref, mine, other, out_ref):
    x = pos_ref[0] & 1
    for k in range(4):
        lanes = slice(k * 128, (k + 1) * 128)
        out_ref[pl.ds(pl.multiple_of(x * 64, 64), 64), lanes] = mine[k]
        out_ref[pl.ds(pl.multiple_of((1 - x) * 64, 64), 64), lanes] = other[k]


def gram_kernel(pos_ref, own, core, far, far_core, g_ref, far_ref):
    b, y = pos_ref[1], pos_ref[2]
    half = SLAB // 2

    def add(totals, place, value):
        totals[place] = value if totals.get(place) is None else totals[place] + value

    totals = {}
    for q in range(half):
        for mine in (True, False):
            at = q + y * half if mine else q + (1 - y) * half
            zh, zl = halves(own[at])
            ch, cl = halves(core[at])
            add(totals, "own", dot3(zh, zl, zh, zl, NT))
            add(totals, "core", dot3(zh, zl, ch, cl, NT))
            if mine:
                fh, fl = halves(far[q])
                gh, gl = halves(far_core[q])
                add(totals, "far", dot3(zh, zl, fh, fl, NT))
                add(totals, "far_core", dot3(zh, zl, gh, gl, NT))
                add(totals, "back", dot3(fh, fl, zh, zl, NT))
                add(totals, "back_core", dot3(fh, fl, ch, cl, NT))
    g_ref[b] = totals["own"]
    g_ref[b ^ 1] = totals["core"]
    g_ref[b ^ 2] = totals["far"]
    g_ref[b ^ 3] = totals["far_core"]
    far_ref[b & 1] = totals["back"]
    far_ref[(b & 1) ^ 1] = totals["back_core"]


def call(kernel, out_shape, operands, scratch=(), name=None, ties=()):
    specs = [
        pl.BlockSpec(memory_space=pltpu.SMEM if o.dtype == jnp.int32 and o.size < 128 else pltpu.VMEM) for o in operands
    ] + [pl.BlockSpec(memory_space=pl.ANY) for _ in ties]
    single = not isinstance(out_shape, (list, tuple))
    return pl.pallas_call(
        kernel,
        out_shape=out_shape,
        in_specs=specs,
        out_specs=(
            pl.BlockSpec(memory_space=pltpu.VMEM)
            if single
            else [pl.BlockSpec(memory_space=pltpu.VMEM) for _ in out_shape]
        ),
        scratch_shapes=list(scratch),
        compiler_params=pltpu.CompilerParams(vmem_limit_bytes=VMEM_LIMIT),
        name=name,
    )(*operands, *ties)


def shape(*dims, dtype=F32):
    return jax.ShapeDtypeStruct(dims, dtype)


def xor_permute(value, axis, step):
    count = lax.axis_size(axis)
    return lax.ppermute(value, axis, [(k, k ^ step) for k in range(count)])


def both_permute(value):
    nd, ng = lax.axis_size("dom"), lax.axis_size("band")
    pairs = [(b * nd + d, (b ^ 2) * nd + (d ^ 1)) for b in range(ng) for d in range(nd)]
    return lax.ppermute(value, ("band", "dom"), pairs)


def swap_all(pieces, direct):
    if direct:
        got = {0: pieces[0]}
        for j in range(1, len(pieces)):
            got[j] = xor_permute(pieces[j], "dom", j)
        return [got[j] for j in range(len(pieces))]
    stacked = lax.all_to_all(jnp.stack(pieces), "dom", 0, 0, tiled=True)
    return [stacked[j] for j in range(len(pieces))]


def packed_atoms(potential, proj_weights, atom_cell, point_codes):
    cube = 2 * REACH + 1
    off_x = point_codes // (cube * cube)
    off_y = point_codes // cube % cube
    off_z = point_codes % cube
    plane = atom_cell[:, 0:1] % SLAB + off_x
    cell_y = (atom_cell[:, 1:2] + off_y - REACH) % SIDE
    cell_z = (atom_cell[:, 2:3] + off_z - REACH) % SIDE
    lateral = cell_y * SIDE + cell_z
    return jnp.concatenate(
        [
            proj_weights.reshape(-1, 256),
            plane.astype(F32),
            lateral.astype(F32),
            jnp.zeros((4, 256), F32),
            potential.reshape(SLAB, LAT),
        ],
        axis=0,
    )


def on_device(trial_waves, potential, proj_weights, kb_energy, atom_cell, point_codes):
    nd = lax.axis_size("dom")
    bands = trial_waves.shape[-1]
    direct = nd == 8
    chunks = CHUNKS if direct else 1
    real = bands // (nd * chunks)
    nb = max(real, 8)
    total = nd * SLAB * LAT
    dom = lax.axis_index("dom") if direct else jnp.int32(0)
    band = lax.axis_index("band")
    pos = jnp.stack([dom, band if direct else jnp.int32(0), band // 2]).astype(jnp.int32)
    pos_band = jnp.stack([dom, band, band // 2]).astype(jnp.int32)
    R = SLAB * nb

    waves = trial_waves.reshape(SLAB, LAT, bands)
    if direct:
        cut = call(
            functools.partial(split_kernel, nd, nb, chunks),
            [shape(R + (0 if c else 32), LAT) for c in range(chunks) for j in range(nd)],
            [pos, atom_cell, waves, potential, proj_weights, point_codes],
            [pltpu.VMEM((SLAB, bands, LAT), F32), pltpu.VMEM((32, 256), F32)],
            "split",
        )
    else:
        packed = packed_atoms(potential, proj_weights, atom_cell, point_codes)
        gathered = lax.all_gather(packed, "dom", axis=0)
        turned = waves.transpose(0, 2, 1).reshape(SLAB, nd, real, LAT).transpose(1, 0, 2, 3)
        cut = [turned[j] for j in range(nd)]

    lh, ll = split_const(lateral_matrix())
    fold = jnp.asarray(fold_matrix()).astype(BF16)
    kb_row = jnp.concatenate([kb_energy, kb_energy, jnp.zeros((112,), F32)])[None]
    arrived = [swap_all(cut[c * nd : (c + 1) * nd], direct) for c in range(chunks)]
    if not direct:
        arrived[0] = [
            jnp.concatenate([jnp.pad(p, ((0, 0), (0, nb - real), (0, 0))).reshape(R, LAT), gathered[j]])
            for j, p in enumerate(arrived[0])
        ]
    order = arrival_order(nd)
    projectors = call(
        functools.partial(weights_kernel, nd, R),
        [shape(nd * 256, 256, dtype=BF16), shape(nd * 256, 256, dtype=BF16), shape(nd * SLAB, LAT)],
        [pos] + [arrived[0][j] for j in order],
        [pltpu.VMEM((nd, 32, 256), F32)],
        "weights",
    )
    back = []
    for pieces in arrived:
        ready = call(
            functools.partial(filter_kernel, nd, nb, float(total)),
            [shape(R, LAT)] * nd,
            [pos, kb_row, lh, ll, fold, *projectors] + [pieces[j] for j in order],
            [
                pltpu.VMEM(((nd * SLAB + 2 * HALO) * nb, LAT), F32),
                pltpu.VMEM(((nd * SLAB + 2 * HALO) * nb, LAT), F32),
                pltpu.VMEM((nd * nb, 256), F32),
                pltpu.VMEM((nd * nb, 256), F32),
            ],
            "filter",
        )
        if not direct:
            ready = [p.reshape(SLAB, nb, LAT)[:, :real] for p in ready]
        back.append(swap_all(ready, direct))
    if direct:
        filtered, correlation = finish_direct(back, pos, nb, bands, float(total))
    else:
        filtered, correlation = finish_plain(jnp.concatenate(back[0], axis=1), pos_band, band, bands, float(total))
    return filtered.reshape(trial_waves.shape), correlation


def finish_direct(back, pos, nb, bands, total):
    chunks, nd, half = len(back), len(back[0]), SLAB // 2
    z, core, far, far_core = [], [], [], []
    for pieces in back:
        joined, send = call(
            functools.partial(join_kernel, nd, nb),
            [shape(SLAB, nd * nb, LAT), shape(half, nd * nb, LAT)],
            [pos] + pieces,
            (),
            "join",
            far,
        )
        z.append(joined)
        far.append(xor_permute(send, "band", 2))
        core.append(xor_permute(joined, "band", 1))
    part = shape(2, bands // 2, bands)
    block = pltpu.VMEM((2, bands, bands), F32)
    own_keep, own_send = call(
        functools.partial(own_kernel, chunks), [part, part], [pos] + z + core, [block], "own"
    )
    own_1 = own_keep + xor_permute(own_send, "dom", 1)
    far[-1], own_1 = lax.optimization_barrier((far[-1], own_1))
    far_core = [xor_permute(f, "band", 1) for f in far]
    own_2 = own_1 + xor_permute(own_1, "dom", 2)
    own = own_2 + xor_permute(own_2, "dom", 4)
    keep, send, back_keep, back_send = call(
        functools.partial(cross_kernel, chunks),
        [part] * 4,
        [pos] + z + core + far + far_core,
        [block, block],
        "cross",
        [own_2],
    )
    cross = call(
        sum_kernel,
        part,
        [
            keep,
            xor_permute(send, "dom", 1),
            xor_permute(back_keep, "band", 2),
            both_permute(back_send),
        ],
        (),
        "sum",
        [own],
    )
    cross = cross + xor_permute(cross, "dom", 2)
    rows = call(
        functools.partial(pair_kernel, total),
        shape(4, bands // 2, bands),
        [pos, own, cross, xor_permute(cross, "dom", 4)],
        (),
        "pair",
    )
    filtered = call(output_kernel, shape(SLAB, LAT, bands), z, (), "output")
    correlation = call(place_kernel, shape(bands, 4 * bands), [pos, rows, xor_permute(rows, "dom", 1)], (), "place")
    return filtered, correlation


def finish_plain(z, pos, band, bands, total):
    send = lax.dynamic_slice_in_dim(z, (1 - band // 2) * (SLAB // 2), SLAB // 2, 0)
    far = xor_permute(send, "band", 2)
    gram, gram_far = call(
        gram_kernel,
        [shape(4, bands, bands), shape(2, bands, bands)],
        [pos, z, xor_permute(z, "band", 1), far, xor_permute(far, "band", 1)],
        (),
        "gram",
    )
    filtered = call(output_kernel, shape(SLAB, LAT, bands), [z], (), "output")
    start = (1 - band // 2) * 2
    cross = lax.dynamic_slice_in_dim(gram, start, 2, 0) + xor_permute(gram_far, "band", 2)
    gram = lax.dynamic_update_slice_in_dim(gram, cross, start, 0)
    wide = gram.transpose(1, 0, 2).reshape(bands, 4 * bands)
    return filtered, lax.psum(wide, "dom") / total


def solution(mesh):
    return jax.shard_map(
        on_device,
        mesh=mesh,
        in_specs=(
            P("dom", None, None, "band"),
            P("dom", None, None),
            P("dom", None, None),
            P(),
            P("dom", None),
            P("dom", None),
        ),
        out_specs=(P("dom", None, None, "band"), P("band", None)),
        check_vma=False,
    )
```

```python
import functools

import jax
import jax.numpy as jnp
import numpy as np
from jax import lax
from jax.experimental import pallas as pl
from jax.experimental.pallas import tpu as pltpu
from jax.sharding import PartitionSpec as P

HALO = 6
REACH = 4
SLAB = 8
SIDE = 16
LAT = SIDE * SIDE

COEFFS = (
    -5369.0 / 1800.0,
    12.0 / 7.0,
    -15.0 / 56.0,
    10.0 / 189.0,
    -1.0 / 112.0,
    2.0 / 1925.0,
    -1.0 / 16632.0,
)
FILTER_LOWER = 5.0
FILTER_UPPER = 24.0
SPECTRUM_BOTTOM = 0.0
EPSILON = 1e-06

HALF_WIDTH = (FILTER_UPPER - FILTER_LOWER) / 2.0
CENTRE = (FILTER_UPPER + FILTER_LOWER) / 2.0
SIGMA_1 = HALF_WIDTH / (SPECTRUM_BOTTOM - CENTRE)
SIGMA_2 = 1.0 / (2.0 / SIGMA_1 - SIGMA_1)

VMEM_LIMIT = 48 * 1024 * 1024
BF16 = jnp.bfloat16
F32 = jnp.float32
NN = (((1,), (0,)), ((), ()))
NT = (((1,), (1,)), ((), ()))


def dot(a, b, dims=NN):
    return lax.dot_general(a, b, dims, preferred_element_type=F32)


def halves(x):
    hi = x.astype(BF16)
    return hi, (x - hi.astype(F32)).astype(BF16)


def dot3(ah, al, bh, bl, dims=NN):
    return dot(ah, bh, dims) + dot(al, bh, dims) + dot(ah, bl, dims)


def lateral_matrix():
    line = np.zeros((SIDE, SIDE))
    at = np.arange(SIDE)
    for k in range(1, HALO + 1):
        for sign in (1, -1):
            np.add.at(line, ((at + sign * k) % SIDE, at), -0.5 * COEFFS[k])
    eye = np.eye(SIDE)
    return np.kron(line, eye) + np.kron(eye, line)


def relation():
    return [[-1, 0] if q < REACH else [0, 1] for q in range(SLAB)]


def fold_matrix():
    out = np.zeros((256, 384), np.float32)
    for q, pair in enumerate(relation()):
        for half, rel in enumerate(pair):
            for r in range(16):
                out[q * 32 + half * 16 + r, (rel + 1) * 128 + r] = 1.0
    return out


def split_const(matrix):
    matrix = np.asarray(matrix, np.float32)
    hi = jnp.asarray(matrix, F32).astype(BF16)
    lo = (jnp.asarray(matrix, F32) - hi.astype(F32)).astype(BF16)
    return hi, lo


def split_kernel(nd, nb, cell_hbm, x_hbm, v_hbm, w_hbm, code_hbm, *refs):
    outs, (cell_ref, x_ref, v_ref, w_ref, code_ref, scratch, packed, sems) = refs[:nd], refs[nd:]
    copies = [
        pltpu.make_async_copy(source, target, sems.at[k])
        for k, (source, target) in enumerate(
            ((x_hbm, x_ref), (cell_hbm, cell_ref), (v_hbm, v_ref), (w_hbm, w_ref), (code_hbm, code_ref))
        )
    ]
    for copy in copies:
        copy.start()
    i = lax.axis_index("dom")
    for copy in copies[1:]:
        copy.wait()
    cell = cell_ref[...].astype(F32)
    cube = 2 * REACH + 1
    code = code_ref[...].astype(F32)
    off_x = jnp.floor((code + 0.5) * (1.0 / (cube * cube)))
    rest = code - off_x * (cube * cube)
    off_y = jnp.floor((rest + 0.5) * (1.0 / cube))
    off_z = rest - off_y * cube
    for a in range(2):
        packed[a * 8 : a * 8 + 8] = w_ref[a]
        cell_x, cell_y, cell_z = (
            cell[a : a + 1, k : k + 1] - n * jnp.floor(cell[a : a + 1, k : k + 1] * (1.0 / n))
            for k, n in enumerate((SLAB, SIDE, SIDE))
        )
        y = off_y[a : a + 1] + (cell_y + float(SIDE - REACH))
        z = off_z[a : a + 1] + (cell_z + float(SIDE - REACH))
        y = y - SIDE * jnp.floor(y * (1.0 / SIDE))
        z = z - SIDE * jnp.floor(z * (1.0 / SIDE))
        packed[16 + a : 17 + a] = off_x[a : a + 1] + cell_x
        packed[18 + a : 19 + a] = y * SIDE + z
    packed[20:24] = jnp.zeros((4, LAT), F32)
    packed[24:32] = jnp.concatenate([v_ref[:, y, :] for y in range(SIDE)], axis=1)
    copies[0].wait()
    for q in range(SLAB):
        scratch[q] = x_ref[q].T
    for j in range(nd):
        start = (i ^ j) * nb
        for q in range(SLAB):
            outs[j][q * nb : (q + 1) * nb] = scratch[q, pl.ds(pl.multiple_of(start, nb), nb)]
        outs[j][SLAB * nb :] = packed[...]


def build_projectors(nd, scratch, wh_ref, wl_ref, v_ref):
    lat = lax.broadcasted_iota(jnp.int32, (LAT, 256), 0).astype(F32)
    plane = lax.broadcasted_iota(jnp.int32, (16, 1, 1), 0).astype(F32)
    diagonal = -1.5 * COEFFS[0] - CENTRE

    def body(s, carry):
        his, los = [], []
        for a in range(2):
            w = scratch[s, a * 8 : a * 8 + 8]
            px = scratch[s, 16 + a : 17 + a]
            place = scratch[s, 18 + a : 19 + a]
            hot = jnp.where(lat == place, 1.0, 0.0).astype(BF16)
            masked = jnp.where(px[None] == plane, w[None], 0.0).reshape(128, 256)
            mh, ml = halves(masked)
            his.append(dot(mh, hot, NT).reshape(16, 8, LAT))
            los.append(dot(ml, hot, NT).reshape(16, 8, LAT))
        hi = jnp.concatenate(his, axis=1).astype(BF16)
        lo = jnp.concatenate(los, axis=1).astype(BF16)
        for t in range(16):
            p = (s * SLAB - REACH + t + nd * SLAB) % (nd * SLAB) if isinstance(s, int) else lax.rem(
                s * SLAB - REACH + t + nd * SLAB, nd * SLAB
            )
            row = pl.ds(pl.multiple_of(p * 32 + (16 if t < SLAB else 0), 16), 16)
            wh_ref[row] = hi[t]
            wl_ref[row] = lo[t]
        v_ref[pl.ds(pl.multiple_of(s * SLAB, SLAB), SLAB)] = scratch[s, 24:32] + diagonal
        return carry

    if nd <= 8:
        for s in range(nd):
            body(s, 0)
    else:
        lax.fori_loop(0, nd, body, 0)


def arrival_order(nd):
    return [*range(nd // 2, nd), *range(1, nd // 2), 0]


def filter_kernel(nd, nb, total, pos_ref, kb_ref, lh_ref, ll_ref, fold_ref, *refs):
    pieces, outs = refs[:nd], refs[nd : 2 * nd]
    f0_ref, f1_ref, fold_out, spread_out, wh_ref, wl_ref, v_ref, packed, fh_ref, fl_ref, acc_ref = refs[2 * nd :]
    i = pos_ref[0]
    R = SLAB * nb
    rows_q = lax.broadcasted_iota(jnp.int32, (SLAB, nb, 256), 0)
    lanes_q = lax.broadcasted_iota(jnp.int32, (SLAB, nb, 256), 2) // 32
    same = rows_q == lanes_q

    def slab_rows(s, k=0):
        return pl.ds(pl.multiple_of((s * SLAB + HALO + k) * nb, nb), R)

    def wrap(ref):
        ref[0 : HALO * nb] = ref[nd * R : nd * R + HALO * nb]
        ref[HALO * nb + nd * R : 2 * HALO * nb + nd * R] = ref[HALO * nb : 2 * HALO * nb]

    def each(body):
        if nd <= 8:
            for s in range(nd):
                body(s)
        else:
            lax.fori_loop(0, nd, lambda s, c: (body(s), c)[1], 0)

    for piece, j in zip(pieces, arrival_order(nd)):
        f0_ref[slab_rows(i ^ j)] = piece[:R]
        packed[i ^ j] = piece[R:]
    wrap(f0_ref)
    build_projectors(nd, packed, wh_ref, wl_ref, v_ref)

    def apply(ref, finish):
        def project(s):
            rows = pl.ds(pl.multiple_of(s * R, R), R)
            fh, fl = halves(ref[slab_rows(s)])
            fh_ref[rows] = fh
            fl_ref[rows] = fl
            w = pl.ds(pl.multiple_of(s * 256, 256), 256)
            g = dot3(fh, fl, wh_ref[w], wl_ref[w], NT).reshape(SLAB, nb, 256)
            fold_out[pl.ds(pl.multiple_of(s * nb, nb), nb)] = jnp.sum(jnp.where(same, g, 0.0), axis=0)

        def lateral(s):
            rows = pl.ds(pl.multiple_of(s * 4 * R, 4 * R), 4 * R)
            acc_ref[rows] = dot3(fh_ref[rows], fl_ref[rows], lh_ref[...], ll_ref[...])

        each(project)
        if nd <= 8:
            for s in range(nd // 4):
                lateral(s)
        else:
            lax.fori_loop(0, nd // 4, lambda s, c: (lateral(s), c)[1], 0)
        gh, gl = halves(fold_out[...])
        h = dot(gh, fold_ref[...]) + dot(gl, fold_ref[...])
        below, at, above = h[:, :128], h[:, 128:256], h[:, 256:]

        def next_slab(x):
            return jnp.concatenate([x[-nb:], x[:-nb]], axis=0)

        def previous_slab(x):
            return jnp.concatenate([x[nb:], x[:nb]], axis=0)

        p = (at + next_slab(above) + previous_slab(below)) * kb_ref[...]
        wide = jnp.concatenate([next_slab(p), p, previous_slab(p)], axis=1)
        ph, plo = halves(wide)
        spread_out[...] = dot(ph, fold_ref[...], NT) + dot(plo, fold_ref[...], NT)

        def step(s):
            f = ref[slab_rows(s)]
            x = jnp.where(same, spread_out[pl.ds(pl.multiple_of(s * nb, nb), nb)][None], 0.0).reshape(R, 256)
            xh, xl = halves(x)
            w = pl.ds(pl.multiple_of(s * 256, 256), 256)
            acc = dot3(xh, xl, wh_ref[w], wl_ref[w]) + acc_ref[pl.ds(pl.multiple_of(s * R, R), R)]
            v = v_ref[pl.ds(pl.multiple_of(s * SLAB, SLAB), SLAB)]
            acc = acc + (f.reshape(SLAB, nb, LAT) * v[:, None, :]).reshape(R, LAT)
            for k in range(1, HALO + 1):
                acc = acc + (-0.5 * COEFFS[k]) * (ref[slab_rows(s, k)] + ref[slab_rows(s, -k)])
            finish(s, acc)

        each(step)

    def first(s, acc):
        f1_ref[slab_rows(s)] = (SIGMA_1 / HALF_WIDTH) * acc

    apply(f0_ref, first)
    wrap(f1_ref)

    def second(s, acc):
        f0_ref_new = (2.0 * SIGMA_2 / HALF_WIDTH) * acc - (SIGMA_1 * SIGMA_2) * f0_ref[slab_rows(s)]
        y2_store(s, f0_ref_new)

    def y2_store(s, value):
        f0_ref[slab_rows(s)] = value

    apply(f1_ref, second)
    square = jnp.zeros((nb, LAT), F32)
    if nd <= 8:
        for s in range(nd):
            y = f0_ref[slab_rows(s)].reshape(SLAB, nb, LAT)
            square = square + jnp.sum(y * y, axis=0)
    else:

        def add(s, total_square):
            y = f0_ref[slab_rows(s)].reshape(SLAB, nb, LAT)
            return total_square + jnp.sum(y * y, axis=0)

        square = lax.fori_loop(0, nd, add, square)
    scale = 1.0 / jnp.sqrt(jnp.sum(square, axis=1, keepdims=True) / total + EPSILON)
    for j in range(nd):
        y = f0_ref[slab_rows(i ^ j)].reshape(SLAB, nb, LAT)
        outs[j][...] = (y * scale[None]).reshape(R, LAT)


def join_kernel(nd, nb, pos_ref, *refs):
    pieces, (z_ref, first_ref, second_ref) = refs[:nd], refs[nd:]
    i, y = pos_ref[0], pos_ref[2]
    for j in range(nd):
        rows = pl.ds(pl.multiple_of((i ^ j) * nb, nb), nb)
        for q in range(SLAB):
            z_ref[q, rows] = pieces[j][q * nb : (q + 1) * nb]
    half = SLAB // 2
    for q in range(half // 2):
        first_ref[q] = z_ref[(1 - y) * half + q]
        second_ref[q] = z_ref[(1 - y) * half + half // 2 + q]


def own_kernel(pos_ref, z_ref, zc_ref, keep_ref, send_ref, g_ref):
    i, b = pos_ref[0], pos_ref[1]
    own = core = None
    for q in range(SLAB):
        zh, zl = halves(z_ref[q])
        ch, cl = halves(zc_ref[q])
        mine, other = dot3(zh, zl, zh, zl, NT), dot3(zh, zl, ch, cl, NT)
        own, core = (mine, other) if own is None else (own + mine, core + other)
    g_ref[b & 1] = own
    g_ref[(b & 1) ^ 1] = core
    cut_rows(i, g_ref, keep_ref, send_ref)


def cut_rows(i, g_ref, keep_ref, send_ref):
    x = i & 1
    for c in range(2):
        keep_ref[c] = g_ref[c, pl.ds(pl.multiple_of(x * 64, 64), 64)]
        send_ref[c] = g_ref[c, pl.ds(pl.multiple_of((1 - x) * 64, 64), 64)]


def cross_kernel(
    pos_ref, z_ref, zc_ref, first, second, core_first, core_second, tie, keep, send, back, back_send, g_ref, back_ref
):
    i, b, y = pos_ref[0], pos_ref[1], pos_ref[2]
    half = SLAB // 2
    totals = None
    for q in range(half):
        zh, zl = halves(z_ref[y * half + q])
        ch, cl = halves(zc_ref[y * half + q])
        fh, fl = halves((first, second)[q // (half // 2)][q % (half // 2)])
        gh, gl = halves((core_first, core_second)[q // (half // 2)][q % (half // 2)])
        now = (
            dot3(zh, zl, fh, fl, NT),
            dot3(zh, zl, gh, gl, NT),
            dot3(fh, fl, zh, zl, NT),
            dot3(fh, fl, ch, cl, NT),
        )
        totals = now if totals is None else tuple(t + n for t, n in zip(totals, now))
    c = b & 1
    g_ref[c], g_ref[c ^ 1], back_ref[c], back_ref[c ^ 1] = totals
    cut_rows(i, g_ref, keep, send)
    cut_rows(i, back_ref, back, back_send)


def sum_kernel(a_ref, b_ref, c_ref, d_ref, tie, out_ref):
    out_ref[...] = (a_ref[...] + b_ref[...]) + (c_ref[...] + d_ref[...])


def pair_kernel(total, pos_ref, own, cross, near, far, far_near, out_ref):
    y = pos_ref[2]
    for c in range(2):
        out_ref[y * 2 + c] = own[c] * (1.0 / total)
        out_ref[(1 - y) * 2 + c] = ((cross[c] + near[c]) + (far[c] + far_near[c])) * (1.0 / total)


def output_kernel(z_ref, out_ref):
    for q in range(SLAB):
        out_ref[q] = z_ref[q].T


def place_kernel(pos_ref, mine, other, out_ref):
    x = pos_ref[0] & 1
    for k in range(4):
        lanes = slice(k * 128, (k + 1) * 128)
        out_ref[pl.ds(pl.multiple_of(x * 64, 64), 64), lanes] = mine[k]
        out_ref[pl.ds(pl.multiple_of((1 - x) * 64, 64), 64), lanes] = other[k]


def gram_kernel(pos_ref, own, core, far, far_core, g_ref, far_ref):
    b, y = pos_ref[1], pos_ref[2]
    half = SLAB // 2

    def add(totals, place, value):
        totals[place] = value if totals.get(place) is None else totals[place] + value

    totals = {}
    for q in range(half):
        for mine in (True, False):
            at = q + y * half if mine else q + (1 - y) * half
            zh, zl = halves(own[at])
            ch, cl = halves(core[at])
            add(totals, "own", dot3(zh, zl, zh, zl, NT))
            add(totals, "core", dot3(zh, zl, ch, cl, NT))
            if mine:
                fh, fl = halves(far[q])
                gh, gl = halves(far_core[q])
                add(totals, "far", dot3(zh, zl, fh, fl, NT))
                add(totals, "far_core", dot3(zh, zl, gh, gl, NT))
                add(totals, "back", dot3(fh, fl, zh, zl, NT))
                add(totals, "back_core", dot3(fh, fl, ch, cl, NT))
    g_ref[b] = totals["own"]
    g_ref[b ^ 1] = totals["core"]
    g_ref[b ^ 2] = totals["far"]
    g_ref[b ^ 3] = totals["far_core"]
    far_ref[b & 1] = totals["back"]
    far_ref[(b & 1) ^ 1] = totals["back_core"]


def call(kernel, out_shape, operands, scratch=(), name=None, ties=()):
    specs = [
        pl.BlockSpec(memory_space=pltpu.SMEM if o.dtype == jnp.int32 and o.size < 128 else pltpu.VMEM) for o in operands
    ] + [pl.BlockSpec(memory_space=pl.ANY) for _ in ties]
    single = not isinstance(out_shape, (list, tuple))
    return pl.pallas_call(
        kernel,
        out_shape=out_shape,
        in_specs=specs,
        out_specs=(
            pl.BlockSpec(memory_space=pltpu.VMEM)
            if single
            else [pl.BlockSpec(memory_space=pltpu.VMEM) for _ in out_shape]
        ),
        scratch_shapes=list(scratch),
        compiler_params=pltpu.CompilerParams(vmem_limit_bytes=VMEM_LIMIT),
        name=name,
    )(*operands, *ties)


def shape(*dims, dtype=F32):
    return jax.ShapeDtypeStruct(dims, dtype)


def xor_permute(value, axis, step):
    count = lax.axis_size(axis)
    return lax.ppermute(value, axis, [(k, k ^ step) for k in range(count)])


def both_permute(value):
    nd, ng = lax.axis_size("dom"), lax.axis_size("band")
    pairs = [(b * nd + d, (b ^ 2) * nd + (d ^ 1)) for b in range(ng) for d in range(nd)]
    return lax.ppermute(value, ("band", "dom"), pairs)


def swap_all(pieces, direct):
    if direct:
        got = {0: pieces[0]}
        for j in range(1, len(pieces)):
            got[j] = xor_permute(pieces[j], "dom", j)
        return [got[j] for j in range(len(pieces))]
    stacked = lax.all_to_all(jnp.stack(pieces), "dom", 0, 0, tiled=True)
    return [stacked[j] for j in range(len(pieces))]


def packed_atoms(potential, proj_weights, atom_cell, point_codes):
    cube = 2 * REACH + 1
    off_x = point_codes // (cube * cube)
    off_y = point_codes // cube % cube
    off_z = point_codes % cube
    plane = atom_cell[:, 0:1] % SLAB + off_x
    cell_y = (atom_cell[:, 1:2] + off_y - REACH) % SIDE
    cell_z = (atom_cell[:, 2:3] + off_z - REACH) % SIDE
    lateral = cell_y * SIDE + cell_z
    return jnp.concatenate(
        [
            proj_weights.reshape(-1, 256),
            plane.astype(F32),
            lateral.astype(F32),
            jnp.zeros((4, 256), F32),
            potential.reshape(SLAB, LAT),
        ],
        axis=0,
    )


def on_device(trial_waves, potential, proj_weights, kb_energy, atom_cell, point_codes):
    nd = lax.axis_size("dom")
    bands = trial_waves.shape[-1]
    direct = nd == 8
    real = bands // nd
    nb = max(real, 8)
    total = nd * SLAB * LAT
    dom = lax.axis_index("dom") if direct else jnp.int32(0)
    band = lax.axis_index("band")
    pos = jnp.stack([dom, band if direct else jnp.int32(0), band // 2]).astype(jnp.int32)
    pos_band = jnp.stack([dom, band, band // 2]).astype(jnp.int32)
    R = SLAB * nb

    waves = trial_waves.reshape(SLAB, LAT, bands)
    if direct:
        cut = call(
            functools.partial(split_kernel, nd, nb),
            [shape(R + 32, LAT)] * nd,
            [],
            [
                pltpu.VMEM(atom_cell.shape, jnp.int32),
                pltpu.VMEM(waves.shape, F32),
                pltpu.VMEM(potential.shape, F32),
                pltpu.VMEM(proj_weights.shape, F32),
                pltpu.VMEM(point_codes.shape, jnp.int32),
                pltpu.VMEM((SLAB, bands, LAT), F32),
                pltpu.VMEM((32, 256), F32),
                pltpu.SemaphoreType.DMA((5,)),
            ],
            "split",
            [atom_cell, waves, potential, proj_weights, point_codes],
        )
    else:
        packed = packed_atoms(potential, proj_weights, atom_cell, point_codes)
        gathered = lax.all_gather(packed, "dom", axis=0)
        turned = waves.transpose(0, 2, 1).reshape(SLAB, nd, real, LAT).transpose(1, 0, 2, 3)
        cut = [turned[j] for j in range(nd)]

    lh, ll = split_const(lateral_matrix())
    fold = jnp.asarray(fold_matrix()).astype(BF16)
    kb_row = jnp.concatenate([kb_energy, kb_energy, jnp.zeros((112,), F32)])[None]
    pieces = swap_all(cut, direct)
    if not direct:
        pieces = [
            jnp.concatenate([jnp.pad(p, ((0, 0), (0, nb - real), (0, 0))).reshape(R, LAT), gathered[j]])
            for j, p in enumerate(pieces)
        ]
    ready = call(
        functools.partial(filter_kernel, nd, nb, float(total)),
        [shape(R, LAT)] * nd,
        [pos, kb_row, lh, ll, fold] + [pieces[j] for j in arrival_order(nd)],
        [
            pltpu.VMEM(((nd * SLAB + 2 * HALO) * nb, LAT), F32),
            pltpu.VMEM(((nd * SLAB + 2 * HALO) * nb, LAT), F32),
            pltpu.VMEM((nd * nb, 256), F32),
            pltpu.VMEM((nd * nb, 256), F32),
            pltpu.VMEM((nd * 256, 256), BF16),
            pltpu.VMEM((nd * 256, 256), BF16),
            pltpu.VMEM((nd * SLAB, LAT), F32),
            pltpu.VMEM((nd, 32, 256), F32),
            pltpu.VMEM((nd * R, LAT), BF16),
            pltpu.VMEM((nd * R, LAT), BF16),
            pltpu.VMEM((nd * R, LAT), F32),
        ],
        "filter",
    )
    if not direct:
        ready = [p.reshape(SLAB, nb, LAT)[:, :real] for p in ready]
    back = swap_all(ready, direct)
    if direct:
        filtered, correlation = finish_direct(back, pos, nb, bands, float(total))
    else:
        filtered, correlation = finish_plain(jnp.concatenate(back, axis=1), pos_band, band, bands, float(total))
    return filtered.reshape(trial_waves.shape), correlation


def finish_direct(back, pos, nb, bands, total):
    nd, half = len(back), SLAB // 2
    z, first, second = call(
        functools.partial(join_kernel, nd, nb),
        [shape(SLAB, bands, LAT), shape(half // 2, bands, LAT), shape(half // 2, bands, LAT)],
        [pos] + back,
        (),
        "join",
    )
    far_first = xor_permute(first, "band", 2)
    z_core = xor_permute(z, "band", 1)
    far_second = xor_permute(second, "band", 2)
    part = shape(2, bands // 2, bands)
    block = pltpu.VMEM((2, bands, bands), F32)
    own_keep, own_send = call(own_kernel, [part, part], [pos, z, z_core], [block], "own")
    own_1 = own_keep + xor_permute(own_send, "dom", 1)
    own_2 = own_1 + xor_permute(own_1, "dom", 2)
    far_second, own_2 = lax.optimization_barrier((far_second, own_2))
    own = own_2 + xor_permute(own_2, "dom", 4)
    keep, send, back_keep, back_send = call(
        cross_kernel,
        [part] * 4,
        [pos, z, z_core, far_first, far_second, xor_permute(far_first, "band", 1), xor_permute(far_second, "band", 1)],
        [block, block],
        "cross",
        [own_2],
    )
    cross = call(
        sum_kernel,
        part,
        [
            keep,
            xor_permute(send, "dom", 1),
            xor_permute(back_keep, "band", 2),
            both_permute(back_send),
        ],
        (),
        "sum",
        [own],
    )
    rows = call(
        functools.partial(pair_kernel, total),
        shape(4, bands // 2, bands),
        [pos, own, cross] + [xor_permute(cross, "dom", step) for step in (2, 4, 6)],
        (),
        "pair",
    )
    filtered = call(output_kernel, shape(SLAB, LAT, bands), [z], (), "output")
    correlation = call(place_kernel, shape(bands, 4 * bands), [pos, rows, xor_permute(rows, "dom", 1)], (), "place")
    return filtered, correlation


def finish_plain(z, pos, band, bands, total):
    send = lax.dynamic_slice_in_dim(z, (1 - band // 2) * (SLAB // 2), SLAB // 2, 0)
    far = xor_permute(send, "band", 2)
    gram, gram_far = call(
        gram_kernel,
        [shape(4, bands, bands), shape(2, bands, bands)],
        [pos, z, xor_permute(z, "band", 1), far, xor_permute(far, "band", 1)],
        (),
        "gram",
    )
    filtered = call(output_kernel, shape(SLAB, LAT, bands), [z], (), "output")
    start = (1 - band // 2) * 2
    cross = lax.dynamic_slice_in_dim(gram, start, 2, 0) + xor_permute(gram_far, "band", 2)
    gram = lax.dynamic_update_slice_in_dim(gram, cross, start, 0)
    wide = gram.transpose(1, 0, 2).reshape(bands, 4 * bands)
    return filtered, lax.psum(wide, "dom") / total


def solution(mesh):
    return jax.shard_map(
        on_device,
        mesh=mesh,
        in_specs=(
            P("dom", None, None, "band"),
            P("dom", None, None),
            P("dom", None, None),
            P(),
            P("dom", None),
            P("dom", None),
        ),
        out_specs=(P("dom", None, None, "band"), P("band", None)),
        check_vma=False,
    )
```

```python
import functools

import jax
import jax.numpy as jnp
import numpy as np
from jax import lax
from jax.experimental import pallas as pl
from jax.experimental.pallas import tpu as pltpu
from jax.sharding import PartitionSpec as P

HALO = 6
REACH = 4
SLAB = 8
SIDE = 16
LAT = SIDE * SIDE

COEFFS = (
    -5369.0 / 1800.0,
    12.0 / 7.0,
    -15.0 / 56.0,
    10.0 / 189.0,
    -1.0 / 112.0,
    2.0 / 1925.0,
    -1.0 / 16632.0,
)
FILTER_LOWER = 5.0
FILTER_UPPER = 24.0
SPECTRUM_BOTTOM = 0.0
EPSILON = 1e-06

HALF_WIDTH = (FILTER_UPPER - FILTER_LOWER) / 2.0
CENTRE = (FILTER_UPPER + FILTER_LOWER) / 2.0
SIGMA_1 = HALF_WIDTH / (SPECTRUM_BOTTOM - CENTRE)
SIGMA_2 = 1.0 / (2.0 / SIGMA_1 - SIGMA_1)

VMEM_LIMIT = 48 * 1024 * 1024
BF16 = jnp.bfloat16
F32 = jnp.float32
NN = (((1,), (0,)), ((), ()))
NT = (((1,), (1,)), ((), ()))


def dot(a, b, dims=NN):
    return lax.dot_general(a, b, dims, preferred_element_type=F32)


def halves(x):
    hi = x.astype(BF16)
    return hi, (x - hi.astype(F32)).astype(BF16)


def dot3(ah, al, bh, bl, dims=NN):
    return dot(ah, bh, dims) + dot(al, bh, dims) + dot(ah, bl, dims)


def lateral_matrix():
    line = np.zeros((SIDE, SIDE))
    at = np.arange(SIDE)
    for k in range(1, HALO + 1):
        for sign in (1, -1):
            np.add.at(line, ((at + sign * k) % SIDE, at), -0.5 * COEFFS[k])
    eye = np.eye(SIDE)
    return np.kron(line, eye) + np.kron(eye, line)


def relation():
    return [[-1, 0] if q < REACH else [0, 1] for q in range(SLAB)]


def fold_matrix():
    out = np.zeros((256, 384), np.float32)
    for q, pair in enumerate(relation()):
        for half, rel in enumerate(pair):
            for r in range(16):
                out[q * 32 + half * 16 + r, (rel + 1) * 128 + r] = 1.0
    return out


def split_const(matrix):
    matrix = np.asarray(matrix, np.float32)
    hi = jnp.asarray(matrix, F32).astype(BF16)
    lo = (jnp.asarray(matrix, F32) - hi.astype(F32)).astype(BF16)
    return hi, lo


def split_kernel(nd, nb, cell_hbm, x_hbm, v_hbm, w_hbm, code_hbm, *refs):
    outs, (cell_ref, x_ref, v_ref, w_ref, code_ref, scratch, packed, sems) = refs[:nd], refs[nd:]
    copies = [
        pltpu.make_async_copy(source, target, sems.at[k])
        for k, (source, target) in enumerate(
            ((x_hbm, x_ref), (cell_hbm, cell_ref), (v_hbm, v_ref), (w_hbm, w_ref), (code_hbm, code_ref))
        )
    ]
    for copy in copies:
        copy.start()
    i = lax.axis_index("dom")
    for copy in copies[1:]:
        copy.wait()
    cell = cell_ref[...].astype(F32)
    cube = 2 * REACH + 1
    code = code_ref[...].astype(F32)
    off_x = jnp.floor((code + 0.5) * (1.0 / (cube * cube)))
    rest = code - off_x * (cube * cube)
    off_y = jnp.floor((rest + 0.5) * (1.0 / cube))
    off_z = rest - off_y * cube
    for a in range(2):
        packed[a * 8 : a * 8 + 8] = w_ref[a]
        cell_x, cell_y, cell_z = (
            cell[a : a + 1, k : k + 1] - n * jnp.floor(cell[a : a + 1, k : k + 1] * (1.0 / n))
            for k, n in enumerate((SLAB, SIDE, SIDE))
        )
        y = off_y[a : a + 1] + (cell_y + float(SIDE - REACH))
        z = off_z[a : a + 1] + (cell_z + float(SIDE - REACH))
        y = y - SIDE * jnp.floor(y * (1.0 / SIDE))
        z = z - SIDE * jnp.floor(z * (1.0 / SIDE))
        packed[16 + a : 17 + a] = off_x[a : a + 1] + cell_x
        packed[18 + a : 19 + a] = y * SIDE + z
    packed[20:24] = jnp.zeros((4, LAT), F32)
    packed[24:32] = jnp.concatenate([v_ref[:, y, :] for y in range(SIDE)], axis=1)
    copies[0].wait()
    for q in range(SLAB):
        scratch[q] = x_ref[q].T
    for j in range(nd):
        start = (i ^ j) * nb
        for q in range(SLAB):
            outs[j][q * nb : (q + 1) * nb] = scratch[q, pl.ds(pl.multiple_of(start, nb), nb)]
        outs[j][SLAB * nb :] = packed[...]


def build_projectors(nd, scratch, wh_ref, wl_ref, v_ref):
    lat = lax.broadcasted_iota(jnp.int32, (LAT, 256), 0).astype(F32)
    plane = lax.broadcasted_iota(jnp.int32, (16, 1, 1), 0).astype(F32)
    diagonal = -1.5 * COEFFS[0] - CENTRE

    def body(s, carry):
        his, los = [], []
        for a in range(2):
            w = scratch[s, a * 8 : a * 8 + 8]
            px = scratch[s, 16 + a : 17 + a]
            place = scratch[s, 18 + a : 19 + a]
            hot = jnp.where(lat == place, 1.0, 0.0).astype(BF16)
            masked = jnp.where(px[None] == plane, w[None], 0.0).reshape(128, 256)
            mh, ml = halves(masked)
            his.append(dot(mh, hot, NT).reshape(16, 8, LAT))
            los.append(dot(ml, hot, NT).reshape(16, 8, LAT))
        hi = jnp.concatenate(his, axis=1).astype(BF16)
        lo = jnp.concatenate(los, axis=1).astype(BF16)
        for t in range(16):
            p = (s * SLAB - REACH + t + nd * SLAB) % (nd * SLAB) if isinstance(s, int) else lax.rem(
                s * SLAB - REACH + t + nd * SLAB, nd * SLAB
            )
            row = pl.ds(pl.multiple_of(p * 32 + (16 if t < SLAB else 0), 16), 16)
            wh_ref[row] = hi[t]
            wl_ref[row] = lo[t]
        v_ref[pl.ds(pl.multiple_of(s * SLAB, SLAB), SLAB)] = scratch[s, 24:32] + diagonal
        return carry

    if nd <= 8:
        for s in range(nd):
            body(s, 0)
    else:
        lax.fori_loop(0, nd, body, 0)


def arrival_order(nd):
    return [*range(nd // 2, nd), *range(1, nd // 2), 0]


def filter_kernel(nd, nb, total, pos_ref, kb_ref, lh_ref, ll_ref, fold_ref, *refs):
    pieces, outs = refs[:nd], refs[nd : 3 * nd]
    f0_ref, f1_ref, fold_out, spread_out, wh_ref, wl_ref, v_ref, packed, fh_ref, fl_ref, acc_ref = refs[3 * nd :]
    i = pos_ref[0]
    R = SLAB * nb
    rows_q = lax.broadcasted_iota(jnp.int32, (SLAB, nb, 256), 0)
    lanes_q = lax.broadcasted_iota(jnp.int32, (SLAB, nb, 256), 2) // 32
    same = rows_q == lanes_q

    def slab_rows(s, k=0):
        return pl.ds(pl.multiple_of((s * SLAB + HALO + k) * nb, nb), R)

    def wrap(ref):
        ref[0 : HALO * nb] = ref[nd * R : nd * R + HALO * nb]
        ref[HALO * nb + nd * R : 2 * HALO * nb + nd * R] = ref[HALO * nb : 2 * HALO * nb]

    def each(body):
        if nd <= 8:
            for s in range(nd):
                body(s)
        else:
            lax.fori_loop(0, nd, lambda s, c: (body(s), c)[1], 0)

    for piece, j in zip(pieces, arrival_order(nd)):
        f0_ref[slab_rows(i ^ j)] = piece[:R]
        packed[i ^ j] = piece[R:]
    wrap(f0_ref)
    build_projectors(nd, packed, wh_ref, wl_ref, v_ref)

    def apply(ref, finish):
        def project(s):
            rows = pl.ds(pl.multiple_of(s * R, R), R)
            fh, fl = halves(ref[slab_rows(s)])
            fh_ref[rows] = fh
            fl_ref[rows] = fl
            w = pl.ds(pl.multiple_of(s * 256, 256), 256)
            g = dot3(fh, fl, wh_ref[w], wl_ref[w], NT).reshape(SLAB, nb, 256)
            fold_out[pl.ds(pl.multiple_of(s * nb, nb), nb)] = jnp.sum(jnp.where(same, g, 0.0), axis=0)

        def lateral(s):
            rows = pl.ds(pl.multiple_of(s * 4 * R, 4 * R), 4 * R)
            acc_ref[rows] = dot3(fh_ref[rows], fl_ref[rows], lh_ref[...], ll_ref[...])

        each(project)
        if nd <= 8:
            for s in range(nd // 4):
                lateral(s)
        else:
            lax.fori_loop(0, nd // 4, lambda s, c: (lateral(s), c)[1], 0)
        gh, gl = halves(fold_out[...])
        h = dot(gh, fold_ref[...]) + dot(gl, fold_ref[...])
        below, at, above = h[:, :128], h[:, 128:256], h[:, 256:]

        def next_slab(x):
            return jnp.concatenate([x[-nb:], x[:-nb]], axis=0)

        def previous_slab(x):
            return jnp.concatenate([x[nb:], x[:nb]], axis=0)

        p = (at + next_slab(above) + previous_slab(below)) * kb_ref[...]
        wide = jnp.concatenate([next_slab(p), p, previous_slab(p)], axis=1)
        ph, plo = halves(wide)
        spread_out[...] = dot(ph, fold_ref[...], NT) + dot(plo, fold_ref[...], NT)

        def step(s):
            f = ref[slab_rows(s)]
            x = jnp.where(same, spread_out[pl.ds(pl.multiple_of(s * nb, nb), nb)][None], 0.0).reshape(R, 256)
            xh, xl = halves(x)
            w = pl.ds(pl.multiple_of(s * 256, 256), 256)
            acc = dot3(xh, xl, wh_ref[w], wl_ref[w]) + acc_ref[pl.ds(pl.multiple_of(s * R, R), R)]
            v = v_ref[pl.ds(pl.multiple_of(s * SLAB, SLAB), SLAB)]
            acc = acc + (f.reshape(SLAB, nb, LAT) * v[:, None, :]).reshape(R, LAT)
            for k in range(1, HALO + 1):
                acc = acc + (-0.5 * COEFFS[k]) * (ref[slab_rows(s, k)] + ref[slab_rows(s, -k)])
            finish(s, acc)

        each(step)

    def first(s, acc):
        f1_ref[slab_rows(s)] = (SIGMA_1 / HALF_WIDTH) * acc

    apply(f0_ref, first)
    wrap(f1_ref)

    def second(s, acc):
        f0_ref_new = (2.0 * SIGMA_2 / HALF_WIDTH) * acc - (SIGMA_1 * SIGMA_2) * f0_ref[slab_rows(s)]
        y2_store(s, f0_ref_new)

    def y2_store(s, value):
        f0_ref[slab_rows(s)] = value

    apply(f1_ref, second)
    square = jnp.zeros((nb, LAT), F32)
    if nd <= 8:
        for s in range(nd):
            y = f0_ref[slab_rows(s)].reshape(SLAB, nb, LAT)
            square = square + jnp.sum(y * y, axis=0)
    else:

        def add(s, total_square):
            y = f0_ref[slab_rows(s)].reshape(SLAB, nb, LAT)
            return total_square + jnp.sum(y * y, axis=0)

        square = lax.fori_loop(0, nd, add, square)
    scale = 1.0 / jnp.sqrt(jnp.sum(square, axis=1, keepdims=True) / total + EPSILON)
    chip, half = pos_ref[2], SLAB // 2
    for j in range(nd):
        for h, out in ((1 - chip, outs[j]), (chip, outs[nd + j])):
            start = ((i ^ j) * SLAB + HALO + h * half) * nb
            y = f0_ref[pl.ds(pl.multiple_of(start, nb), half * nb)].reshape(half, nb, LAT)
            out[...] = (y * scale[None]).reshape(half * nb, LAT)


def join_kernel(nd, nb, pos_ref, *refs):
    pieces, z_ref = refs[:nd], refs[-1]
    i = pos_ref[0]
    for j in range(nd):
        rows = pl.ds(pl.multiple_of((i ^ j) * nb, nb), nb)
        for q in range(SLAB // 2):
            z_ref[q, rows] = pieces[j][q * nb : (q + 1) * nb]


def blocks_kernel(pos_ref, za, zb, ca, cb, far, far_core, keep, send, back, back_send, g_ref, back_ref):
    i, c = pos_ref[0], pos_ref[1] & 1
    totals = None
    for q in range(SLAB // 2):
        zh, zl = halves(zb[q])
        ch, cl = halves(cb[q])
        fh, fl = halves(far[q])
        gh, gl = halves(far_core[q])
        wh, wl = halves(za[q])
        xh, xl = halves(ca[q])
        now = (
            dot3(zh, zl, zh, zl, NT) + dot3(wh, wl, wh, wl, NT),
            dot3(zh, zl, ch, cl, NT) + dot3(wh, wl, xh, xl, NT),
            dot3(zh, zl, fh, fl, NT),
            dot3(zh, zl, gh, gl, NT),
            dot3(fh, fl, zh, zl, NT),
            dot3(fh, fl, ch, cl, NT),
        )
        totals = now if totals is None else tuple(t + n for t, n in zip(totals, now))
    g_ref[c], g_ref[c ^ 1], g_ref[2 + c], g_ref[2 + (c ^ 1)], back_ref[c], back_ref[c ^ 1] = totals
    cut_rows(i & 1, g_ref, keep, send)
    cut_rows(i & 1, back_ref, back, back_send)


def cut_rows(bit, g_ref, keep_ref, send_ref):
    size = keep_ref.shape[1]
    keep_ref[...] = g_ref[:, pl.ds(pl.multiple_of(bit * size, size), size)]
    send_ref[...] = g_ref[:, pl.ds(pl.multiple_of((1 - bit) * size, size), size)]


def sum_kernel(pos_ref, keep, other, back, back_other, keep_ref, send_ref, sum_ref):
    sum_ref[0:2] = keep[0:2] + other[0:2]
    sum_ref[2:4] = (keep[2:4] + other[2:4]) + (back[...] + back_other[...])
    cut_rows((pos_ref[0] >> 1) & 1, sum_ref, keep_ref, send_ref)


def pair_kernel(total, pos_ref, mine, other, out_ref):
    y = pos_ref[2]
    for c in range(2):
        out_ref[y * 2 + c] = (mine[c] + other[c]) * (1.0 / total)
        out_ref[(1 - y) * 2 + c] = (mine[2 + c] + other[2 + c]) * (1.0 / total)


def output_kernel(pos_ref, za, zb, out_ref):
    y, half = pos_ref[2], SLAB // 2
    for q in range(half):
        out_ref[(1 - y) * half + q] = za[q].T
        out_ref[y * half + q] = zb[q].T


def place_kernel(pos_ref, *refs):
    pieces, out_ref = refs[:-1], refs[-1]
    size = pieces[0].shape[1]
    for j, piece in enumerate(pieces):
        source = pos_ref[0] ^ j
        start = (source & 1) * (2 * size) + ((source >> 1) & 1) * size
        for k in range(4):
            out_ref[pl.ds(pl.multiple_of(start, size), size), k * 128 : (k + 1) * 128] = piece[k]


def gram_kernel(pos_ref, own, core, far, far_core, g_ref, far_ref):
    b, y = pos_ref[1], pos_ref[2]
    half = SLAB // 2

    def add(totals, place, value):
        totals[place] = value if totals.get(place) is None else totals[place] + value

    totals = {}
    for q in range(half):
        for mine in (True, False):
            at = q + y * half if mine else q + (1 - y) * half
            zh, zl = halves(own[at])
            ch, cl = halves(core[at])
            add(totals, "own", dot3(zh, zl, zh, zl, NT))
            add(totals, "core", dot3(zh, zl, ch, cl, NT))
            if mine:
                fh, fl = halves(far[q])
                gh, gl = halves(far_core[q])
                add(totals, "far", dot3(zh, zl, fh, fl, NT))
                add(totals, "far_core", dot3(zh, zl, gh, gl, NT))
                add(totals, "back", dot3(fh, fl, zh, zl, NT))
                add(totals, "back_core", dot3(fh, fl, ch, cl, NT))
    g_ref[b] = totals["own"]
    g_ref[b ^ 1] = totals["core"]
    g_ref[b ^ 2] = totals["far"]
    g_ref[b ^ 3] = totals["far_core"]
    far_ref[b & 1] = totals["back"]
    far_ref[(b & 1) ^ 1] = totals["back_core"]


def call(kernel, out_shape, operands, scratch=(), name=None, ties=(), hbm=()):
    specs = [
        pl.BlockSpec(memory_space=pltpu.SMEM if o.dtype == jnp.int32 and o.size < 128 else pltpu.VMEM) for o in operands
    ]
    specs = [pl.BlockSpec(memory_space=pltpu.HBM) for _ in hbm] + specs + [pl.BlockSpec(memory_space=pl.ANY) for _ in ties]
    single = not isinstance(out_shape, (list, tuple))
    return pl.pallas_call(
        kernel,
        out_shape=out_shape,
        in_specs=specs,
        out_specs=(
            pl.BlockSpec(memory_space=pltpu.VMEM)
            if single
            else [pl.BlockSpec(memory_space=pltpu.VMEM) for _ in out_shape]
        ),
        scratch_shapes=list(scratch),
        compiler_params=pltpu.CompilerParams(vmem_limit_bytes=VMEM_LIMIT),
        name=name,
    )(*hbm, *operands, *ties)


def shape(*dims, dtype=F32):
    return jax.ShapeDtypeStruct(dims, dtype)


def xor_permute(value, axis, step):
    count = lax.axis_size(axis)
    return lax.ppermute(value, axis, [(k, k ^ step) for k in range(count)])


def both_permute(value):
    nd, ng = lax.axis_size("dom"), lax.axis_size("band")
    pairs = [(b * nd + d, (b ^ 2) * nd + (d ^ 1)) for b in range(ng) for d in range(nd)]
    return lax.ppermute(value, ("band", "dom"), pairs)


def swap_all(pieces, direct):
    if direct:
        got = {0: pieces[0]}
        for j in range(1, len(pieces)):
            got[j] = xor_permute(pieces[j], "dom", j)
        return [got[j] for j in range(len(pieces))]
    stacked = lax.all_to_all(jnp.stack(pieces), "dom", 0, 0, tiled=True)
    return [stacked[j] for j in range(len(pieces))]


def packed_atoms(potential, proj_weights, atom_cell, point_codes):
    cube = 2 * REACH + 1
    off_x = point_codes // (cube * cube)
    off_y = point_codes // cube % cube
    off_z = point_codes % cube
    plane = atom_cell[:, 0:1] % SLAB + off_x
    cell_y = (atom_cell[:, 1:2] + off_y - REACH) % SIDE
    cell_z = (atom_cell[:, 2:3] + off_z - REACH) % SIDE
    lateral = cell_y * SIDE + cell_z
    return jnp.concatenate(
        [
            proj_weights.reshape(-1, 256),
            plane.astype(F32),
            lateral.astype(F32),
            jnp.zeros((4, 256), F32),
            potential.reshape(SLAB, LAT),
        ],
        axis=0,
    )


def on_device(trial_waves, potential, proj_weights, kb_energy, atom_cell, point_codes):
    nd = lax.axis_size("dom")
    bands = trial_waves.shape[-1]
    direct = nd == 8
    real = bands // nd
    nb = max(real, 8)
    total = nd * SLAB * LAT
    dom = lax.axis_index("dom") if direct else jnp.int32(0)
    band = lax.axis_index("band")
    pos = jnp.stack([dom, band if direct else jnp.int32(0), band // 2 if direct else jnp.int32(0)]).astype(jnp.int32)
    pos_band = jnp.stack([dom, band, band // 2]).astype(jnp.int32)
    R = SLAB * nb

    waves = trial_waves.reshape(SLAB, LAT, bands)
    if direct:
        cut = call(
            functools.partial(split_kernel, nd, nb),
            [shape(R + 32, LAT)] * nd,
            [],
            [
                pltpu.VMEM(atom_cell.shape, jnp.int32),
                pltpu.VMEM(waves.shape, F32),
                pltpu.VMEM(potential.shape, F32),
                pltpu.VMEM(proj_weights.shape, F32),
                pltpu.VMEM(point_codes.shape, jnp.int32),
                pltpu.VMEM((SLAB, bands, LAT), F32),
                pltpu.VMEM((32, 256), F32),
                pltpu.SemaphoreType.DMA((5,)),
            ],
            "split",
            hbm=[atom_cell, waves, potential, proj_weights, point_codes],
        )
    else:
        packed = packed_atoms(potential, proj_weights, atom_cell, point_codes)
        gathered = lax.all_gather(packed, "dom", axis=0)
        turned = waves.transpose(0, 2, 1).reshape(SLAB, nd, real, LAT).transpose(1, 0, 2, 3)
        cut = [turned[j] for j in range(nd)]

    lh, ll = split_const(lateral_matrix())
    fold = jnp.asarray(fold_matrix()).astype(BF16)
    kb_row = jnp.concatenate([kb_energy, kb_energy, jnp.zeros((112,), F32)])[None]
    pieces = swap_all(cut, direct)
    if not direct:
        pieces = [
            jnp.concatenate([jnp.pad(p, ((0, 0), (0, nb - real), (0, 0))).reshape(R, LAT), gathered[j]])
            for j, p in enumerate(pieces)
        ]
    ready = call(
        functools.partial(filter_kernel, nd, nb, float(total)),
        [shape(R // 2, LAT)] * (2 * nd),
        [pos, kb_row, lh, ll, fold] + [pieces[j] for j in arrival_order(nd)],
        [
            pltpu.VMEM(((nd * SLAB + 2 * HALO) * nb, LAT), F32),
            pltpu.VMEM(((nd * SLAB + 2 * HALO) * nb, LAT), F32),
            pltpu.VMEM((nd * nb, 256), F32),
            pltpu.VMEM((nd * nb, 256), F32),
            pltpu.VMEM((nd * 256, 256), BF16),
            pltpu.VMEM((nd * 256, 256), BF16),
            pltpu.VMEM((nd * SLAB, LAT), F32),
            pltpu.VMEM((nd, 32, 256), F32),
            pltpu.VMEM((nd * R, LAT), BF16),
            pltpu.VMEM((nd * R, LAT), BF16),
            pltpu.VMEM((nd * R, LAT), F32),
        ],
        "filter",
    )
    if direct:
        filtered, correlation = finish_direct(swap_all(ready[:nd], True), swap_all(ready[nd:], True), pos, bands, float(total))
    else:
        ready = [
            jnp.concatenate([ready[nd + j], ready[j]]).reshape(SLAB, nb, LAT)[:, :real] for j in range(nd)
        ]
        back = swap_all(ready, False)
        filtered, correlation = finish_plain(jnp.concatenate(back, axis=1), pos_band, band, bands, float(total))
    return filtered.reshape(trial_waves.shape), correlation


def finish_direct(first, second, pos, bands, total):
    nd, half = len(first), SLAB // 2
    nb = bands // nd

    def join(pieces, ties):
        return call(
            functools.partial(join_kernel, nd, nb), shape(half, bands, LAT), [pos] + pieces, (), "join", ties
        )

    za = join(first, [])
    far = xor_permute(za, "band", 2)
    core_a = xor_permute(za, "band", 1)
    zb = join(second, [far])
    core_b = xor_permute(zb, "band", 1)
    far_core = xor_permute(far, "band", 1)
    part, share = shape(4, bands // 2, bands), shape(2, bands // 2, bands)
    keep, send, back, back_send = call(
        blocks_kernel,
        [part, part, share, share],
        [pos, za, zb, core_a, core_b, far, far_core],
        [pltpu.VMEM((4, bands, bands), F32), pltpu.VMEM((2, bands, bands), F32)],
        "blocks",
    )
    piece = shape(4, bands // 4, bands)
    keep, send = call(
        sum_kernel,
        [piece, piece],
        [pos, keep, xor_permute(send, "dom", 1), xor_permute(back, "band", 2), both_permute(back_send)],
        [pltpu.VMEM((4, bands // 2, bands), F32)],
        "sum",
    )
    mine = keep + xor_permute(send, "dom", 2)
    rows = call(
        functools.partial(pair_kernel, total), piece, [pos, mine, xor_permute(mine, "dom", 4)], (), "pair"
    )
    filtered = call(output_kernel, shape(SLAB, LAT, bands), [pos, za, zb], (), "output")
    correlation = call(
        place_kernel,
        shape(bands, 4 * bands),
        [pos, rows] + [xor_permute(rows, "dom", step) for step in (1, 2, 3)],
        (),
        "place",
    )
    return filtered, correlation


def finish_plain(z, pos, band, bands, total):
    send = lax.dynamic_slice_in_dim(z, (1 - band // 2) * (SLAB // 2), SLAB // 2, 0)
    far = xor_permute(send, "band", 2)
    gram, gram_far = call(
        gram_kernel,
        [shape(4, bands, bands), shape(2, bands, bands)],
        [pos, z, xor_permute(z, "band", 1), far, xor_permute(far, "band", 1)],
        (),
        "gram",
    )
    filtered = z.transpose(0, 2, 1)
    start = (1 - band // 2) * 2
    cross = lax.dynamic_slice_in_dim(gram, start, 2, 0) + xor_permute(gram_far, "band", 2)
    gram = lax.dynamic_update_slice_in_dim(gram, cross, start, 0)
    wide = gram.transpose(1, 0, 2).reshape(bands, 4 * bands)
    return filtered, lax.psum(wide, "dom") / total


def solution(mesh):
    return jax.shard_map(
        on_device,
        mesh=mesh,
        in_specs=(
            P("dom", None, None, "band"),
            P("dom", None, None),
            P("dom", None, None),
            P(),
            P("dom", None),
            P("dom", None),
        ),
        out_specs=(P("dom", None, None, "band"), P("band", None)),
        check_vma=False,
    )
```

```python
import functools

import jax
import jax.numpy as jnp
import numpy as np
from jax import lax
from jax.experimental import pallas as pl
from jax.experimental.pallas import tpu as pltpu
from jax.sharding import PartitionSpec as P

HALO = 6
REACH = 4
SLAB = 8
PARTS = 4
SIDE = 16
LAT = SIDE * SIDE

COEFFS = (
    -5369.0 / 1800.0,
    12.0 / 7.0,
    -15.0 / 56.0,
    10.0 / 189.0,
    -1.0 / 112.0,
    2.0 / 1925.0,
    -1.0 / 16632.0,
)
FILTER_LOWER = 5.0
FILTER_UPPER = 24.0
SPECTRUM_BOTTOM = 0.0
EPSILON = 1e-06

HALF_WIDTH = (FILTER_UPPER - FILTER_LOWER) / 2.0
CENTRE = (FILTER_UPPER + FILTER_LOWER) / 2.0
SIGMA_1 = HALF_WIDTH / (SPECTRUM_BOTTOM - CENTRE)
SIGMA_2 = 1.0 / (2.0 / SIGMA_1 - SIGMA_1)

VMEM_LIMIT = 48 * 1024 * 1024
BF16 = jnp.bfloat16
F32 = jnp.float32
NN = (((1,), (0,)), ((), ()))
NT = (((1,), (1,)), ((), ()))


def dot(a, b, dims=NN):
    return lax.dot_general(a, b, dims, preferred_element_type=F32)


def halves(x):
    hi = x.astype(BF16)
    return hi, (x - hi.astype(F32)).astype(BF16)


def dot3(ah, al, bh, bl, dims=NN):
    return dot(ah, bh, dims) + dot(al, bh, dims) + dot(ah, bl, dims)


def lateral_matrix():
    line = np.zeros((SIDE, SIDE))
    at = np.arange(SIDE)
    for k in range(1, HALO + 1):
        for sign in (1, -1):
            np.add.at(line, ((at + sign * k) % SIDE, at), -0.5 * COEFFS[k])
    eye = np.eye(SIDE)
    return np.kron(line, eye) + np.kron(eye, line)


def relation():
    return [[-1, 0] if q < REACH else [0, 1] for q in range(SLAB)]


def fold_matrix():
    out = np.zeros((256, 384), np.float32)
    for q, pair in enumerate(relation()):
        for half, rel in enumerate(pair):
            for r in range(16):
                out[q * 32 + half * 16 + r, (rel + 1) * 128 + r] = 1.0
    return out


def split_const(matrix):
    matrix = np.asarray(matrix, np.float32)
    hi = jnp.asarray(matrix, F32).astype(BF16)
    lo = (jnp.asarray(matrix, F32) - hi.astype(F32)).astype(BF16)
    return hi, lo


def split_kernel(nd, nb, x_ref, packed_ref, *refs):
    outs, scratch = refs[:-1], refs[-1]
    i = lax.axis_index("dom")
    for q in range(SLAB):
        scratch[q] = x_ref[q].T
    for j in range(nd):
        start = (i ^ j) * nb
        for q in range(SLAB):
            outs[j][q * nb : (q + 1) * nb] = scratch[q, pl.ds(pl.multiple_of(start, nb), nb)]
        outs[j][SLAB * nb :] = packed_ref[...]


def build_projectors(nd, scratch, wh_ref, wl_ref, v_ref):
    lat = lax.broadcasted_iota(jnp.int32, (LAT, 256), 0).astype(F32)
    plane = lax.broadcasted_iota(jnp.int32, (16, 1, 1), 0).astype(F32)
    diagonal = -1.5 * COEFFS[0] - CENTRE

    def body(s, carry):
        his, los = [], []
        for a in range(2):
            w = scratch[s, a * 8 : a * 8 + 8]
            px = scratch[s, 16 + a : 17 + a]
            place = scratch[s, 18 + a : 19 + a]
            hot = jnp.where(lat == place, 1.0, 0.0).astype(BF16)
            masked = jnp.where(px[None] == plane, w[None], 0.0).reshape(128, 256)
            mh, ml = halves(masked)
            his.append(dot(mh, hot, NT).reshape(16, 8, LAT))
            los.append(dot(ml, hot, NT).reshape(16, 8, LAT))
        hi = jnp.concatenate(his, axis=1).astype(BF16)
        lo = jnp.concatenate(los, axis=1).astype(BF16)
        for t in range(16):
            p = (s * SLAB - REACH + t + nd * SLAB) % (nd * SLAB) if isinstance(s, int) else lax.rem(
                s * SLAB - REACH + t + nd * SLAB, nd * SLAB
            )
            row = pl.ds(pl.multiple_of(p * 32 + (16 if t < SLAB else 0), 16), 16)
            wh_ref[row] = hi[t]
            wl_ref[row] = lo[t]
        v_ref[pl.ds(pl.multiple_of(s * SLAB, SLAB), SLAB)] = scratch[s, 24:32] + diagonal
        return carry

    if nd <= 8:
        for s in range(nd):
            body(s, 0)
    else:
        lax.fori_loop(0, nd, body, 0)


def arrival_order(nd):
    return [1, 2, *range(nd // 2, nd), *range(3, nd // 2), 0]


def filter_kernel(nd, nb, total, pos_ref, kb_ref, lh_ref, ll_ref, fold_ref, *refs):
    pieces, outs = refs[:nd], refs[nd : 3 * nd]
    f0_ref, f1_ref, fold_out, spread_out, wh_ref, wl_ref, v_ref, packed, fh_ref, fl_ref, acc_ref = refs[3 * nd :]
    i = pos_ref[0]
    R = SLAB * nb
    rows_q = lax.broadcasted_iota(jnp.int32, (SLAB, nb, 256), 0)
    lanes_q = lax.broadcasted_iota(jnp.int32, (SLAB, nb, 256), 2) // 32
    same = rows_q == lanes_q

    def slab_rows(s, k=0):
        return pl.ds(pl.multiple_of((s * SLAB + HALO + k) * nb, nb), R)

    def wrap(ref):
        ref[0 : HALO * nb] = ref[nd * R : nd * R + HALO * nb]
        ref[HALO * nb + nd * R : 2 * HALO * nb + nd * R] = ref[HALO * nb : 2 * HALO * nb]

    def each(body):
        if nd <= 8:
            for s in range(nd):
                body(s)
        else:
            lax.fori_loop(0, nd, lambda s, c: (body(s), c)[1], 0)

    for piece, j in zip(pieces, arrival_order(nd)):
        f0_ref[slab_rows(i ^ j)] = piece[:R]
        packed[i ^ j] = piece[R:]
    wrap(f0_ref)
    build_projectors(nd, packed, wh_ref, wl_ref, v_ref)

    def apply(ref, finish):
        def project(s):
            rows = pl.ds(pl.multiple_of(s * R, R), R)
            fh, fl = halves(ref[slab_rows(s)])
            fh_ref[rows] = fh
            fl_ref[rows] = fl
            w = pl.ds(pl.multiple_of(s * 256, 256), 256)
            g = dot3(fh, fl, wh_ref[w], wl_ref[w], NT).reshape(SLAB, nb, 256)
            fold_out[pl.ds(pl.multiple_of(s * nb, nb), nb)] = jnp.sum(jnp.where(same, g, 0.0), axis=0)

        def lateral(s):
            rows = pl.ds(pl.multiple_of(s * 4 * R, 4 * R), 4 * R)
            acc_ref[rows] = dot3(fh_ref[rows], fl_ref[rows], lh_ref[...], ll_ref[...])

        each(project)
        if nd <= 8:
            for s in range(nd // 4):
                lateral(s)
        else:
            lax.fori_loop(0, nd // 4, lambda s, c: (lateral(s), c)[1], 0)
        gh, gl = halves(fold_out[...])
        h = dot(gh, fold_ref[...]) + dot(gl, fold_ref[...])
        below, at, above = h[:, :128], h[:, 128:256], h[:, 256:]

        def next_slab(x):
            return jnp.concatenate([x[-nb:], x[:-nb]], axis=0)

        def previous_slab(x):
            return jnp.concatenate([x[nb:], x[:nb]], axis=0)

        p = (at + next_slab(above) + previous_slab(below)) * kb_ref[...]
        wide = jnp.concatenate([next_slab(p), p, previous_slab(p)], axis=1)
        ph, plo = halves(wide)
        spread_out[...] = dot(ph, fold_ref[...], NT) + dot(plo, fold_ref[...], NT)

        def step(s):
            f = ref[slab_rows(s)]
            x = jnp.where(same, spread_out[pl.ds(pl.multiple_of(s * nb, nb), nb)][None], 0.0).reshape(R, 256)
            xh, xl = halves(x)
            w = pl.ds(pl.multiple_of(s * 256, 256), 256)
            acc = dot3(xh, xl, wh_ref[w], wl_ref[w]) + acc_ref[pl.ds(pl.multiple_of(s * R, R), R)]
            v = v_ref[pl.ds(pl.multiple_of(s * SLAB, SLAB), SLAB)]
            acc = acc + (f.reshape(SLAB, nb, LAT) * v[:, None, :]).reshape(R, LAT)
            for k in range(1, HALO + 1):
                acc = acc + (-0.5 * COEFFS[k]) * (ref[slab_rows(s, k)] + ref[slab_rows(s, -k)])
            finish(s, acc)

        each(step)

    def first(s, acc):
        f1_ref[slab_rows(s)] = (SIGMA_1 / HALF_WIDTH) * acc

    apply(f0_ref, first)
    wrap(f1_ref)

    def second(s, acc):
        f0_ref_new = (2.0 * SIGMA_2 / HALF_WIDTH) * acc - (SIGMA_1 * SIGMA_2) * f0_ref[slab_rows(s)]
        y2_store(s, f0_ref_new)

    def y2_store(s, value):
        f0_ref[slab_rows(s)] = value

    apply(f1_ref, second)
    square = jnp.zeros((nb, LAT), F32)
    if nd <= 8:
        for s in range(nd):
            y = f0_ref[slab_rows(s)].reshape(SLAB, nb, LAT)
            square = square + jnp.sum(y * y, axis=0)
    else:

        def add(s, total_square):
            y = f0_ref[slab_rows(s)].reshape(SLAB, nb, LAT)
            return total_square + jnp.sum(y * y, axis=0)

        square = lax.fori_loop(0, nd, add, square)
    scale = 1.0 / jnp.sqrt(jnp.sum(square, axis=1, keepdims=True) / total + EPSILON)
    chip, half = pos_ref[2], SLAB // 2
    for j in range(nd):
        for h, out in ((1 - chip, outs[j]), (chip, outs[nd + j])):
            start = ((i ^ j) * SLAB + HALO + h * half) * nb
            y = f0_ref[pl.ds(pl.multiple_of(start, nb), half * nb)].reshape(half, nb, LAT)
            out[...] = (y * scale[None]).reshape(half * nb, LAT)


def join_kernel(nd, nb, outs, pos_ref, *refs):
    pieces, (z_ref, *parts) = refs[:nd], refs[-outs:]
    i = pos_ref[0]
    for j in range(nd):
        rows = pl.ds(pl.multiple_of((i ^ j) * nb, nb), nb)
        for q in range(SLAB // 2):
            z_ref[q, rows] = pieces[j][q * nb : (q + 1) * nb]
    for k, part in enumerate(parts):
        part[...] = z_ref[k * part.shape[0] : (k + 1) * part.shape[0]]


def blocks_kernel(parts, pos_ref, za, zb, ca, cb, *refs):
    far, far_core = refs[:parts], refs[parts : 2 * parts]
    keep, send, back, back_send, g_ref, back_ref = refs[2 * parts :]
    i, c = pos_ref[0], pos_ref[1] & 1
    per = SLAB // 2 // parts
    totals = None
    for q in range(SLAB // 2):
        zh, zl = halves(zb[q])
        ch, cl = halves(cb[q])
        fh, fl = halves(far[q // per][q % per])
        gh, gl = halves(far_core[q // per][q % per])
        wh, wl = halves(za[q])
        xh, xl = halves(ca[q])
        now = (
            dot3(zh, zl, zh, zl, NT) + dot3(wh, wl, wh, wl, NT),
            dot3(zh, zl, ch, cl, NT) + dot3(wh, wl, xh, xl, NT),
            dot3(zh, zl, fh, fl, NT),
            dot3(zh, zl, gh, gl, NT),
            dot3(fh, fl, zh, zl, NT),
            dot3(fh, fl, ch, cl, NT),
        )
        totals = now if totals is None else tuple(t + n for t, n in zip(totals, now))
    g_ref[c], g_ref[c ^ 1], g_ref[2 + c], g_ref[2 + (c ^ 1)], back_ref[c], back_ref[c ^ 1] = totals
    cut_rows(i & 1, g_ref, keep, send)
    cut_rows(i & 1, back_ref, back, back_send)


def cut_rows(bit, g_ref, keep_ref, send_ref):
    size = keep_ref.shape[1]
    keep_ref[...] = g_ref[:, pl.ds(pl.multiple_of(bit * size, size), size)]
    send_ref[...] = g_ref[:, pl.ds(pl.multiple_of((1 - bit) * size, size), size)]


def sum_kernel(pos_ref, keep, other, back, back_other, keep_ref, send_ref, sum_ref):
    sum_ref[0:2] = keep[0:2] + other[0:2]
    sum_ref[2:4] = (keep[2:4] + other[2:4]) + (back[...] + back_other[...])
    cut_rows((pos_ref[0] >> 1) & 1, sum_ref, keep_ref, send_ref)


def pair_kernel(total, pos_ref, mine, other, out_ref):
    y = pos_ref[2]
    for c in range(2):
        out_ref[y * 2 + c] = (mine[c] + other[c]) * (1.0 / total)
        out_ref[(1 - y) * 2 + c] = (mine[2 + c] + other[2 + c]) * (1.0 / total)


def output_kernel(pos_ref, za, zb, out_ref):
    y, half = pos_ref[2], SLAB // 2
    for q in range(half):
        out_ref[(1 - y) * half + q] = za[q].T
        out_ref[y * half + q] = zb[q].T


def place_kernel(pos_ref, *refs):
    pieces, out_ref = refs[:-1], refs[-1]
    size = pieces[0].shape[1]
    for j, piece in enumerate(pieces):
        source = pos_ref[0] ^ j
        start = (source & 1) * (2 * size) + ((source >> 1) & 1) * size
        for k in range(4):
            out_ref[pl.ds(pl.multiple_of(start, size), size), k * 128 : (k + 1) * 128] = piece[k]


def gram_kernel(pos_ref, own, core, far, far_core, g_ref, far_ref):
    b, y = pos_ref[1], pos_ref[2]
    half = SLAB // 2

    def add(totals, place, value):
        totals[place] = value if totals.get(place) is None else totals[place] + value

    totals = {}
    for q in range(half):
        for mine in (True, False):
            at = q + y * half if mine else q + (1 - y) * half
            zh, zl = halves(own[at])
            ch, cl = halves(core[at])
            add(totals, "own", dot3(zh, zl, zh, zl, NT))
            add(totals, "core", dot3(zh, zl, ch, cl, NT))
            if mine:
                fh, fl = halves(far[q])
                gh, gl = halves(far_core[q])
                add(totals, "far", dot3(zh, zl, fh, fl, NT))
                add(totals, "far_core", dot3(zh, zl, gh, gl, NT))
                add(totals, "back", dot3(fh, fl, zh, zl, NT))
                add(totals, "back_core", dot3(fh, fl, ch, cl, NT))
    g_ref[b] = totals["own"]
    g_ref[b ^ 1] = totals["core"]
    g_ref[b ^ 2] = totals["far"]
    g_ref[b ^ 3] = totals["far_core"]
    far_ref[b & 1] = totals["back"]
    far_ref[(b & 1) ^ 1] = totals["back_core"]


def call(kernel, out_shape, operands, scratch=(), name=None, ties=()):
    specs = [
        pl.BlockSpec(memory_space=pltpu.SMEM if o.dtype == jnp.int32 and o.size < 128 else pltpu.VMEM) for o in operands
    ] + [pl.BlockSpec(memory_space=pl.ANY) for _ in ties]
    single = not isinstance(out_shape, (list, tuple))
    return pl.pallas_call(
        kernel,
        out_shape=out_shape,
        in_specs=specs,
        out_specs=(
            pl.BlockSpec(memory_space=pltpu.VMEM)
            if single
            else [pl.BlockSpec(memory_space=pltpu.VMEM) for _ in out_shape]
        ),
        scratch_shapes=list(scratch),
        compiler_params=pltpu.CompilerParams(vmem_limit_bytes=VMEM_LIMIT),
        name=name,
    )(*operands, *ties)


def shape(*dims, dtype=F32):
    return jax.ShapeDtypeStruct(dims, dtype)


def xor_permute(value, axis, step):
    count = lax.axis_size(axis)
    return lax.ppermute(value, axis, [(k, k ^ step) for k in range(count)])


def both_permute(value):
    nd, ng = lax.axis_size("dom"), lax.axis_size("band")
    pairs = [(b * nd + d, (b ^ 2) * nd + (d ^ 1)) for b in range(ng) for d in range(nd)]
    return lax.ppermute(value, ("band", "dom"), pairs)


def swap_all(pieces, direct):
    if direct:
        got = {0: pieces[0]}
        for j in range(1, len(pieces)):
            got[j] = xor_permute(pieces[j], "dom", j)
        return [got[j] for j in range(len(pieces))]
    stacked = lax.all_to_all(jnp.stack(pieces), "dom", 0, 0, tiled=True)
    return [stacked[j] for j in range(len(pieces))]


def packed_atoms(potential, proj_weights, atom_cell, point_codes):
    cube = 2 * REACH + 1
    off_x = point_codes // (cube * cube)
    off_y = point_codes // cube % cube
    off_z = point_codes % cube
    plane = atom_cell[:, 0:1] % SLAB + off_x
    cell_y = (atom_cell[:, 1:2] + off_y - REACH) % SIDE
    cell_z = (atom_cell[:, 2:3] + off_z - REACH) % SIDE
    lateral = cell_y * SIDE + cell_z
    return jnp.concatenate(
        [
            proj_weights.reshape(-1, 256),
            plane.astype(F32),
            lateral.astype(F32),
            jnp.zeros((4, 256), F32),
            potential.reshape(SLAB, LAT),
        ],
        axis=0,
    )


def on_device(trial_waves, potential, proj_weights, kb_energy, atom_cell, point_codes):
    nd = lax.axis_size("dom")
    bands = trial_waves.shape[-1]
    direct = nd == 8
    real = bands // nd
    nb = max(real, 8)
    total = nd * SLAB * LAT
    dom = lax.axis_index("dom") if direct else jnp.int32(0)
    band = lax.axis_index("band")
    pos = jnp.stack([dom, band if direct else jnp.int32(0), band // 2 if direct else jnp.int32(0)]).astype(jnp.int32)
    pos_band = jnp.stack([dom, band, band // 2]).astype(jnp.int32)
    R = SLAB * nb

    waves = trial_waves.reshape(SLAB, LAT, bands)
    packed = packed_atoms(potential, proj_weights, atom_cell, point_codes)
    if direct:
        cut = call(
            functools.partial(split_kernel, nd, nb),
            [shape(R + 32, LAT)] * nd,
            [waves, packed],
            [pltpu.VMEM((SLAB, bands, LAT), F32)],
            "split",
        )
    else:
        gathered = lax.all_gather(packed, "dom", axis=0)
        turned = waves.transpose(0, 2, 1).reshape(SLAB, nd, real, LAT).transpose(1, 0, 2, 3)
        cut = [turned[j] for j in range(nd)]

    lh, ll = split_const(lateral_matrix())
    fold = jnp.asarray(fold_matrix()).astype(BF16)
    kb_row = jnp.concatenate([kb_energy, kb_energy, jnp.zeros((112,), F32)])[None]
    pieces = swap_all(cut, direct)
    if not direct:
        pieces = [
            jnp.concatenate([jnp.pad(p, ((0, 0), (0, nb - real), (0, 0))).reshape(R, LAT), gathered[j]])
            for j, p in enumerate(pieces)
        ]
    ready = call(
        functools.partial(filter_kernel, nd, nb, float(total)),
        [shape(R // 2, LAT)] * (2 * nd),
        [pos, kb_row, lh, ll, fold] + [pieces[j] for j in arrival_order(nd)],
        [
            pltpu.VMEM(((nd * SLAB + 2 * HALO) * nb, LAT), F32),
            pltpu.VMEM(((nd * SLAB + 2 * HALO) * nb, LAT), F32),
            pltpu.VMEM((nd * nb, 256), F32),
            pltpu.VMEM((nd * nb, 256), F32),
            pltpu.VMEM((nd * 256, 256), BF16),
            pltpu.VMEM((nd * 256, 256), BF16),
            pltpu.VMEM((nd * SLAB, LAT), F32),
            pltpu.VMEM((nd, 32, 256), F32),
            pltpu.VMEM((nd * R, LAT), BF16),
            pltpu.VMEM((nd * R, LAT), BF16),
            pltpu.VMEM((nd * R, LAT), F32),
        ],
        "filter",
    )
    if direct:
        filtered, correlation = finish_direct(swap_all(ready[:nd], True), swap_all(ready[nd:], True), pos, bands, float(total))
    else:
        ready = [
            jnp.concatenate([ready[nd + j], ready[j]]).reshape(SLAB, nb, LAT)[:, :real] for j in range(nd)
        ]
        back = swap_all(ready, False)
        filtered, correlation = finish_plain(jnp.concatenate(back, axis=1), pos_band, band, bands, float(total))
    return filtered.reshape(trial_waves.shape), correlation


def finish_direct(first, second, pos, bands, total):
    nd, half = len(first), SLAB // 2
    nb = bands // nd

    def join(pieces, outs, ties):
        return call(
            functools.partial(join_kernel, nd, nb, len(outs) + 1),
            [shape(half, bands, LAT)] + outs,
            [pos] + pieces,
            (),
            "join",
            ties,
        )

    za, *sends = join(first, [shape(half // PARTS, bands, LAT)] * PARTS, [])
    far = [xor_permute(p, "band", 2) for p in sends]
    core_a = xor_permute(za, "band", 1)
    (zb,) = join(second, [], far)
    core_b = xor_permute(zb, "band", 1)
    far_core = [xor_permute(p, "band", 1) for p in far]
    part, share = shape(4, bands // 2, bands), shape(2, bands // 2, bands)
    keep, send, back, back_send = call(
        functools.partial(blocks_kernel, PARTS),
        [part, part, share, share],
        [pos, za, zb, core_a, core_b] + far + far_core,
        [pltpu.VMEM((4, bands, bands), F32), pltpu.VMEM((2, bands, bands), F32)],
        "blocks",
    )
    piece = shape(4, bands // 4, bands)
    keep, send = call(
        sum_kernel,
        [piece, piece],
        [pos, keep, xor_permute(send, "dom", 1), xor_permute(back, "band", 2), both_permute(back_send)],
        [pltpu.VMEM((4, bands // 2, bands), F32)],
        "sum",
    )
    mine = keep + xor_permute(send, "dom", 2)
    rows = call(
        functools.partial(pair_kernel, total), piece, [pos, mine, xor_permute(mine, "dom", 4)], (), "pair"
    )
    filtered = call(output_kernel, shape(SLAB, LAT, bands), [pos, za, zb], (), "output")
    correlation = call(
        place_kernel,
        shape(bands, 4 * bands),
        [pos, rows] + [xor_permute(rows, "dom", step) for step in (1, 2, 3)],
        (),
        "place",
    )
    return filtered, correlation


def finish_plain(z, pos, band, bands, total):
    send = lax.dynamic_slice_in_dim(z, (1 - band // 2) * (SLAB // 2), SLAB // 2, 0)
    far = xor_permute(send, "band", 2)
    gram, gram_far = call(
        gram_kernel,
        [shape(4, bands, bands), shape(2, bands, bands)],
        [pos, z, xor_permute(z, "band", 1), far, xor_permute(far, "band", 1)],
        (),
        "gram",
    )
    filtered = z.transpose(0, 2, 1)
    start = (1 - band // 2) * 2
    cross = lax.dynamic_slice_in_dim(gram, start, 2, 0) + xor_permute(gram_far, "band", 2)
    gram = lax.dynamic_update_slice_in_dim(gram, cross, start, 0)
    wide = gram.transpose(1, 0, 2).reshape(bands, 4 * bands)
    return filtered, lax.psum(wide, "dom") / total


def solution(mesh):
    return jax.shard_map(
        on_device,
        mesh=mesh,
        in_specs=(
            P("dom", None, None, "band"),
            P("dom", None, None),
            P("dom", None, None),
            P(),
            P("dom", None),
            P("dom", None),
        ),
        out_specs=(P("dom", None, None, "band"), P("band", None)),
        check_vma=False,
    )
```

```python
import functools

import jax
import jax.numpy as jnp
import numpy as np
from jax import lax
from jax.experimental import pallas as pl
from jax.experimental.pallas import tpu as pltpu
from jax.sharding import PartitionSpec as P

HALO = 6
REACH = 4
SLAB = 8
PARTS = 4
SIDE = 16
LAT = SIDE * SIDE

COEFFS = (
    -5369.0 / 1800.0,
    12.0 / 7.0,
    -15.0 / 56.0,
    10.0 / 189.0,
    -1.0 / 112.0,
    2.0 / 1925.0,
    -1.0 / 16632.0,
)
FILTER_LOWER = 5.0
FILTER_UPPER = 24.0
SPECTRUM_BOTTOM = 0.0
EPSILON = 1e-06

HALF_WIDTH = (FILTER_UPPER - FILTER_LOWER) / 2.0
CENTRE = (FILTER_UPPER + FILTER_LOWER) / 2.0
SIGMA_1 = HALF_WIDTH / (SPECTRUM_BOTTOM - CENTRE)
SIGMA_2 = 1.0 / (2.0 / SIGMA_1 - SIGMA_1)

VMEM_LIMIT = 48 * 1024 * 1024
BF16 = jnp.bfloat16
F32 = jnp.float32
NN = (((1,), (0,)), ((), ()))
NT = (((1,), (1,)), ((), ()))


def dot(a, b, dims=NN):
    return lax.dot_general(a, b, dims, preferred_element_type=F32)


def halves(x):
    hi = x.astype(BF16)
    return hi, (x - hi.astype(F32)).astype(BF16)


def dot3(ah, al, bh, bl, dims=NN):
    rows = ah.shape[0]
    both = dot(jnp.concatenate([ah, al], axis=0), bh, dims)
    return both[:rows] + both[rows:] + dot(ah, bl, dims)


def lateral_matrix():
    line = np.zeros((SIDE, SIDE))
    at = np.arange(SIDE)
    for k in range(1, HALO + 1):
        for sign in (1, -1):
            np.add.at(line, ((at + sign * k) % SIDE, at), -0.5 * COEFFS[k])
    eye = np.eye(SIDE)
    return np.kron(line, eye) + np.kron(eye, line)


def relation():
    return [[-1, 0] if q < REACH else [0, 1] for q in range(SLAB)]


def fold_matrix():
    out = np.zeros((256, 384), np.float32)
    for q, pair in enumerate(relation()):
        for half, rel in enumerate(pair):
            for r in range(16):
                out[q * 32 + half * 16 + r, (rel + 1) * 128 + r] = 1.0
    return out


def split_const(matrix):
    matrix = np.asarray(matrix, np.float32)
    hi = jnp.asarray(matrix, F32).astype(BF16)
    lo = (jnp.asarray(matrix, F32) - hi.astype(F32)).astype(BF16)
    return hi, lo


def split_kernel(nd, nb, x_ref, packed_ref, *refs):
    outs, scratch = refs[:-1], refs[-1]
    i = lax.axis_index("dom")
    for q in range(SLAB):
        scratch[q] = x_ref[q].T
    for j in range(nd):
        start = (i ^ j) * nb
        for q in range(SLAB):
            outs[j][q * nb : (q + 1) * nb] = scratch[q, pl.ds(pl.multiple_of(start, nb), nb)]
        outs[j][SLAB * nb :] = packed_ref[...]


def build_projectors(nd, scratch, wh_ref, wl_ref, v_ref):
    lat = lax.broadcasted_iota(jnp.int32, (LAT, 256), 0).astype(F32)
    plane = lax.broadcasted_iota(jnp.int32, (16, 1, 1), 0).astype(F32)
    diagonal = -1.5 * COEFFS[0] - CENTRE

    def body(s, carry):
        his, los = [], []
        for a in range(2):
            w = scratch[s, a * 8 : a * 8 + 8]
            px = scratch[s, 16 + a : 17 + a]
            place = scratch[s, 18 + a : 19 + a]
            hot = jnp.where(lat == place, 1.0, 0.0).astype(BF16)
            masked = jnp.where(px[None] == plane, w[None], 0.0).reshape(128, 256)
            mh, ml = halves(masked)
            his.append(dot(mh, hot, NT).reshape(16, 8, LAT))
            los.append(dot(ml, hot, NT).reshape(16, 8, LAT))
        hi = jnp.concatenate(his, axis=1).astype(BF16)
        lo = jnp.concatenate(los, axis=1).astype(BF16)
        for t in range(16):
            p = (s * SLAB - REACH + t + nd * SLAB) % (nd * SLAB) if isinstance(s, int) else lax.rem(
                s * SLAB - REACH + t + nd * SLAB, nd * SLAB
            )
            row = pl.ds(pl.multiple_of(p * 32 + (16 if t < SLAB else 0), 16), 16)
            wh_ref[row] = hi[t]
            wl_ref[row] = lo[t]
        v_ref[pl.ds(pl.multiple_of(s * SLAB, SLAB), SLAB)] = scratch[s, 24:32] + diagonal
        return carry

    if nd <= 8:
        for s in range(nd):
            body(s, 0)
    else:
        lax.fori_loop(0, nd, body, 0)


def arrival_order(nd):
    return [1, 2, *range(nd // 2, nd), *range(3, nd // 2), 0]


def filter_kernel(nd, nb, total, pos_ref, kb_ref, lh_ref, ll_ref, fold_ref, *refs):
    pieces, outs = refs[:nd], refs[nd : 3 * nd]
    f0_ref, f1_ref, fold_out, spread_out, wh_ref, wl_ref, v_ref, packed, fh_ref, fl_ref, acc_ref = refs[3 * nd :]
    i = pos_ref[0]
    R = SLAB * nb
    rows_q = lax.broadcasted_iota(jnp.int32, (SLAB, nb, 256), 0)
    lanes_q = lax.broadcasted_iota(jnp.int32, (SLAB, nb, 256), 2) // 32
    same = rows_q == lanes_q

    def slab_rows(s, k=0):
        return pl.ds(pl.multiple_of((s * SLAB + HALO + k) * nb, nb), R)

    def wrap(ref):
        ref[0 : HALO * nb] = ref[nd * R : nd * R + HALO * nb]
        ref[HALO * nb + nd * R : 2 * HALO * nb + nd * R] = ref[HALO * nb : 2 * HALO * nb]

    def each(body):
        if nd <= 8:
            for s in range(nd):
                body(s)
        else:
            lax.fori_loop(0, nd, lambda s, c: (body(s), c)[1], 0)

    for piece, j in zip(pieces, arrival_order(nd)):
        f0_ref[slab_rows(i ^ j)] = piece[:R]
        packed[i ^ j] = piece[R:]
    wrap(f0_ref)
    build_projectors(nd, packed, wh_ref, wl_ref, v_ref)

    def apply(ref, finish):
        def project(s):
            rows = pl.ds(pl.multiple_of(s * R, R), R)
            fh, fl = halves(ref[slab_rows(s)])
            fh_ref[rows] = fh
            fl_ref[rows] = fl
            w = pl.ds(pl.multiple_of(s * 256, 256), 256)
            g = dot3(fh, fl, wh_ref[w], wl_ref[w], NT).reshape(SLAB, nb, 256)
            fold_out[pl.ds(pl.multiple_of(s * nb, nb), nb)] = jnp.sum(jnp.where(same, g, 0.0), axis=0)

        def lateral(s):
            rows = pl.ds(pl.multiple_of(s * 4 * R, 4 * R), 4 * R)
            acc_ref[rows] = dot3(fh_ref[rows], fl_ref[rows], lh_ref[...], ll_ref[...])

        each(project)
        if nd <= 8:
            for s in range(nd // 4):
                lateral(s)
        else:
            lax.fori_loop(0, nd // 4, lambda s, c: (lateral(s), c)[1], 0)
        gh, gl = halves(fold_out[...])
        h = dot(gh, fold_ref[...]) + dot(gl, fold_ref[...])
        below, at, above = h[:, :128], h[:, 128:256], h[:, 256:]

        def next_slab(x):
            return jnp.concatenate([x[-nb:], x[:-nb]], axis=0)

        def previous_slab(x):
            return jnp.concatenate([x[nb:], x[:nb]], axis=0)

        p = (at + next_slab(above) + previous_slab(below)) * kb_ref[...]
        wide = jnp.concatenate([next_slab(p), p, previous_slab(p)], axis=1)
        ph, plo = halves(wide)
        spread_out[...] = dot(ph, fold_ref[...], NT) + dot(plo, fold_ref[...], NT)

        def step(s):
            f = ref[slab_rows(s)]
            x = jnp.where(same, spread_out[pl.ds(pl.multiple_of(s * nb, nb), nb)][None], 0.0).reshape(R, 256)
            xh, xl = halves(x)
            w = pl.ds(pl.multiple_of(s * 256, 256), 256)
            acc = dot3(xh, xl, wh_ref[w], wl_ref[w]) + acc_ref[pl.ds(pl.multiple_of(s * R, R), R)]
            v = v_ref[pl.ds(pl.multiple_of(s * SLAB, SLAB), SLAB)]
            acc = acc + (f.reshape(SLAB, nb, LAT) * v[:, None, :]).reshape(R, LAT)
            for k in range(1, HALO + 1):
                acc = acc + (-0.5 * COEFFS[k]) * (ref[slab_rows(s, k)] + ref[slab_rows(s, -k)])
            finish(s, acc)

        each(step)

    def first(s, acc):
        f1_ref[slab_rows(s)] = (SIGMA_1 / HALF_WIDTH) * acc

    apply(f0_ref, first)
    wrap(f1_ref)

    def second(s, acc):
        f0_ref_new = (2.0 * SIGMA_2 / HALF_WIDTH) * acc - (SIGMA_1 * SIGMA_2) * f0_ref[slab_rows(s)]
        y2_store(s, f0_ref_new)

    def y2_store(s, value):
        f0_ref[slab_rows(s)] = value

    apply(f1_ref, second)
    square = jnp.zeros((nb, LAT), F32)
    if nd <= 8:
        for s in range(nd):
            y = f0_ref[slab_rows(s)].reshape(SLAB, nb, LAT)
            square = square + jnp.sum(y * y, axis=0)
    else:

        def add(s, total_square):
            y = f0_ref[slab_rows(s)].reshape(SLAB, nb, LAT)
            return total_square + jnp.sum(y * y, axis=0)

        square = lax.fori_loop(0, nd, add, square)
    scale = 1.0 / jnp.sqrt(jnp.sum(square, axis=1, keepdims=True) / total + EPSILON)
    chip, half = pos_ref[2], SLAB // 2
    for j in range(nd):
        for h, out in ((1 - chip, outs[j]), (chip, outs[nd + j])):
            start = ((i ^ j) * SLAB + HALO + h * half) * nb
            y = f0_ref[pl.ds(pl.multiple_of(start, nb), half * nb)].reshape(half, nb, LAT)
            out[...] = (y * scale[None]).reshape(half * nb, LAT)


def join_kernel(order, nb, outs, pos_ref, *refs):
    pieces, (z_ref, *parts) = refs[: len(order)], refs[-outs:]
    i = pos_ref[0]
    for piece, j in zip(pieces, order):
        rows = pl.ds(pl.multiple_of((i ^ j) * nb, nb), nb)
        for q in range(SLAB // 2):
            z_ref[q, rows] = piece[q * nb : (q + 1) * nb]
    for k, part in enumerate(parts):
        part[...] = z_ref[k * part.shape[0] : (k + 1) * part.shape[0]]


def blocks_kernel(parts, pos_ref, za, zb, ca, cb, *refs):
    far, far_core = refs[:parts], refs[parts : 2 * parts]
    keep, send, back, back_send, g_ref, back_ref = refs[2 * parts :]
    i, c = pos_ref[0], pos_ref[1] & 1
    per = SLAB // 2 // parts
    totals = None
    for q in range(SLAB // 2):
        zh, zl = halves(zb[q])
        ch, cl = halves(cb[q])
        fh, fl = halves(far[q // per][q % per])
        gh, gl = halves(far_core[q // per][q % per])
        wh, wl = halves(za[q])
        xh, xl = halves(ca[q])
        now = (
            dot3(zh, zl, zh, zl, NT) + dot3(wh, wl, wh, wl, NT),
            dot3(zh, zl, ch, cl, NT) + dot3(wh, wl, xh, xl, NT),
            dot3(zh, zl, fh, fl, NT),
            dot3(zh, zl, gh, gl, NT),
            dot3(fh, fl, zh, zl, NT),
            dot3(fh, fl, ch, cl, NT),
        )
        totals = now if totals is None else tuple(t + n for t, n in zip(totals, now))
    g_ref[c], g_ref[c ^ 1], g_ref[2 + c], g_ref[2 + (c ^ 1)], back_ref[c], back_ref[c ^ 1] = totals
    cut_rows(i & 1, g_ref, keep, send)
    cut_rows(i & 1, back_ref, back, back_send)


def cut_rows(bit, g_ref, keep_ref, send_ref):
    size = keep_ref.shape[1]
    keep_ref[...] = g_ref[:, pl.ds(pl.multiple_of(bit * size, size), size)]
    send_ref[...] = g_ref[:, pl.ds(pl.multiple_of((1 - bit) * size, size), size)]


def sum_kernel(pos_ref, keep, other, back, back_other, keep_ref, send_ref, sum_ref):
    sum_ref[0:2] = keep[0:2] + other[0:2]
    sum_ref[2:4] = (keep[2:4] + other[2:4]) + (back[...] + back_other[...])
    cut_rows((pos_ref[0] >> 1) & 1, sum_ref, keep_ref, send_ref)


def pair_kernel(total, pos_ref, mine, other, out_ref):
    y = pos_ref[2]
    for c in range(2):
        out_ref[y * 2 + c] = (mine[c] + other[c]) * (1.0 / total)
        out_ref[(1 - y) * 2 + c] = (mine[2 + c] + other[2 + c]) * (1.0 / total)


def output_kernel(pos_ref, za, zb, out_ref):
    y, half = pos_ref[2], SLAB // 2
    for q in range(half):
        out_ref[(1 - y) * half + q] = za[q].T
        out_ref[y * half + q] = zb[q].T


def place_kernel(pos_ref, *refs):
    pieces, out_ref = refs[:-1], refs[-1]
    size = pieces[0].shape[1]
    for j, piece in enumerate(pieces):
        source = pos_ref[0] ^ j
        start = (source & 1) * (2 * size) + ((source >> 1) & 1) * size
        for k in range(4):
            out_ref[pl.ds(pl.multiple_of(start, size), size), k * 128 : (k + 1) * 128] = piece[k]


def gram_kernel(pos_ref, own, core, far, far_core, g_ref, far_ref):
    b, y = pos_ref[1], pos_ref[2]
    half = SLAB // 2

    def add(totals, place, value):
        totals[place] = value if totals.get(place) is None else totals[place] + value

    totals = {}
    for q in range(half):
        for mine in (True, False):
            at = q + y * half if mine else q + (1 - y) * half
            zh, zl = halves(own[at])
            ch, cl = halves(core[at])
            add(totals, "own", dot3(zh, zl, zh, zl, NT))
            add(totals, "core", dot3(zh, zl, ch, cl, NT))
            if mine:
                fh, fl = halves(far[q])
                gh, gl = halves(far_core[q])
                add(totals, "far", dot3(zh, zl, fh, fl, NT))
                add(totals, "far_core", dot3(zh, zl, gh, gl, NT))
                add(totals, "back", dot3(fh, fl, zh, zl, NT))
                add(totals, "back_core", dot3(fh, fl, ch, cl, NT))
    g_ref[b] = totals["own"]
    g_ref[b ^ 1] = totals["core"]
    g_ref[b ^ 2] = totals["far"]
    g_ref[b ^ 3] = totals["far_core"]
    far_ref[b & 1] = totals["back"]
    far_ref[(b & 1) ^ 1] = totals["back_core"]


def call(kernel, out_shape, operands, scratch=(), name=None, ties=()):
    specs = [
        pl.BlockSpec(memory_space=pltpu.SMEM if o.dtype == jnp.int32 and o.size < 128 else pltpu.VMEM) for o in operands
    ] + [pl.BlockSpec(memory_space=pl.ANY) for _ in ties]
    single = not isinstance(out_shape, (list, tuple))
    return pl.pallas_call(
        kernel,
        out_shape=out_shape,
        in_specs=specs,
        out_specs=(
            pl.BlockSpec(memory_space=pltpu.VMEM)
            if single
            else [pl.BlockSpec(memory_space=pltpu.VMEM) for _ in out_shape]
        ),
        scratch_shapes=list(scratch),
        compiler_params=pltpu.CompilerParams(vmem_limit_bytes=VMEM_LIMIT),
        name=name,
    )(*operands, *ties)


def shape(*dims, dtype=F32):
    return jax.ShapeDtypeStruct(dims, dtype)


def xor_permute(value, axis, step):
    count = lax.axis_size(axis)
    return lax.ppermute(value, axis, [(k, k ^ step) for k in range(count)])


def both_permute(value):
    nd, ng = lax.axis_size("dom"), lax.axis_size("band")
    pairs = [(b * nd + d, (b ^ 2) * nd + (d ^ 1)) for b in range(ng) for d in range(nd)]
    return lax.ppermute(value, ("band", "dom"), pairs)


def swap_all(pieces, direct):
    if direct:
        got = {0: pieces[0]}
        for j in range(1, len(pieces)):
            got[j] = xor_permute(pieces[j], "dom", j)
        return [got[j] for j in range(len(pieces))]
    stacked = lax.all_to_all(jnp.stack(pieces), "dom", 0, 0, tiled=True)
    return [stacked[j] for j in range(len(pieces))]


def packed_atoms(potential, proj_weights, atom_cell, point_codes):
    cube = 2 * REACH + 1
    off_x = point_codes // (cube * cube)
    off_y = point_codes // cube % cube
    off_z = point_codes % cube
    plane = atom_cell[:, 0:1] % SLAB + off_x
    cell_y = (atom_cell[:, 1:2] + off_y - REACH) % SIDE
    cell_z = (atom_cell[:, 2:3] + off_z - REACH) % SIDE
    lateral = cell_y * SIDE + cell_z
    return jnp.concatenate(
        [
            proj_weights.reshape(-1, 256),
            plane.astype(F32),
            lateral.astype(F32),
            jnp.zeros((4, 256), F32),
            potential.reshape(SLAB, LAT),
        ],
        axis=0,
    )


def on_device(trial_waves, potential, proj_weights, kb_energy, atom_cell, point_codes):
    nd = lax.axis_size("dom")
    bands = trial_waves.shape[-1]
    direct = nd == 8
    real = bands // nd
    nb = max(real, 8)
    total = nd * SLAB * LAT
    dom = lax.axis_index("dom") if direct else jnp.int32(0)
    band = lax.axis_index("band")
    pos = jnp.stack([dom, band if direct else jnp.int32(0), band // 2 if direct else jnp.int32(0)]).astype(jnp.int32)
    pos_band = jnp.stack([dom, band, band // 2]).astype(jnp.int32)
    R = SLAB * nb

    waves = trial_waves.reshape(SLAB, LAT, bands)
    packed = packed_atoms(potential, proj_weights, atom_cell, point_codes)
    if direct:
        cut = call(
            functools.partial(split_kernel, nd, nb),
            [shape(R + 32, LAT)] * nd,
            [waves, packed],
            [pltpu.VMEM((SLAB, bands, LAT), F32)],
            "split",
        )
    else:
        gathered = lax.all_gather(packed, "dom", axis=0)
        turned = waves.transpose(0, 2, 1).reshape(SLAB, nd, real, LAT).transpose(1, 0, 2, 3)
        cut = [turned[j] for j in range(nd)]

    lh, ll = split_const(lateral_matrix())
    fold = jnp.asarray(fold_matrix()).astype(BF16)
    kb_row = jnp.concatenate([kb_energy, kb_energy, jnp.zeros((112,), F32)])[None]
    pieces = swap_all(cut, direct)
    if not direct:
        pieces = [
            jnp.concatenate([jnp.pad(p, ((0, 0), (0, nb - real), (0, 0))).reshape(R, LAT), gathered[j]])
            for j, p in enumerate(pieces)
        ]
    ready = call(
        functools.partial(filter_kernel, nd, nb, float(total)),
        [shape(R // 2, LAT)] * (2 * nd),
        [pos, kb_row, lh, ll, fold] + [pieces[j] for j in arrival_order(nd)],
        [
            pltpu.VMEM(((nd * SLAB + 2 * HALO) * nb, LAT), F32),
            pltpu.VMEM(((nd * SLAB + 2 * HALO) * nb, LAT), F32),
            pltpu.VMEM((nd * nb, 256), F32),
            pltpu.VMEM((nd * nb, 256), F32),
            pltpu.VMEM((nd * 256, 256), BF16),
            pltpu.VMEM((nd * 256, 256), BF16),
            pltpu.VMEM((nd * SLAB, LAT), F32),
            pltpu.VMEM((nd, 32, 256), F32),
            pltpu.VMEM((nd * R, LAT), BF16),
            pltpu.VMEM((nd * R, LAT), BF16),
            pltpu.VMEM((nd * R, LAT), F32),
        ],
        "filter",
    )
    if direct:
        filtered, correlation = finish_direct(swap_all(ready[:nd], True), swap_all(ready[nd:], True), pos, bands, float(total))
    else:
        ready = [
            jnp.concatenate([ready[nd + j], ready[j]]).reshape(SLAB, nb, LAT)[:, :real] for j in range(nd)
        ]
        back = swap_all(ready, False)
        filtered, correlation = finish_plain(jnp.concatenate(back, axis=1), pos_band, band, bands, float(total))
    return filtered.reshape(trial_waves.shape), correlation


def finish_direct(first, second, pos, bands, total):
    nd, half = len(first), SLAB // 2
    nb = bands // nd

    def join(pieces, order, outs, ties):
        return call(
            functools.partial(join_kernel, order, nb, len(outs) + 1),
            [shape(half, bands, LAT)] + outs,
            [pos] + [pieces[j] for j in order],
            (),
            "join",
            ties,
        )

    za, *sends = join(first, (0, 1, 2, 4, 5, 6, 7, 3), [shape(half // PARTS, bands, LAT)] * PARTS, [])
    far = [xor_permute(p, "band", 2) for p in sends]
    core_a = xor_permute(za, "band", 1)
    (zb,) = join(second, range(nd), [], far)
    core_b = xor_permute(zb, "band", 1)
    far_core = [xor_permute(p, "band", 1) for p in far]
    part, share = shape(4, bands // 2, bands), shape(2, bands // 2, bands)
    keep, send, back, back_send = call(
        functools.partial(blocks_kernel, PARTS),
        [part, part, share, share],
        [pos, za, zb, core_a, core_b] + far + far_core,
        [pltpu.VMEM((4, bands, bands), F32), pltpu.VMEM((2, bands, bands), F32)],
        "blocks",
    )
    piece = shape(4, bands // 4, bands)
    keep, send = call(
        sum_kernel,
        [piece, piece],
        [pos, keep, xor_permute(send, "dom", 1), xor_permute(back, "band", 2), both_permute(back_send)],
        [pltpu.VMEM((4, bands // 2, bands), F32)],
        "sum",
    )
    mine = keep + xor_permute(send, "dom", 2)
    rows = call(
        functools.partial(pair_kernel, total), piece, [pos, mine, xor_permute(mine, "dom", 4)], (), "pair"
    )
    filtered = call(output_kernel, shape(SLAB, LAT, bands), [pos, za, zb], (), "output")
    correlation = call(
        place_kernel,
        shape(bands, 4 * bands),
        [pos, rows] + [xor_permute(rows, "dom", step) for step in (1, 2, 3)],
        (),
        "place",
    )
    return filtered, correlation


def finish_plain(z, pos, band, bands, total):
    send = lax.dynamic_slice_in_dim(z, (1 - band // 2) * (SLAB // 2), SLAB // 2, 0)
    far = xor_permute(send, "band", 2)
    gram, gram_far = call(
        gram_kernel,
        [shape(4, bands, bands), shape(2, bands, bands)],
        [pos, z, xor_permute(z, "band", 1), far, xor_permute(far, "band", 1)],
        (),
        "gram",
    )
    filtered = z.transpose(0, 2, 1)
    start = (1 - band // 2) * 2
    cross = lax.dynamic_slice_in_dim(gram, start, 2, 0) + xor_permute(gram_far, "band", 2)
    gram = lax.dynamic_update_slice_in_dim(gram, cross, start, 0)
    wide = gram.transpose(1, 0, 2).reshape(bands, 4 * bands)
    return filtered, lax.psum(wide, "dom") / total


def solution(mesh):
    return jax.shard_map(
        on_device,
        mesh=mesh,
        in_specs=(
            P("dom", None, None, "band"),
            P("dom", None, None),
            P("dom", None, None),
            P(),
            P("dom", None),
            P("dom", None),
        ),
        out_specs=(P("dom", None, None, "band"), P("band", None)),
        check_vma=False,
    )
```

```python
import functools

import jax
import jax.numpy as jnp
import numpy as np
from jax import lax
from jax.experimental import pallas as pl
from jax.experimental.pallas import tpu as pltpu
from jax.sharding import PartitionSpec as P

HALO = 6
REACH = 4
SLAB = 8
PARTS = 4
SIDE = 16
LAT = SIDE * SIDE

COEFFS = (
    -5369.0 / 1800.0,
    12.0 / 7.0,
    -15.0 / 56.0,
    10.0 / 189.0,
    -1.0 / 112.0,
    2.0 / 1925.0,
    -1.0 / 16632.0,
)
FILTER_LOWER = 5.0
FILTER_UPPER = 24.0
SPECTRUM_BOTTOM = 0.0
EPSILON = 1e-06

HALF_WIDTH = (FILTER_UPPER - FILTER_LOWER) / 2.0
CENTRE = (FILTER_UPPER + FILTER_LOWER) / 2.0
SIGMA_1 = HALF_WIDTH / (SPECTRUM_BOTTOM - CENTRE)
SIGMA_2 = 1.0 / (2.0 / SIGMA_1 - SIGMA_1)

VMEM_LIMIT = 48 * 1024 * 1024
BF16 = jnp.bfloat16
F32 = jnp.float32
NN = (((1,), (0,)), ((), ()))
NT = (((1,), (1,)), ((), ()))


def dot(a, b, dims=NN):
    return lax.dot_general(a, b, dims, preferred_element_type=F32)


def halves(x):
    hi = x.astype(BF16)
    return hi, (x - hi.astype(F32)).astype(BF16)


def dot3(ah, al, bh, bl, dims=NN):
    rows = ah.shape[0]
    both = dot(jnp.concatenate([ah, al], axis=0), bh, dims)
    return both[:rows] + both[rows:] + dot(ah, bl, dims)


def lateral_matrix():
    line = np.zeros((SIDE, SIDE))
    at = np.arange(SIDE)
    for k in range(1, HALO + 1):
        for sign in (1, -1):
            np.add.at(line, ((at + sign * k) % SIDE, at), -0.5 * COEFFS[k])
    eye = np.eye(SIDE)
    return np.kron(line, eye) + np.kron(eye, line)


def relation():
    return [[-1, 0] if q < REACH else [0, 1] for q in range(SLAB)]


def fold_matrix():
    out = np.zeros((256, 384), np.float32)
    for q, pair in enumerate(relation()):
        for half, rel in enumerate(pair):
            for r in range(16):
                out[q * 32 + half * 16 + r, (rel + 1) * 128 + r] = 1.0
    return out


def split_const(matrix):
    matrix = np.asarray(matrix, np.float32)
    hi = jnp.asarray(matrix, F32).astype(BF16)
    lo = (jnp.asarray(matrix, F32) - hi.astype(F32)).astype(BF16)
    return hi, lo


def split_kernel(nd, nb, cell_ref, x_ref, v_ref, w_ref, code_ref, *refs):
    outs, (scratch, packed) = refs[:-2], refs[-2:]
    i = lax.axis_index("dom")
    cube = 2 * REACH + 1
    code = code_ref[...].astype(F32)
    off_x = jnp.floor((code + 0.5) * (1.0 / (cube * cube)))
    rest = code - off_x * (cube * cube)
    off_y = jnp.floor((rest + 0.5) * (1.0 / cube))
    off_z = rest - off_y * cube
    for a in range(2):
        packed[a * 8 : a * 8 + 8] = w_ref[a]
        cell_x, cell_y, cell_z = (
            lax.rem(cell_ref[a, k], n).astype(F32) for k, n in enumerate((SLAB, SIDE, SIDE))
        )
        y = off_y[a : a + 1] + (cell_y + float(SIDE - REACH))
        z = off_z[a : a + 1] + (cell_z + float(SIDE - REACH))
        y = y - SIDE * jnp.floor(y * (1.0 / SIDE))
        z = z - SIDE * jnp.floor(z * (1.0 / SIDE))
        packed[16 + a : 17 + a] = off_x[a : a + 1] + cell_x
        packed[18 + a : 19 + a] = y * SIDE + z
    packed[20:24] = jnp.zeros((4, LAT), F32)
    packed[24:32] = jnp.concatenate([v_ref[:, y, :] for y in range(SIDE)], axis=1)
    for q in range(SLAB):
        scratch[q] = x_ref[q].T
    for j in range(nd):
        start = (i ^ j) * nb
        for q in range(SLAB):
            outs[j][q * nb : (q + 1) * nb] = scratch[q, pl.ds(pl.multiple_of(start, nb), nb)]
        outs[j][SLAB * nb :] = packed[...]


def build_projectors(nd, scratch, wh_ref, wl_ref, v_ref):
    lat = lax.broadcasted_iota(jnp.int32, (LAT, 256), 0).astype(F32)
    plane = lax.broadcasted_iota(jnp.int32, (16, 1, 1), 0).astype(F32)
    diagonal = -1.5 * COEFFS[0] - CENTRE

    def body(s, carry):
        his, los = [], []
        for a in range(2):
            w = scratch[s, a * 8 : a * 8 + 8]
            px = scratch[s, 16 + a : 17 + a]
            place = scratch[s, 18 + a : 19 + a]
            hot = jnp.where(lat == place, 1.0, 0.0).astype(BF16)
            masked = jnp.where(px[None] == plane, w[None], 0.0).reshape(128, 256)
            mh, ml = halves(masked)
            both = dot(jnp.concatenate([mh, ml], axis=0), hot, NT).reshape(2, 16, 8, LAT)
            his.append(both[0])
            los.append(both[1])
        hi = jnp.concatenate(his, axis=1).astype(BF16)
        lo = jnp.concatenate(los, axis=1).astype(BF16)
        for t in range(16):
            p = (s * SLAB - REACH + t + nd * SLAB) % (nd * SLAB) if isinstance(s, int) else lax.rem(
                s * SLAB - REACH + t + nd * SLAB, nd * SLAB
            )
            row = pl.ds(pl.multiple_of(p * 32 + (16 if t < SLAB else 0), 16), 16)
            wh_ref[row] = hi[t]
            wl_ref[row] = lo[t]
        v_ref[pl.ds(pl.multiple_of(s * SLAB, SLAB), SLAB)] = scratch[s, 24:32] + diagonal
        return carry

    if nd <= 8:
        for s in range(nd):
            body(s, 0)
    else:
        lax.fori_loop(0, nd, body, 0)


def arrival_order(nd):
    return [1, 2, *range(nd // 2, nd), *range(3, nd // 2), 0]


def filter_kernel(nd, nb, total, pos_ref, kb_ref, lh_ref, ll_ref, fold_ref, *refs):
    pieces, outs = refs[:nd], refs[nd : 3 * nd]
    f0_ref, f1_ref, fold_out, spread_out, wh_ref, wl_ref, v_ref, packed, fh_ref, fl_ref, acc_ref = refs[3 * nd :]
    i = pos_ref[0]
    R = SLAB * nb
    rows_q = lax.broadcasted_iota(jnp.int32, (SLAB, nb, 256), 0)
    lanes_q = lax.broadcasted_iota(jnp.int32, (SLAB, nb, 256), 2) // 32
    same = rows_q == lanes_q

    def slab_rows(s, k=0):
        return pl.ds(pl.multiple_of((s * SLAB + HALO + k) * nb, nb), R)

    def wrap(ref):
        ref[0 : HALO * nb] = ref[nd * R : nd * R + HALO * nb]
        ref[HALO * nb + nd * R : 2 * HALO * nb + nd * R] = ref[HALO * nb : 2 * HALO * nb]

    def each(body):
        if nd <= 8:
            for s in range(nd):
                body(s)
        else:
            lax.fori_loop(0, nd, lambda s, c: (body(s), c)[1], 0)

    for piece, j in zip(pieces, arrival_order(nd)):
        f0_ref[slab_rows(i ^ j)] = piece[:R]
        packed[i ^ j] = piece[R:]
    wrap(f0_ref)
    build_projectors(nd, packed, wh_ref, wl_ref, v_ref)

    def apply(ref, finish):
        def project(s):
            rows = pl.ds(pl.multiple_of(s * R, R), R)
            fh, fl = halves(ref[slab_rows(s)])
            fh_ref[rows] = fh
            fl_ref[rows] = fl
            w = pl.ds(pl.multiple_of(s * 256, 256), 256)
            g = dot3(fh, fl, wh_ref[w], wl_ref[w], NT).reshape(SLAB, nb, 256)
            fold_out[pl.ds(pl.multiple_of(s * nb, nb), nb)] = jnp.sum(jnp.where(same, g, 0.0), axis=0)

        def lateral(s):
            rows = pl.ds(pl.multiple_of(s * 4 * R, 4 * R), 4 * R)
            acc_ref[rows] = dot3(fh_ref[rows], fl_ref[rows], lh_ref[...], ll_ref[...])

        each(project)
        if nd <= 8:
            for s in range(nd // 4):
                lateral(s)
        else:
            lax.fori_loop(0, nd // 4, lambda s, c: (lateral(s), c)[1], 0)
        gh, gl = halves(fold_out[...])
        h = dot(gh, fold_ref[...]) + dot(gl, fold_ref[...])
        below, at, above = h[:, :128], h[:, 128:256], h[:, 256:]

        def next_slab(x):
            return jnp.concatenate([x[-nb:], x[:-nb]], axis=0)

        def previous_slab(x):
            return jnp.concatenate([x[nb:], x[:nb]], axis=0)

        p = (at + next_slab(above) + previous_slab(below)) * kb_ref[...]
        wide = jnp.concatenate([next_slab(p), p, previous_slab(p)], axis=1)
        ph, plo = halves(wide)
        spread_out[...] = dot(ph, fold_ref[...], NT) + dot(plo, fold_ref[...], NT)

        def step(s):
            f = ref[slab_rows(s)]
            x = jnp.where(same, spread_out[pl.ds(pl.multiple_of(s * nb, nb), nb)][None], 0.0).reshape(R, 256)
            xh, xl = halves(x)
            w = pl.ds(pl.multiple_of(s * 256, 256), 256)
            acc = dot3(xh, xl, wh_ref[w], wl_ref[w]) + acc_ref[pl.ds(pl.multiple_of(s * R, R), R)]
            v = v_ref[pl.ds(pl.multiple_of(s * SLAB, SLAB), SLAB)]
            acc = acc + (f.reshape(SLAB, nb, LAT) * v[:, None, :]).reshape(R, LAT)
            for k in range(1, HALO + 1):
                acc = acc + (-0.5 * COEFFS[k]) * (ref[slab_rows(s, k)] + ref[slab_rows(s, -k)])
            finish(s, acc)

        each(step)

    def first(s, acc):
        f1_ref[slab_rows(s)] = (SIGMA_1 / HALF_WIDTH) * acc

    apply(f0_ref, first)
    wrap(f1_ref)

    def second(s, acc):
        f0_ref_new = (2.0 * SIGMA_2 / HALF_WIDTH) * acc - (SIGMA_1 * SIGMA_2) * f0_ref[slab_rows(s)]
        y2_store(s, f0_ref_new)

    def y2_store(s, value):
        f0_ref[slab_rows(s)] = value

    apply(f1_ref, second)
    square = jnp.zeros((nb, LAT), F32)
    if nd <= 8:
        for s in range(nd):
            y = f0_ref[slab_rows(s)].reshape(SLAB, nb, LAT)
            square = square + jnp.sum(y * y, axis=0)
    else:

        def add(s, total_square):
            y = f0_ref[slab_rows(s)].reshape(SLAB, nb, LAT)
            return total_square + jnp.sum(y * y, axis=0)

        square = lax.fori_loop(0, nd, add, square)
    scale = 1.0 / jnp.sqrt(jnp.sum(square, axis=1, keepdims=True) / total + EPSILON)
    chip, half = pos_ref[2], SLAB // 2
    for j in range(nd):
        for h, out in ((1 - chip, outs[j]), (chip, outs[nd + j])):
            start = ((i ^ j) * SLAB + HALO + h * half) * nb
            y = f0_ref[pl.ds(pl.multiple_of(start, nb), half * nb)].reshape(half, nb, LAT)
            out[...] = (y * scale[None]).reshape(half * nb, LAT)


def join_kernel(order, nb, outs, pos_ref, *refs):
    pieces, (z_ref, *parts) = refs[: len(order)], refs[-outs:]
    i = pos_ref[0]
    for piece, j in zip(pieces, order):
        rows = pl.ds(pl.multiple_of((i ^ j) * nb, nb), nb)
        for q in range(SLAB // 2):
            z_ref[q, rows] = piece[q * nb : (q + 1) * nb]
    for k, part in enumerate(parts):
        part[...] = z_ref[k * part.shape[0] : (k + 1) * part.shape[0]]


def blocks_kernel(parts, pos_ref, za, zb, ca, cb, *refs):
    far, far_core = refs[:parts], refs[parts : 2 * parts]
    keep, send, back, back_send, g_ref, back_ref = refs[2 * parts :]
    i, c = pos_ref[0], pos_ref[1] & 1
    per = SLAB // 2 // parts
    totals = None
    for q in range(SLAB // 2):
        zh, zl = halves(zb[q])
        ch, cl = halves(cb[q])
        fh, fl = halves(far[q // per][q % per])
        gh, gl = halves(far_core[q // per][q % per])
        wh, wl = halves(za[q])
        xh, xl = halves(ca[q])
        now = (
            dot3(zh, zl, zh, zl, NT) + dot3(wh, wl, wh, wl, NT),
            dot3(zh, zl, ch, cl, NT) + dot3(wh, wl, xh, xl, NT),
            dot3(zh, zl, fh, fl, NT),
            dot3(zh, zl, gh, gl, NT),
            dot3(fh, fl, zh, zl, NT),
            dot3(fh, fl, ch, cl, NT),
        )
        totals = now if totals is None else tuple(t + n for t, n in zip(totals, now))
    g_ref[c], g_ref[c ^ 1], g_ref[2 + c], g_ref[2 + (c ^ 1)], back_ref[c], back_ref[c ^ 1] = totals
    cut_rows(i & 1, g_ref, keep, send)
    cut_rows(i & 1, back_ref, back, back_send)


def cut_rows(bit, g_ref, keep_ref, send_ref):
    size = keep_ref.shape[1]
    keep_ref[...] = g_ref[:, pl.ds(pl.multiple_of(bit * size, size), size)]
    send_ref[...] = g_ref[:, pl.ds(pl.multiple_of((1 - bit) * size, size), size)]


def sum_kernel(pos_ref, keep, other, back, back_other, keep_ref, send_ref, sum_ref):
    sum_ref[0:2] = keep[0:2] + other[0:2]
    sum_ref[2:4] = (keep[2:4] + other[2:4]) + (back[...] + back_other[...])
    cut_rows((pos_ref[0] >> 1) & 1, sum_ref, keep_ref, send_ref)


def pair_kernel(total, pos_ref, mine, other, out_ref):
    y = pos_ref[2]
    for c in range(2):
        out_ref[y * 2 + c] = (mine[c] + other[c]) * (1.0 / total)
        out_ref[(1 - y) * 2 + c] = (mine[2 + c] + other[2 + c]) * (1.0 / total)


def output_kernel(pos_ref, za, zb, out_ref):
    y, half = pos_ref[2], SLAB // 2
    for q in range(half):
        out_ref[(1 - y) * half + q] = za[q].T
        out_ref[y * half + q] = zb[q].T


def place_kernel(pos_ref, *refs):
    pieces, out_ref = refs[:-1], refs[-1]
    size = pieces[0].shape[1]
    for j, piece in enumerate(pieces):
        source = pos_ref[0] ^ j
        start = (source & 1) * (2 * size) + ((source >> 1) & 1) * size
        for k in range(4):
            out_ref[pl.ds(pl.multiple_of(start, size), size), k * 128 : (k + 1) * 128] = piece[k]


def gram_kernel(pos_ref, own, core, far, far_core, g_ref, far_ref):
    b, y = pos_ref[1], pos_ref[2]
    half = SLAB // 2

    def add(totals, place, value):
        totals[place] = value if totals.get(place) is None else totals[place] + value

    totals = {}
    for q in range(half):
        for mine in (True, False):
            at = q + y * half if mine else q + (1 - y) * half
            zh, zl = halves(own[at])
            ch, cl = halves(core[at])
            add(totals, "own", dot3(zh, zl, zh, zl, NT))
            add(totals, "core", dot3(zh, zl, ch, cl, NT))
            if mine:
                fh, fl = halves(far[q])
                gh, gl = halves(far_core[q])
                add(totals, "far", dot3(zh, zl, fh, fl, NT))
                add(totals, "far_core", dot3(zh, zl, gh, gl, NT))
                add(totals, "back", dot3(fh, fl, zh, zl, NT))
                add(totals, "back_core", dot3(fh, fl, ch, cl, NT))
    g_ref[b] = totals["own"]
    g_ref[b ^ 1] = totals["core"]
    g_ref[b ^ 2] = totals["far"]
    g_ref[b ^ 3] = totals["far_core"]
    far_ref[b & 1] = totals["back"]
    far_ref[(b & 1) ^ 1] = totals["back_core"]


def call(kernel, out_shape, operands, scratch=(), name=None, ties=()):
    specs = [
        pl.BlockSpec(memory_space=pltpu.SMEM if o.dtype == jnp.int32 and o.size < 128 else pltpu.VMEM) for o in operands
    ] + [pl.BlockSpec(memory_space=pl.ANY) for _ in ties]
    single = not isinstance(out_shape, (list, tuple))
    return pl.pallas_call(
        kernel,
        out_shape=out_shape,
        in_specs=specs,
        out_specs=(
            pl.BlockSpec(memory_space=pltpu.VMEM)
            if single
            else [pl.BlockSpec(memory_space=pltpu.VMEM) for _ in out_shape]
        ),
        scratch_shapes=list(scratch),
        compiler_params=pltpu.CompilerParams(vmem_limit_bytes=VMEM_LIMIT),
        name=name,
    )(*operands, *ties)


def shape(*dims, dtype=F32):
    return jax.ShapeDtypeStruct(dims, dtype)


def xor_permute(value, axis, step):
    count = lax.axis_size(axis)
    return lax.ppermute(value, axis, [(k, k ^ step) for k in range(count)])


def both_permute(value):
    nd, ng = lax.axis_size("dom"), lax.axis_size("band")
    pairs = [(b * nd + d, (b ^ 2) * nd + (d ^ 1)) for b in range(ng) for d in range(nd)]
    return lax.ppermute(value, ("band", "dom"), pairs)


def swap_all(pieces, direct):
    if direct:
        got = {0: pieces[0]}
        for j in range(1, len(pieces)):
            got[j] = xor_permute(pieces[j], "dom", j)
        return [got[j] for j in range(len(pieces))]
    stacked = lax.all_to_all(jnp.stack(pieces), "dom", 0, 0, tiled=True)
    return [stacked[j] for j in range(len(pieces))]


def packed_atoms(potential, proj_weights, atom_cell, point_codes):
    cube = 2 * REACH + 1
    off_x = point_codes // (cube * cube)
    off_y = point_codes // cube % cube
    off_z = point_codes % cube
    plane = atom_cell[:, 0:1] % SLAB + off_x
    cell_y = (atom_cell[:, 1:2] + off_y - REACH) % SIDE
    cell_z = (atom_cell[:, 2:3] + off_z - REACH) % SIDE
    lateral = cell_y * SIDE + cell_z
    return jnp.concatenate(
        [
            proj_weights.reshape(-1, 256),
            plane.astype(F32),
            lateral.astype(F32),
            jnp.zeros((4, 256), F32),
            potential.reshape(SLAB, LAT),
        ],
        axis=0,
    )


def on_device(trial_waves, potential, proj_weights, kb_energy, atom_cell, point_codes):
    nd = lax.axis_size("dom")
    bands = trial_waves.shape[-1]
    direct = nd == 8
    real = bands // nd
    nb = max(real, 8)
    total = nd * SLAB * LAT
    dom = lax.axis_index("dom") if direct else jnp.int32(0)
    band = lax.axis_index("band")
    pos = jnp.stack([dom, band if direct else jnp.int32(0), band // 2 if direct else jnp.int32(0)]).astype(jnp.int32)
    pos_band = jnp.stack([dom, band, band // 2]).astype(jnp.int32)
    R = SLAB * nb

    waves = trial_waves.reshape(SLAB, LAT, bands)
    if direct:
        cut = call(
            functools.partial(split_kernel, nd, nb),
            [shape(R + 32, LAT)] * nd,
            [atom_cell, waves, potential, proj_weights, point_codes],
            [pltpu.VMEM((SLAB, bands, LAT), F32), pltpu.VMEM((32, 256), F32)],
            "split",
        )
    else:
        packed = packed_atoms(potential, proj_weights, atom_cell, point_codes)
        gathered = lax.all_gather(packed, "dom", axis=0)
        turned = waves.transpose(0, 2, 1).reshape(SLAB, nd, real, LAT).transpose(1, 0, 2, 3)
        cut = [turned[j] for j in range(nd)]

    lh, ll = split_const(lateral_matrix())
    fold = jnp.asarray(fold_matrix()).astype(BF16)
    kb_row = jnp.concatenate([kb_energy, kb_energy, jnp.zeros((112,), F32)])[None]
    pieces = swap_all(cut, direct)
    if not direct:
        pieces = [
            jnp.concatenate([jnp.pad(p, ((0, 0), (0, nb - real), (0, 0))).reshape(R, LAT), gathered[j]])
            for j, p in enumerate(pieces)
        ]
    ready = call(
        functools.partial(filter_kernel, nd, nb, float(total)),
        [shape(R // 2, LAT)] * (2 * nd),
        [pos, kb_row, lh, ll, fold] + [pieces[j] for j in arrival_order(nd)],
        [
            pltpu.VMEM(((nd * SLAB + 2 * HALO) * nb, LAT), F32),
            pltpu.VMEM(((nd * SLAB + 2 * HALO) * nb, LAT), F32),
            pltpu.VMEM((nd * nb, 256), F32),
            pltpu.VMEM((nd * nb, 256), F32),
            pltpu.VMEM((nd * 256, 256), BF16),
            pltpu.VMEM((nd * 256, 256), BF16),
            pltpu.VMEM((nd * SLAB, LAT), F32),
            pltpu.VMEM((nd, 32, 256), F32),
            pltpu.VMEM((nd * R, LAT), BF16),
            pltpu.VMEM((nd * R, LAT), BF16),
            pltpu.VMEM((nd * R, LAT), F32),
        ],
        "filter",
    )
    if direct:
        filtered, correlation = finish_direct(swap_all(ready[:nd], True), swap_all(ready[nd:], True), pos, bands, float(total))
    else:
        ready = [
            jnp.concatenate([ready[nd + j], ready[j]]).reshape(SLAB, nb, LAT)[:, :real] for j in range(nd)
        ]
        back = swap_all(ready, False)
        filtered, correlation = finish_plain(jnp.concatenate(back, axis=1), pos_band, band, bands, float(total))
    return filtered.reshape(trial_waves.shape), correlation


def finish_direct(first, second, pos, bands, total):
    nd, half = len(first), SLAB // 2
    nb = bands // nd

    def join(pieces, order, outs, ties):
        return call(
            functools.partial(join_kernel, order, nb, len(outs) + 1),
            [shape(half, bands, LAT)] + outs,
            [pos] + [pieces[j] for j in order],
            (),
            "join",
            ties,
        )

    za, *sends = join(first, (0, 1, 2, 4, 5, 6, 7, 3), [shape(half // PARTS, bands, LAT)] * PARTS, [])
    far = [xor_permute(p, "band", 2) for p in sends]
    core_a = xor_permute(za, "band", 1)
    (zb,) = join(second, range(nd), [], far)
    core_b = xor_permute(zb, "band", 1)
    far_core = [xor_permute(p, "band", 1) for p in far]
    part, share = shape(4, bands // 2, bands), shape(2, bands // 2, bands)
    keep, send, back, back_send = call(
        functools.partial(blocks_kernel, PARTS),
        [part, part, share, share],
        [pos, za, zb, core_a, core_b] + far + far_core,
        [pltpu.VMEM((4, bands, bands), F32), pltpu.VMEM((2, bands, bands), F32)],
        "blocks",
    )
    piece = shape(4, bands // 4, bands)
    keep, send = call(
        sum_kernel,
        [piece, piece],
        [pos, keep, xor_permute(send, "dom", 1), xor_permute(back, "band", 2), both_permute(back_send)],
        [pltpu.VMEM((4, bands // 2, bands), F32)],
        "sum",
    )
    mine = keep + xor_permute(send, "dom", 2)
    rows = call(
        functools.partial(pair_kernel, total), piece, [pos, mine, xor_permute(mine, "dom", 4)], (), "pair"
    )
    filtered = call(output_kernel, shape(SLAB, LAT, bands), [pos, za, zb], (), "output")
    correlation = call(
        place_kernel,
        shape(bands, 4 * bands),
        [pos, rows] + [xor_permute(rows, "dom", step) for step in (1, 2, 3)],
        (),
        "place",
    )
    return filtered, correlation


def finish_plain(z, pos, band, bands, total):
    send = lax.dynamic_slice_in_dim(z, (1 - band // 2) * (SLAB // 2), SLAB // 2, 0)
    far = xor_permute(send, "band", 2)
    gram, gram_far = call(
        gram_kernel,
        [shape(4, bands, bands), shape(2, bands, bands)],
        [pos, z, xor_permute(z, "band", 1), far, xor_permute(far, "band", 1)],
        (),
        "gram",
    )
    filtered = z.transpose(0, 2, 1)
    start = (1 - band // 2) * 2
    cross = lax.dynamic_slice_in_dim(gram, start, 2, 0) + xor_permute(gram_far, "band", 2)
    gram = lax.dynamic_update_slice_in_dim(gram, cross, start, 0)
    wide = gram.transpose(1, 0, 2).reshape(bands, 4 * bands)
    return filtered, lax.psum(wide, "dom") / total


def solution(mesh):
    return jax.shard_map(
        on_device,
        mesh=mesh,
        in_specs=(
            P("dom", None, None, "band"),
            P("dom", None, None),
            P("dom", None, None),
            P(),
            P("dom", None),
            P("dom", None),
        ),
        out_specs=(P("dom", None, None, "band"), P("band", None)),
        check_vma=False,
    )
```

```python
import functools

import jax
import jax.numpy as jnp
import numpy as np
from jax import lax
from jax.experimental import pallas as pl
from jax.experimental.pallas import tpu as pltpu
from jax.sharding import PartitionSpec as P

HALO = 6
REACH = 4
SLAB = 8
PARTS = 4
SIDE = 16
LAT = SIDE * SIDE

COEFFS = (
    -5369.0 / 1800.0,
    12.0 / 7.0,
    -15.0 / 56.0,
    10.0 / 189.0,
    -1.0 / 112.0,
    2.0 / 1925.0,
    -1.0 / 16632.0,
)
FILTER_LOWER = 5.0
FILTER_UPPER = 24.0
SPECTRUM_BOTTOM = 0.0
EPSILON = 1e-06

HALF_WIDTH = (FILTER_UPPER - FILTER_LOWER) / 2.0
CENTRE = (FILTER_UPPER + FILTER_LOWER) / 2.0
SIGMA_1 = HALF_WIDTH / (SPECTRUM_BOTTOM - CENTRE)
SIGMA_2 = 1.0 / (2.0 / SIGMA_1 - SIGMA_1)

VMEM_LIMIT = 48 * 1024 * 1024
BF16 = jnp.bfloat16
F32 = jnp.float32
NN = (((1,), (0,)), ((), ()))
NT = (((1,), (1,)), ((), ()))


def dot(a, b, dims=NN):
    return lax.dot_general(a, b, dims, preferred_element_type=F32)


def halves(x):
    hi = x.astype(BF16)
    return hi, (x - hi.astype(F32)).astype(BF16)


def dot3(ah, al, bh, bl, dims=NN):
    rows = ah.shape[0]
    both = dot(jnp.concatenate([ah, al], axis=0), bh, dims)
    return both[:rows] + both[rows:] + dot(ah, bl, dims)


def lateral_matrix():
    line = np.zeros((SIDE, SIDE))
    at = np.arange(SIDE)
    for k in range(1, HALO + 1):
        for sign in (1, -1):
            np.add.at(line, ((at + sign * k) % SIDE, at), -0.5 * COEFFS[k])
    eye = np.eye(SIDE)
    return np.kron(line, eye) + np.kron(eye, line)


def relation():
    return [[-1, 0] if q < REACH else [0, 1] for q in range(SLAB)]


def fold_matrix():
    out = np.zeros((256, 384), np.float32)
    for q, pair in enumerate(relation()):
        for half, rel in enumerate(pair):
            for r in range(16):
                out[q * 32 + half * 16 + r, (rel + 1) * 128 + r] = 1.0
    return out


def split_const(matrix):
    matrix = np.asarray(matrix, np.float32)
    hi = jnp.asarray(matrix, F32).astype(BF16)
    lo = (jnp.asarray(matrix, F32) - hi.astype(F32)).astype(BF16)
    return hi, lo


def split_kernel(nd, nb, x_ref, packed_ref, *refs):
    outs, scratch = refs[:-1], refs[-1]
    i = lax.axis_index("dom")
    for q in range(SLAB):
        scratch[q] = x_ref[q].T
    for j in range(nd):
        start = (i ^ j) * nb
        for q in range(SLAB):
            outs[j][q * nb : (q + 1) * nb] = scratch[q, pl.ds(pl.multiple_of(start, nb), nb)]
        outs[j][SLAB * nb :] = packed_ref[...]


def build_projectors(nd, scratch, wh_ref, wl_ref, v_ref):
    lat = lax.broadcasted_iota(jnp.int32, (LAT, 256), 0).astype(F32)
    plane = lax.broadcasted_iota(jnp.int32, (16, 1, 1), 0).astype(F32)
    diagonal = -1.5 * COEFFS[0] - CENTRE

    def body(s, carry):
        his, los = [], []
        for a in range(2):
            w = scratch[s, a * 8 : a * 8 + 8]
            px = scratch[s, 16 + a : 17 + a]
            place = scratch[s, 18 + a : 19 + a]
            hot = jnp.where(lat == place, 1.0, 0.0).astype(BF16)
            masked = jnp.where(px[None] == plane, w[None], 0.0).reshape(128, 256)
            mh, ml = halves(masked)
            his.append(dot(mh, hot, NT).reshape(16, 8, LAT))
            los.append(dot(ml, hot, NT).reshape(16, 8, LAT))
        hi = jnp.concatenate(his, axis=1).astype(BF16)
        lo = jnp.concatenate(los, axis=1).astype(BF16)
        for t in range(16):
            p = (s * SLAB - REACH + t + nd * SLAB) % (nd * SLAB) if isinstance(s, int) else lax.rem(
                s * SLAB - REACH + t + nd * SLAB, nd * SLAB
            )
            row = pl.ds(pl.multiple_of(p * 32 + (16 if t < SLAB else 0), 16), 16)
            wh_ref[row] = hi[t]
            wl_ref[row] = lo[t]
        v_ref[pl.ds(pl.multiple_of(s * SLAB, SLAB), SLAB)] = scratch[s, 24:32] + diagonal
        return carry

    if nd <= 8:
        for s in range(nd):
            body(s, 0)
    else:
        lax.fori_loop(0, nd, body, 0)


def arrival_order(nd):
    return [1, 2, *range(nd // 2, nd), *range(3, nd // 2), 0]


def filter_kernel(nd, nb, total, pos_ref, kb_ref, lh_ref, ll_ref, fold_ref, *refs):
    pieces, outs = refs[:nd], refs[nd : 3 * nd]
    f0_ref, f1_ref, fold_out, spread_out, wh_ref, wl_ref, v_ref, packed, fh_ref, fl_ref, acc_ref = refs[3 * nd :]
    i = pos_ref[0]
    R = SLAB * nb
    rows_q = lax.broadcasted_iota(jnp.int32, (SLAB, nb, 256), 0)
    lanes_q = lax.broadcasted_iota(jnp.int32, (SLAB, nb, 256), 2) // 32
    same = rows_q == lanes_q

    def slab_rows(s, k=0):
        return pl.ds(pl.multiple_of((s * SLAB + HALO + k) * nb, nb), R)

    def wrap(ref):
        ref[0 : HALO * nb] = ref[nd * R : nd * R + HALO * nb]
        ref[HALO * nb + nd * R : 2 * HALO * nb + nd * R] = ref[HALO * nb : 2 * HALO * nb]

    def each(body):
        if nd <= 8:
            for s in range(nd):
                body(s)
        else:
            lax.fori_loop(0, nd, lambda s, c: (body(s), c)[1], 0)

    for piece, j in zip(pieces, arrival_order(nd)):
        f0_ref[slab_rows(i ^ j)] = piece[:R]
        packed[i ^ j] = piece[R:]
    wrap(f0_ref)
    build_projectors(nd, packed, wh_ref, wl_ref, v_ref)

    def apply(ref, finish):
        def project(s):
            rows = pl.ds(pl.multiple_of(s * R, R), R)
            fh, fl = halves(ref[slab_rows(s)])
            fh_ref[rows] = fh
            fl_ref[rows] = fl
            w = pl.ds(pl.multiple_of(s * 256, 256), 256)
            g = dot3(fh, fl, wh_ref[w], wl_ref[w], NT).reshape(SLAB, nb, 256)
            fold_out[pl.ds(pl.multiple_of(s * nb, nb), nb)] = jnp.sum(jnp.where(same, g, 0.0), axis=0)

        def lateral(s):
            rows = pl.ds(pl.multiple_of(s * 4 * R, 4 * R), 4 * R)
            acc_ref[rows] = dot3(fh_ref[rows], fl_ref[rows], lh_ref[...], ll_ref[...])

        each(project)
        if nd <= 8:
            for s in range(nd // 4):
                lateral(s)
        else:
            lax.fori_loop(0, nd // 4, lambda s, c: (lateral(s), c)[1], 0)
        gh, gl = halves(fold_out[...])
        h = dot(gh, fold_ref[...]) + dot(gl, fold_ref[...])
        below, at, above = h[:, :128], h[:, 128:256], h[:, 256:]

        def next_slab(x):
            return jnp.concatenate([x[-nb:], x[:-nb]], axis=0)

        def previous_slab(x):
            return jnp.concatenate([x[nb:], x[:nb]], axis=0)

        p = (at + next_slab(above) + previous_slab(below)) * kb_ref[...]
        wide = jnp.concatenate([next_slab(p), p, previous_slab(p)], axis=1)
        ph, plo = halves(wide)
        spread_out[...] = dot(ph, fold_ref[...], NT) + dot(plo, fold_ref[...], NT)

        def step(s):
            f = ref[slab_rows(s)]
            x = jnp.where(same, spread_out[pl.ds(pl.multiple_of(s * nb, nb), nb)][None], 0.0).reshape(R, 256)
            xh, xl = halves(x)
            w = pl.ds(pl.multiple_of(s * 256, 256), 256)
            acc = dot3(xh, xl, wh_ref[w], wl_ref[w]) + acc_ref[pl.ds(pl.multiple_of(s * R, R), R)]
            v = v_ref[pl.ds(pl.multiple_of(s * SLAB, SLAB), SLAB)]
            acc = acc + (f.reshape(SLAB, nb, LAT) * v[:, None, :]).reshape(R, LAT)
            for k in range(1, HALO + 1):
                acc = acc + (-0.5 * COEFFS[k]) * (ref[slab_rows(s, k)] + ref[slab_rows(s, -k)])
            finish(s, acc)

        each(step)

    def first(s, acc):
        f1_ref[slab_rows(s)] = (SIGMA_1 / HALF_WIDTH) * acc

    apply(f0_ref, first)
    wrap(f1_ref)

    def second(s, acc):
        f0_ref_new = (2.0 * SIGMA_2 / HALF_WIDTH) * acc - (SIGMA_1 * SIGMA_2) * f0_ref[slab_rows(s)]
        y2_store(s, f0_ref_new)

    def y2_store(s, value):
        f0_ref[slab_rows(s)] = value

    apply(f1_ref, second)
    square = jnp.zeros((nb, LAT), F32)
    if nd <= 8:
        for s in range(nd):
            y = f0_ref[slab_rows(s)].reshape(SLAB, nb, LAT)
            square = square + jnp.sum(y * y, axis=0)
    else:

        def add(s, total_square):
            y = f0_ref[slab_rows(s)].reshape(SLAB, nb, LAT)
            return total_square + jnp.sum(y * y, axis=0)

        square = lax.fori_loop(0, nd, add, square)
    scale = 1.0 / jnp.sqrt(jnp.sum(square, axis=1, keepdims=True) / total + EPSILON)
    chip, half = pos_ref[2], SLAB // 2
    for j in range(nd):
        for h, out in ((1 - chip, outs[j]), (chip, outs[nd + j])):
            start = ((i ^ j) * SLAB + HALO + h * half) * nb
            y = f0_ref[pl.ds(pl.multiple_of(start, nb), half * nb)].reshape(half, nb, LAT)
            out[...] = (y * scale[None]).reshape(half * nb, LAT)


def join_kernel(order, nb, outs, pos_ref, *refs):
    pieces, (z_ref, *parts) = refs[: len(order)], refs[-outs:]
    i = pos_ref[0]
    for piece, j in zip(pieces, order):
        rows = pl.ds(pl.multiple_of((i ^ j) * nb, nb), nb)
        for q in range(SLAB // 2):
            z_ref[q, rows] = piece[q * nb : (q + 1) * nb]
    for k, part in enumerate(parts):
        part[...] = z_ref[k * part.shape[0] : (k + 1) * part.shape[0]]


def blocks_kernel(parts, pos_ref, za, zb, ca, cb, *refs):
    far, far_core = refs[:parts], refs[parts : 2 * parts]
    keep, send, back, back_send, g_ref, back_ref = refs[2 * parts :]
    i, c = pos_ref[0], pos_ref[1] & 1
    per = SLAB // 2 // parts
    totals = None
    for q in range(SLAB // 2):
        zh, zl = halves(zb[q])
        ch, cl = halves(cb[q])
        fh, fl = halves(far[q // per][q % per])
        gh, gl = halves(far_core[q // per][q % per])
        wh, wl = halves(za[q])
        xh, xl = halves(ca[q])
        now = (
            dot3(zh, zl, zh, zl, NT) + dot3(wh, wl, wh, wl, NT),
            dot3(zh, zl, ch, cl, NT) + dot3(wh, wl, xh, xl, NT),
            dot3(zh, zl, fh, fl, NT),
            dot3(zh, zl, gh, gl, NT),
            dot3(fh, fl, zh, zl, NT),
            dot3(fh, fl, ch, cl, NT),
        )
        totals = now if totals is None else tuple(t + n for t, n in zip(totals, now))
    g_ref[c], g_ref[c ^ 1], g_ref[2 + c], g_ref[2 + (c ^ 1)], back_ref[c], back_ref[c ^ 1] = totals
    cut_rows(i & 1, g_ref, keep, send)
    cut_rows(i & 1, back_ref, back, back_send)


def cut_rows(bit, g_ref, keep_ref, send_ref):
    size = keep_ref.shape[1]
    keep_ref[...] = g_ref[:, pl.ds(pl.multiple_of(bit * size, size), size)]
    send_ref[...] = g_ref[:, pl.ds(pl.multiple_of((1 - bit) * size, size), size)]


def sum_kernel(pos_ref, keep, other, back, back_other, keep_ref, send_ref, sum_ref):
    sum_ref[0:2] = keep[0:2] + other[0:2]
    sum_ref[2:4] = (keep[2:4] + other[2:4]) + (back[...] + back_other[...])
    cut_rows((pos_ref[0] >> 1) & 1, sum_ref, keep_ref, send_ref)


def pair_kernel(total, pos_ref, mine, other, out_ref):
    y = pos_ref[2]
    for c in range(2):
        out_ref[y * 2 + c] = (mine[c] + other[c]) * (1.0 / total)
        out_ref[(1 - y) * 2 + c] = (mine[2 + c] + other[2 + c]) * (1.0 / total)


def output_kernel(pos_ref, za, zb, out_ref):
    y, half = pos_ref[2], SLAB // 2
    for q in range(half):
        out_ref[(1 - y) * half + q] = za[q].T
        out_ref[y * half + q] = zb[q].T


def place_kernel(pos_ref, *refs):
    pieces, out_ref = refs[:-1], refs[-1]
    size = pieces[0].shape[1]
    for j, piece in enumerate(pieces):
        source = pos_ref[0] ^ j
        start = (source & 1) * (2 * size) + ((source >> 1) & 1) * size
        for k in range(4):
            out_ref[pl.ds(pl.multiple_of(start, size), size), k * 128 : (k + 1) * 128] = piece[k]


def gram_kernel(pos_ref, own, core, far, far_core, g_ref, far_ref):
    b, y = pos_ref[1], pos_ref[2]
    half = SLAB // 2

    def add(totals, place, value):
        totals[place] = value if totals.get(place) is None else totals[place] + value

    totals = {}
    for q in range(half):
        for mine in (True, False):
            at = q + y * half if mine else q + (1 - y) * half
            zh, zl = halves(own[at])
            ch, cl = halves(core[at])
            add(totals, "own", dot3(zh, zl, zh, zl, NT))
            add(totals, "core", dot3(zh, zl, ch, cl, NT))
            if mine:
                fh, fl = halves(far[q])
                gh, gl = halves(far_core[q])
                add(totals, "far", dot3(zh, zl, fh, fl, NT))
                add(totals, "far_core", dot3(zh, zl, gh, gl, NT))
                add(totals, "back", dot3(fh, fl, zh, zl, NT))
                add(totals, "back_core", dot3(fh, fl, ch, cl, NT))
    g_ref[b] = totals["own"]
    g_ref[b ^ 1] = totals["core"]
    g_ref[b ^ 2] = totals["far"]
    g_ref[b ^ 3] = totals["far_core"]
    far_ref[b & 1] = totals["back"]
    far_ref[(b & 1) ^ 1] = totals["back_core"]


def call(kernel, out_shape, operands, scratch=(), name=None, ties=()):
    specs = [
        pl.BlockSpec(memory_space=pltpu.SMEM if o.dtype == jnp.int32 and o.size < 128 else pltpu.VMEM) for o in operands
    ] + [pl.BlockSpec(memory_space=pl.ANY) for _ in ties]
    single = not isinstance(out_shape, (list, tuple))
    return pl.pallas_call(
        kernel,
        out_shape=out_shape,
        in_specs=specs,
        out_specs=(
            pl.BlockSpec(memory_space=pltpu.VMEM)
            if single
            else [pl.BlockSpec(memory_space=pltpu.VMEM) for _ in out_shape]
        ),
        scratch_shapes=list(scratch),
        compiler_params=pltpu.CompilerParams(vmem_limit_bytes=VMEM_LIMIT),
        name=name,
    )(*operands, *ties)


def shape(*dims, dtype=F32):
    return jax.ShapeDtypeStruct(dims, dtype)


def xor_permute(value, axis, step):
    count = lax.axis_size(axis)
    return lax.ppermute(value, axis, [(k, k ^ step) for k in range(count)])


def both_permute(value):
    nd, ng = lax.axis_size("dom"), lax.axis_size("band")
    pairs = [(b * nd + d, (b ^ 2) * nd + (d ^ 1)) for b in range(ng) for d in range(nd)]
    return lax.ppermute(value, ("band", "dom"), pairs)


def swap_all(pieces, direct):
    if direct:
        got = {0: pieces[0]}
        for j in range(1, len(pieces)):
            got[j] = xor_permute(pieces[j], "dom", j)
        return [got[j] for j in range(len(pieces))]
    stacked = lax.all_to_all(jnp.stack(pieces), "dom", 0, 0, tiled=True)
    return [stacked[j] for j in range(len(pieces))]


def packed_atoms(potential, proj_weights, atom_cell, point_codes):
    cube = 2 * REACH + 1
    off_x = point_codes // (cube * cube)
    off_y = point_codes // cube % cube
    off_z = point_codes % cube
    plane = atom_cell[:, 0:1] % SLAB + off_x
    cell_y = (atom_cell[:, 1:2] + off_y - REACH) % SIDE
    cell_z = (atom_cell[:, 2:3] + off_z - REACH) % SIDE
    lateral = cell_y * SIDE + cell_z
    return jnp.concatenate(
        [
            proj_weights.reshape(-1, 256),
            plane.astype(F32),
            lateral.astype(F32),
            jnp.zeros((4, 256), F32),
            potential.reshape(SLAB, LAT),
        ],
        axis=0,
    )


def on_device(trial_waves, potential, proj_weights, kb_energy, atom_cell, point_codes):
    nd = lax.axis_size("dom")
    bands = trial_waves.shape[-1]
    direct = nd == 8
    real = bands // nd
    nb = max(real, 8)
    total = nd * SLAB * LAT
    dom = lax.axis_index("dom") if direct else jnp.int32(0)
    band = lax.axis_index("band")
    pos = jnp.stack([dom, band if direct else jnp.int32(0), band // 2 if direct else jnp.int32(0)]).astype(jnp.int32)
    pos_band = jnp.stack([dom, band, band // 2]).astype(jnp.int32)
    R = SLAB * nb

    waves = trial_waves.reshape(SLAB, LAT, bands)
    packed = packed_atoms(potential, proj_weights, atom_cell, point_codes)
    if direct:
        cut = call(
            functools.partial(split_kernel, nd, nb),
            [shape(R + 32, LAT)] * nd,
            [waves, packed],
            [pltpu.VMEM((SLAB, bands, LAT), F32)],
            "split",
        )
    else:
        gathered = lax.all_gather(packed, "dom", axis=0)
        turned = waves.transpose(0, 2, 1).reshape(SLAB, nd, real, LAT).transpose(1, 0, 2, 3)
        cut = [turned[j] for j in range(nd)]

    lh, ll = split_const(lateral_matrix())
    fold = jnp.asarray(fold_matrix()).astype(BF16)
    kb_row = jnp.concatenate([kb_energy, kb_energy, jnp.zeros((112,), F32)])[None]
    pieces = swap_all(cut, direct)
    if not direct:
        pieces = [
            jnp.concatenate([jnp.pad(p, ((0, 0), (0, nb - real), (0, 0))).reshape(R, LAT), gathered[j]])
            for j, p in enumerate(pieces)
        ]
    ready = call(
        functools.partial(filter_kernel, nd, nb, float(total)),
        [shape(R // 2, LAT)] * (2 * nd),
        [pos, kb_row, lh, ll, fold] + [pieces[j] for j in arrival_order(nd)],
        [
            pltpu.VMEM(((nd * SLAB + 2 * HALO) * nb, LAT), F32),
            pltpu.VMEM(((nd * SLAB + 2 * HALO) * nb, LAT), F32),
            pltpu.VMEM((nd * nb, 256), F32),
            pltpu.VMEM((nd * nb, 256), F32),
            pltpu.VMEM((nd * 256, 256), BF16),
            pltpu.VMEM((nd * 256, 256), BF16),
            pltpu.VMEM((nd * SLAB, LAT), F32),
            pltpu.VMEM((nd, 32, 256), F32),
            pltpu.VMEM((nd * R, LAT), BF16),
            pltpu.VMEM((nd * R, LAT), BF16),
            pltpu.VMEM((nd * R, LAT), F32),
        ],
        "filter",
    )
    if direct:
        filtered, correlation = finish_direct(swap_all(ready[:nd], True), swap_all(ready[nd:], True), pos, bands, float(total))
    else:
        ready = [
            jnp.concatenate([ready[nd + j], ready[j]]).reshape(SLAB, nb, LAT)[:, :real] for j in range(nd)
        ]
        back = swap_all(ready, False)
        filtered, correlation = finish_plain(jnp.concatenate(back, axis=1), pos_band, band, bands, float(total))
    return filtered.reshape(trial_waves.shape), correlation


def finish_direct(first, second, pos, bands, total):
    nd, half = len(first), SLAB // 2
    nb = bands // nd

    def join(pieces, order, outs, ties):
        return call(
            functools.partial(join_kernel, order, nb, len(outs) + 1),
            [shape(half, bands, LAT)] + outs,
            [pos] + [pieces[j] for j in order],
            (),
            "join",
            ties,
        )

    za, *sends = join(first, (0, 1, 2, 4, 5, 6, 7, 3), [shape(half // PARTS, bands, LAT)] * PARTS, [])
    far = [xor_permute(p, "band", 2) for p in sends]
    core_a = xor_permute(za, "band", 1)
    (zb,) = join(second, (0, 1, 2, 4, 5, 6, 7, 3), [], far)
    core_b = xor_permute(zb, "band", 1)
    far_core = [xor_permute(p, "band", 1) for p in far]
    part, share = shape(4, bands // 2, bands), shape(2, bands // 2, bands)
    keep, send, back, back_send = call(
        functools.partial(blocks_kernel, PARTS),
        [part, part, share, share],
        [pos, za, zb, core_a, core_b] + far + far_core,
        [pltpu.VMEM((4, bands, bands), F32), pltpu.VMEM((2, bands, bands), F32)],
        "blocks",
    )
    piece = shape(4, bands // 4, bands)
    keep, send = call(
        sum_kernel,
        [piece, piece],
        [pos, keep, xor_permute(send, "dom", 1), xor_permute(back, "band", 2), both_permute(back_send)],
        [pltpu.VMEM((4, bands // 2, bands), F32)],
        "sum",
    )
    mine = keep + xor_permute(send, "dom", 2)
    rows = call(
        functools.partial(pair_kernel, total), piece, [pos, mine, xor_permute(mine, "dom", 4)], (), "pair"
    )
    filtered = call(output_kernel, shape(SLAB, LAT, bands), [pos, za, zb], (), "output")
    correlation = call(
        place_kernel,
        shape(bands, 4 * bands),
        [pos, rows] + [xor_permute(rows, "dom", step) for step in (1, 2, 3)],
        (),
        "place",
    )
    return filtered, correlation


def finish_plain(z, pos, band, bands, total):
    send = lax.dynamic_slice_in_dim(z, (1 - band // 2) * (SLAB // 2), SLAB // 2, 0)
    far = xor_permute(send, "band", 2)
    gram, gram_far = call(
        gram_kernel,
        [shape(4, bands, bands), shape(2, bands, bands)],
        [pos, z, xor_permute(z, "band", 1), far, xor_permute(far, "band", 1)],
        (),
        "gram",
    )
    filtered = z.transpose(0, 2, 1)
    start = (1 - band // 2) * 2
    cross = lax.dynamic_slice_in_dim(gram, start, 2, 0) + xor_permute(gram_far, "band", 2)
    gram = lax.dynamic_update_slice_in_dim(gram, cross, start, 0)
    wide = gram.transpose(1, 0, 2).reshape(bands, 4 * bands)
    return filtered, lax.psum(wide, "dom") / total


def solution(mesh):
    return jax.shard_map(
        on_device,
        mesh=mesh,
        in_specs=(
            P("dom", None, None, "band"),
            P("dom", None, None),
            P("dom", None, None),
            P(),
            P("dom", None),
            P("dom", None),
        ),
        out_specs=(P("dom", None, None, "band"), P("band", None)),
        check_vma=False,
    )
```
